32 devices in a mesh: batch: 16 (over z, x, core), tm: 2 (over y).
Axes of the slice: x: 2, y: 2, z: 4, core: 2. Of those that a mesh axis runs over, the one named last changes fastest.
Arguments:
- frames: bfloat16 [64, 992, 324], P('batch', 'tm'), may hold values from -6 to 6
- lengths: int32 [64], P('batch'), may hold values from 248 to 992, as said below
- cotangent: bfloat16 [64, 992, 324], P('batch', 'tm'), may hold values from -6 to 6
- query_weight: bfloat16 [324, 324], replicated, may hold values from -0.3125 to 0.3125
- key_weight: bfloat16 [324, 324], replicated, may hold values from -0.3125 to 0.3125
- value_weight: bfloat16 [324, 324], replicated, may hold values from -0.3125 to 0.3125
- position_weight: bfloat16 [324, 324], replicated, may hold values from -0.3125 to 0.3125
- content_bias: float32 [324], replicated, may hold values from -3 to 3
- position_bias: float32 [324], replicated, may hold values from -3 to 3
- output_weight: bfloat16 [324, 324], replicated, may hold values from -6 to 6
- attend_gain: float32 [324], replicated, may hold values from 0.5 to 1.5
- attend_shift: float32 [324], replicated, may hold values from -2 to 2
- inner_first: bfloat16 [324, 1296], replicated, may hold values from -0.3125 to 0.3125
- outer_first: bfloat16 [1296, 324], replicated, may hold values from -0.25 to 0.25
- first_gain: float32 [324], replicated, may hold values from 0.5 to 1.5
- first_shift: float32 [324], replicated, may hold values from -2 to 2
- glu_weight: bfloat16 [324, 648], replicated, may hold values from -0.3125 to 0.3125
- depth_weight: float32 [31, 324], replicated, may hold values from -1 to 1
- batch_gain: float32 [324], replicated, may hold values from 0.5 to 1.5
- batch_shift: float32 [324], replicated, may hold values from -2 to 2
- point_weight: bfloat16 [324, 324], replicated, may hold values from -0.5 to 0.5
- conv_gain: float32 [324], replicated, may hold values from 0.5 to 1.5
- conv_shift: float32 [324], replicated, may hold values from -2 to 2
- inner_second: bfloat16 [324, 1296], replicated, may hold values from -0.3125 to 0.3125
- outer_second: bfloat16 [1296, 324], replicated, may hold values from -0.25 to 0.25
- second_gain: float32 [324], replicated, may hold values from 0.5 to 1.5
- second_shift: float32 [324], replicated, may hold values from -2 to 2
Outputs:
- block_out: bfloat16 [64, 992, 324], P('batch', 'tm')
- frames_grad: bfloat16 [64, 992, 324], P('batch', 'tm')
- grad_query_weight: float32 [324, 324], replicated
- grad_key_weight: float32 [324, 324], replicated
- grad_value_weight: float32 [324, 324], replicated
- grad_position_weight: float32 [324, 324], replicated
- grad_content_bias: float32 [324], replicated
- grad_position_bias: float32 [324], replicated
- grad_output_weight: float32 [324, 324], replicated
- grad_attend_gain: float32 [324], replicated
- grad_attend_shift: float32 [324], replicated
- grad_inner_first: float32 [324, 1296], replicated
- grad_outer_first: float32 [1296, 324], replicated
- grad_first_gain: float32 [324], replicated
- grad_first_shift: float32 [324], replicated
- grad_glu_weight: float32 [324, 648], replicated
- grad_depth_weight: float32 [31, 324], replicated
- grad_batch_gain: float32 [324], replicated
- grad_batch_shift: float32 [324], replicated
- grad_point_weight: float32 [324, 324], replicated
- grad_conv_gain: float32 [324], replicated
- grad_conv_shift: float32 [324], replicated
- grad_inner_second: float32 [324, 1296], replicated
- grad_outer_second: float32 [1296, 324], replicated
- grad_second_gain: float32 [324], replicated
- grad_second_shift: float32 [324], replicated
The draws below stay inside these ranges and needn't reach their ends.
Inputs may be any that keep to these rules, and one draw needn't show every extreme that they name: `lengths`: among the 4 utterances of each index of batch, one has all 992 frames valid.
All inputs are finite; a program needn't handle non-finite values.
Results may differ from the reference program's by a relative error of at most 0.023.
Values may be sent and summed in bfloat16 or wider, within the bound.
No kernel may reach another device: no remote copies, remote signals or barrier semaphores. Data moves between devices by JAX's collectives and lax.ppermute only.
A program may use at most 384 MiB of HBM per device.

```python
import math
import jax
import jax.numpy as jnp
from jax import lax

D = 324
HEADS = 4
FF = 1296
KERNEL = 31
LEN = 992
SEQ_DEV = 4
HEAD_DIM = 81
HALF_K = 15
SEQS = 64


def draw_lengths(key, part):
    key = jax.random.fold_in(key, 11)
    first_key, second_key = jax.random.split(key)
    base_lengths = jax.random.randint(first_key, (SEQS,), LEN // 4, LEN + 1)
    chosen_slot = jax.random.randint(second_key, (SEQS // SEQ_DEV,), 0, SEQ_DEV)
    positions = jnp.arange(SEQS, dtype=jnp.int32)
    longest = positions % SEQ_DEV == chosen_slot[positions // SEQ_DEV]
    return jnp.where(longest, LEN, base_lengths).astype(jnp.int32)


def steps_of(own_key, extent, cuts, low, top_value):
    gain = 1.0
    for dim, parts in cuts:
        draws = jax.random.uniform(jax.random.fold_in(jax.random.fold_in(own_key, 6), dim), (parts,), jnp.float32, low / len(cuts), top_value / len(cuts))
        gain = gain * jnp.repeat(jnp.exp(draws), extent[dim] // parts).reshape((-1,) + (1,) * (len(extent) - 1 - dim))
    return gain


def noise(rng, dims, scale, reach, shards=(), kind=jnp.bfloat16):
    entries = jax.random.normal(rng, dims, jnp.float32) * scale
    if len(shards) > 0:
        entries = steps_of(rng, dims, shards, -0.22, 0.18) * entries
    return jnp.clip(entries, min=-reach, max=reach).astype(kind)


def setup_inputs(seed: int = 0) -> dict:
    keys = jax.random.split(jax.random.key(seed), 28)
    return {
        "frames": noise(keys[0], (SEQS, LEN, D), 1.0, 6.0, ((0, 16), (1, 2))),
        "lengths": draw_lengths(jax.random.fold_in(keys[27], 71), 0),
        "cotangent": noise(keys[2], (SEQS, LEN, D), 1.0, 6.0, ((0, 16), (1, 2))),
        "query_weight": noise(keys[3], (D, D), D ** -0.5, 0.3125),
        "key_weight": noise(keys[4], (D, D), D ** -0.5, 0.3125),
        "value_weight": noise(keys[5], (D, D), D ** -0.5, 0.3125),
        "position_weight": noise(keys[6], (D, D), D ** -0.5, 0.3125),
        "content_bias": noise(keys[7], (D,), 0.5, 3.0, (), jnp.float32),
        "position_bias": noise(keys[8], (D,), 0.5, 3.0, (), jnp.float32),
        "output_weight": noise(keys[9], (D, D), 1 ** -0.5, 6.0),
        "attend_gain": jnp.clip(1.0 + 0.1 * jax.random.normal(keys[10], (D,), jnp.float32), 0.5, 1.5),
        "attend_shift": noise(keys[11], (D,), 0.3, 2.0, (), jnp.float32),
        "inner_first": noise(keys[12], (D, FF), D ** -0.5, 0.3125),
        "outer_first": noise(keys[13], (FF, D), (FF // 2) ** -0.5, 0.25),
        "first_gain": jnp.clip(1.0 + 0.1 * jax.random.normal(keys[14], (D,), jnp.float32), 0.5, 1.5),
        "first_shift": noise(keys[15], (D,), 0.3, 2.0, (), jnp.float32),
        "glu_weight": noise(keys[16], (D, 2 * D), D ** -0.5, 0.3125),
        "depth_weight": noise(keys[17], (KERNEL, D), KERNEL ** -0.5, 1.0, (), jnp.float32),
        "batch_gain": jnp.clip(1.0 + 0.1 * jax.random.normal(keys[18], (D,), jnp.float32), 0.5, 1.5),
        "batch_shift": noise(keys[19], (D,), 0.3, 2.0, (), jnp.float32),
        "point_weight": noise(keys[20], (D, D), (D // 2) ** -0.5, 0.5),
        "conv_gain": jnp.clip(1.0 + 0.1 * jax.random.normal(keys[21], (D,), jnp.float32), 0.5, 1.5),
        "conv_shift": noise(keys[22], (D,), 0.3, 2.0, (), jnp.float32),
        "inner_second": noise(keys[23], (D, FF), D ** -0.5, 0.3125),
        "outer_second": noise(keys[24], (FF, D), (FF // 2) ** -0.5, 0.25),
        "second_gain": jnp.clip(1.0 + 0.1 * jax.random.normal(keys[25], (D,), jnp.float32), 0.5, 1.5),
        "second_shift": noise(keys[26], (D,), 0.3, 2.0, (), jnp.float32),
    }


@jax.custom_vjp
def low(v):
    return lax.optimization_barrier(v.astype(jnp.bfloat16)).astype(jnp.float32)

@jax.custom_vjp
def low_back(v):
    return v

def low_keep(v):
    return (low(v), None)

def low_pass(kept, grad):
    return (grad,)

def back_keep(v):
    return (v, None)

def back_low(kept, grad):
    return (low(grad),)
low.defvjp(low_keep, low_pass)
low_back.defvjp(back_keep, back_low)
EPSILON = 1e-05
MASKED = -1e+30

def position_table(offsets, model_width):
    half_width = model_width // 2
    ladder = jnp.arange(half_width, dtype=jnp.int32).astype(jnp.float32)
    frequency = jnp.exp(ladder * (-2.0 * math.log(10000.0) / model_width))
    angles = offsets.astype(jnp.float32)[:, None] * frequency[None, :]
    return jnp.concatenate([jnp.sin(angles), jnp.cos(angles)], axis=1)

def skew(scores_table, key_count):
    leading = scores_table.shape[:-2]
    row_count = scores_table.shape[-2]
    col_count = scores_table.shape[-1]
    flattened = scores_table.reshape(leading + (row_count * col_count,))
    flattened = lax.slice_in_dim(flattened, row_count - 1, row_count - 1 + row_count * (col_count - 1), axis=flattened.ndim - 1)
    return flattened.reshape(leading + (row_count, col_count - 1))[..., :key_count]

def dense(left_side, right_side):
    return jnp.matmul(left_side, right_side, precision=lax.Precision.HIGHEST)

def post_norm(values, gain_row, shift_row):
    center = lax.optimization_barrier(jnp.mean(values, axis=-1, keepdims=True))
    centred = values - center
    spread_sq = lax.optimization_barrier(jnp.mean(centred * centred, axis=-1, keepdims=True))
    return centred * lax.rsqrt(spread_sq + EPSILON) * gain_row + shift_row

def feed_forward(hidden, inner_weight, outer_weight):
    inner_value = low_back(dense(low(hidden), inner_weight))
    return low_back(dense(low(jax.nn.silu(inner_value)), outer_weight))

def attend_one(query_c, query_p, key_rows, value_rows, key_valid, relative, score_scale):
    content = jnp.einsum('qhe,khe->hqk', query_c, key_rows, precision=lax.Precision.HIGHEST)
    position = jnp.einsum('qhe,rhe->hqr', query_p, relative, precision=lax.Precision.HIGHEST)
    logits = low_back(content + skew(position, key_rows.shape[0]))
    scores = jnp.where(key_valid[None, None, :], logits * score_scale, MASKED)
    row_peak = lax.optimization_barrier(jnp.max(scores, axis=-1, keepdims=True))
    exponent = jnp.exp(scores - row_peak)
    softmax_prob = exponent / lax.optimization_barrier(jnp.sum(exponent, axis=-1, keepdims=True))
    return jnp.einsum('hqk,khe->qhe', low(softmax_prob), value_rows, precision=lax.Precision.HIGHEST)

def reference(frames, lengths, cotangent, query_weight, key_weight, value_weight, position_weight, content_bias, position_bias, output_weight, attend_gain, attend_shift, inner_first, outer_first, first_gain, first_shift, glu_weight, depth_weight, batch_gain, batch_shift, point_weight, conv_gain, conv_shift, inner_second, outer_second, second_gain, second_shift):
    stepper = jnp.arange(LEN, dtype=jnp.int32)
    key_valid = stepper[None, :] < lengths[:, None]
    row_mask = key_valid.astype(jnp.float32)[:, :, None]
    offsets = LEN - 1 - jnp.arange(2 * LEN - 1, dtype=jnp.int32)
    pos_table = low(position_table(offsets, D))
    score_scale = 1.0 / math.sqrt(HEAD_DIM)
    split_shape = (SEQS, LEN, HEADS, HEAD_DIM)

    def forward(source, params):
        query_w, key_w, value_w, position_w, content_b, position_b, output_w, attend_g, attend_s, inner_one, outer_one, first_g, first_s, glu_w, depth_w, batch_g, batch_s, point_w, conv_g, conv_s, inner_two, outer_two, second_g, second_s = params
        queries = low_back(dense(source, query_w))
        key_rows = low(dense(source, key_w))
        value_rows = low(dense(source, value_w))
        query_c = low(queries + content_b)
        query_p = low(queries + position_b)
        relative = low(dense(pos_table, position_w)).reshape(2 * LEN - 1, HEADS, HEAD_DIM)

        def one_sequence(pieces):
            return attend_one(pieces[0], pieces[1], pieces[2], pieces[3], pieces[4], relative, score_scale)
        attended = lax.map(jax.checkpoint(one_sequence), (query_c.reshape(split_shape), query_p.reshape(split_shape), key_rows.reshape(split_shape), value_rows.reshape(split_shape), key_valid))
        mixed = low_back(low(attended.reshape(SEQS, LEN, D)))
        attn_branch = low_back(dense(mixed, output_w))
        hidden_one = post_norm(source + attn_branch, attend_g, attend_s)
        hidden_two = post_norm(hidden_one + feed_forward(hidden_one, inner_one, outer_one), first_g, first_s)
        gated = low_back(dense(low(hidden_two), glu_w))
        glu_out = gated[..., :D] * jax.nn.sigmoid(gated[..., D:])
        spread = low(glu_out * row_mask)
        padded = jnp.pad(spread, ((0, 0), (HALF_K, HALF_K), (0, 0)))
        conv_out = depth_w[0] * padded[:, 0:LEN]
        for offset in range(1, KERNEL):
            conv_out = conv_out + depth_w[offset] * padded[:, offset:offset + LEN]
        conv_out = low_back(conv_out)
        frame_count = jnp.sum(row_mask)
        mean_batch = lax.optimization_barrier(jnp.sum(conv_out * row_mask, axis=(0, 1))) / frame_count
        square_batch = lax.optimization_barrier(jnp.sum(conv_out * conv_out * row_mask, axis=(0, 1))) / frame_count
        rstd_batch = lax.rsqrt(square_batch - mean_batch * mean_batch + EPSILON)
        normed = (conv_out - mean_batch) * rstd_batch * batch_g + batch_s
        point_branch = low_back(dense(low(jax.nn.silu(normed)), point_w))
        hidden_three = post_norm(hidden_two + point_branch, conv_g, conv_s)
        return post_norm(hidden_three + feed_forward(hidden_three, inner_two, outer_two), second_g, second_s)
    params = tuple((member.astype(jnp.float32) for member in (query_weight, key_weight, value_weight, position_weight, content_bias, position_bias, output_weight, attend_gain, attend_shift, inner_first, outer_first, first_gain, first_shift, glu_weight, depth_weight, batch_gain, batch_shift, point_weight, conv_gain, conv_shift, inner_second, outer_second, second_gain, second_shift)))
    output, puller = jax.vjp(forward, frames.astype(jnp.float32), params)
    grad_source, grads = puller(cotangent.astype(jnp.float32))
    grad_query, grad_key, grad_value, grad_position, grad_content, grad_posbias, grad_output, grad_gain_one, grad_shift_one, grad_inner_one, grad_outer_one, grad_gain_two, grad_shift_two, grad_glu, grad_depth, grad_batch_gain, grad_batch_shift, grad_point, grad_gain_three, grad_shift_three, grad_inner_two, grad_outer_two, grad_gain_four, grad_shift_four = grads
    return (output.astype(jnp.bfloat16), grad_source.astype(jnp.bfloat16), grad_query, grad_key, grad_value, grad_position, grad_content, grad_posbias, grad_output, grad_gain_one, grad_shift_one, grad_inner_one, grad_outer_one, grad_gain_two, grad_shift_two, grad_glu, grad_depth, grad_batch_gain, grad_batch_shift, grad_point, grad_gain_three, grad_shift_three, grad_inner_two, grad_outer_two, grad_gain_four, grad_shift_four)
```

```python
import functools
import math

import jax
import jax.numpy as jnp
from jax import lax
from jax.experimental import pallas as pl
from jax.experimental.pallas import tpu as pltpu
from jax.sharding import PartitionSpec as P

HEADS = 4
EPSILON = 1e-05
PAD = 16
LOG2E = 1.4426950408889634
WIDE = 256
VMEM = 60 * 1024 * 1024
bf16 = jnp.bfloat16
f32 = jnp.float32


def project(left_side, right_side):
    return jnp.dot(left_side, right_side, preferred_element_type=jnp.float32)


def project_back(left_side, right_side):
    return lax.dot_general(
        left_side, right_side, (((1,), (1,)), ((), ())), preferred_element_type=jnp.float32
    )


def weight_grad(left_side, right_side):
    return lax.dot_general(
        left_side, right_side, (((0,), (0,)), ((), ())), preferred_element_type=jnp.float32
    )


def post_norm(values, gain_row, shift_row):
    center = jnp.mean(values, axis=-1, keepdims=True)
    centred = values - center
    spread_sq = jnp.mean(centred * centred, axis=-1, keepdims=True)
    return centred * lax.rsqrt(spread_sq + EPSILON) * gain_row + shift_row


def norm_back(values, gain_row, upstream):
    center = jnp.mean(values, axis=-1, keepdims=True)
    centred = values - center
    inv_std = lax.rsqrt(jnp.mean(centred * centred, axis=-1, keepdims=True) + EPSILON)
    normed = centred * inv_std
    scaled = upstream * gain_row
    result_grad = inv_std * (
        scaled
        - jnp.mean(scaled, axis=-1, keepdims=True)
        - normed * jnp.mean(scaled * normed, axis=-1, keepdims=True)
    )
    return (result_grad, jnp.sum(upstream * normed, axis=0), jnp.sum(upstream, axis=0))


def swish_slope(values):
    sigma = jax.nn.sigmoid(values)
    return sigma * (1.0 + values * (1.0 - sigma))


def feed_forward(hidden, inner_weight, outer_weight):
    entry_low = hidden.astype(jnp.bfloat16)
    inner_value = project(entry_low, inner_weight)
    active = jax.nn.silu(inner_value).astype(jnp.bfloat16)
    return (entry_low, inner_value, active, project(active, outer_weight))


def feed_back(upstream, entry_low, inner_value, active, inner_weight, outer_weight):
    upstream_low = upstream.astype(jnp.bfloat16)
    grad_outer = weight_grad(active, upstream_low)
    grad_active = project_back(upstream_low, outer_weight)
    grad_inner_value = (grad_active * swish_slope(inner_value)).astype(jnp.bfloat16)
    grad_inner = weight_grad(entry_low, grad_inner_value)
    return (project_back(grad_inner_value, inner_weight), grad_inner, grad_outer)


def dot(a,b): return jnp.dot(a,b,preferred_element_type=f32)
def dot_nt(a,b): return lax.dot_general(a,b,(((1,),(1,)),((),())),preferred_element_type=f32)
def dot_tn(a,b): return lax.dot_general(a,b,(((0,),(0,)),((),())),preferred_element_type=f32)

def lanes(shape): return lax.broadcasted_iota(jnp.int32,shape,1)

def attend_forward_kernel(len_ref,f_ref,wq_ref,wk_ref,wv_ref,pos_ref,cb_ref,pb_ref,s_ref,c_ref,sb_ref,
                          mixed_ref,qa_ref,qb_ref,ka_ref,v_ref,*,hs,tile):
    u=pl.program_id(0)
    T=f_ref.shape[1]; W=wq_ref.shape[2]
    off=2*hs; one=off+hs
    scale=LOG2E/math.sqrt(hs)
    valid=len_ref[u]
    for r0 in range(0,T,tile):
        rows=pl.ds(r0,tile)
        f=f_ref[0,rows,:]
        lane=lanes((tile,W))
        k=dot(f,wk_ref[0])+c_ref[rows,:]
        row=lax.broadcasted_iota(jnp.int32,(tile,W),0)+r0
        k=jnp.where(lane==one,jnp.where(row<valid,0.0,-1e30),jnp.where((lane>one)&(lane<one+4),1.0,k))
        ka_ref[0,0,rows,:]=k.astype(bf16)
        v=dot(f,wv_ref[0])
        vl=lanes(v.shape)
        v_ref[0,0,rows,:]=jnp.where((vl==hs)|(vl==hs+1),1.0,v).astype(bf16)
    for r0 in range(0,T,tile):
        rows=pl.ds(r0,tile)
        f=f_ref[0,rows,:]
        lane=lanes((tile,W))
        q=dot(f,wq_ref[0])
        qp=(q+pb_ref[0]).astype(bf16)
        e=dot(qp,pos_ref[0])
        es=e[:,:W]; ec=e[:,W:]
        s=s_ref[rows,:]; c=c_ref[rows,:]
        qa=(es*s+ec*c+(q+cb_ref[0]))*scale
        qa=jnp.where(lane==one,1.0,qa)
        qb=((ec*s-es*c)*scale).astype(bf16)
        qb_ref[0,0,rows,:]=qb
        qal=qa.astype(bf16)
        sc=dot_nt(qal,ka_ref[0,0])+dot_nt(qb,sb_ref[...])
        m=jnp.max(sc,axis=1,keepdims=True)
        p=jnp.exp2(sc-m).astype(bf16)
        o=dot(p,v_ref[0,0])
        l=o[:,hs:hs+1]
        mixed_ref[0,rows,:]=(o/l).astype(bf16)
        lse=-(m+jnp.log2(l))
        hi=lse.astype(bf16).astype(f32); mid=(lse-hi).astype(bf16).astype(f32); lo=lse-hi-mid
        qa=jnp.where(lane==one+1,hi,jnp.where(lane==one+2,mid,jnp.where(lane==one+3,lo,qa)))
        qa_ref[0,0,rows,:]=qa.astype(bf16)

def attend_forward(lens,f,wq,wk,wv,pos,cb,pb,s,c,sb,tile=496):
    U,T,D=f.shape; H=wq.shape[0]; W=wq.shape[2]; V=wv.shape[2]
    hs=D//H
    gs=pl.GridSpec(grid=(U,H),in_specs=[
        pl.BlockSpec(memory_space=pltpu.SMEM),
        pl.BlockSpec((1,T,D),lambda u,h:(u,0,0)),
        pl.BlockSpec((1,D,W),lambda u,h:(h,0,0)),
        pl.BlockSpec((1,D,W),lambda u,h:(h,0,0)),
        pl.BlockSpec((1,D,V),lambda u,h:(h,0,0)),
        pl.BlockSpec((1,W,2*W),lambda u,h:(h,0,0)),
        pl.BlockSpec((1,1,W),lambda u,h:(h,0,0)),
        pl.BlockSpec((1,1,W),lambda u,h:(h,0,0)),
        pl.BlockSpec((T,W),lambda u,h:(0,0)),
        pl.BlockSpec((T,W),lambda u,h:(0,0)),
        pl.BlockSpec((T,W),lambda u,h:(0,0)),
    ],out_specs=[
        pl.BlockSpec((1,T,V),lambda u,h:(u,0,h)),
        pl.BlockSpec((1,1,T,W),lambda u,h:(u,h,0,0)),
        pl.BlockSpec((1,1,T,W),lambda u,h:(u,h,0,0)),
        pl.BlockSpec((1,1,T,W),lambda u,h:(u,h,0,0)),
        pl.BlockSpec((1,1,T,V),lambda u,h:(u,h,0,0)),
    ])
    sd=jax.ShapeDtypeStruct
    return pl.pallas_call(functools.partial(attend_forward_kernel,hs=hs,tile=tile),grid_spec=gs,
        out_shape=[sd((U,T,H*V),bf16),sd((U,H,T,W),bf16),sd((U,H,T,W),bf16),sd((U,H,T,W),bf16),sd((U,H,T,V),bf16)],
        compiler_params=pltpu.CompilerParams(vmem_limit_bytes=VMEM,dimension_semantics=("arbitrary","arbitrary")),
        name="attend_forward")(lens,f,wq,wk,wv,pos,cb,pb,s,c,sb)

def attend_backward_kernel(qa_ref,qb_ref,ka_ref,v_ref,sb_ref,do_ref,mixed_ref,st_ref,ct_ref,pos_ref,
                           d_ref,dpos_ref,bias_ref,*,hs,tile):
    u=pl.program_id(1)
    T=qa_ref.shape[2]; W=qa_ref.shape[3]; V=v_ref.shape[3]
    off=2*hs; one=off+hs
    inv=1.0/math.sqrt(hs)
    do=do_ref[0]
    dof=do.astype(f32)
    delta=-jnp.sum(dof*mixed_ref[0].astype(f32),axis=1,keepdims=True)
    hi=delta.astype(bf16).astype(f32); lo=delta-hi
    lv=lanes((T,V))
    dox=jnp.where(lv==hs,hi,jnp.where(lv==hs+1,lo,dof)).astype(bf16)
    qa=qa_ref[0,0]; qb=qb_ref[0,0]
    dqa=None; dqb=None; parts=[]
    for r0 in range(0,T,tile):
        rows=pl.ds(r0,tile)
        ka=ka_ref[0,0,rows,:]; sb=sb_ref[rows,:]
        st=dot_nt(ka,qa)+dot_nt(sb,qb)
        p=jnp.exp2(st)
        dp=dot_nt(v_ref[0,0,rows,:],dox)
        ds=(p*dp).astype(bf16)
        dv=dot(p.astype(bf16),do)
        dk=dot(ds,qa)
        a=dot_tn(ka,ds); b=dot_tn(sb,ds)
        dqa=a if dqa is None else dqa+a
        dqb=b if dqb is None else dqb+b
        parts.append((dv,dk))
    st_=st_ref[...]; ct_=ct_ref[...]
    des=(dqa*st_-dqb*ct_)*inv; dec=(dqa*ct_+dqb*st_)*inv
    de=jnp.concatenate([des,dec],axis=0).astype(bf16)
    dqp=dot(pos_ref[0],de)
    dpos=dot(de,qa)
    sub=lax.broadcasted_iota(jnp.int32,(W,T),0)
    dqc=jnp.where((sub>=off)&(sub<one),dqa*inv,0.0)
    lane8=lax.broadcasted_iota(jnp.int32,(W,128),1)
    bias=jnp.where(lane8==0,jnp.sum(dqc,axis=1,keepdims=True),jnp.sum(dqp,axis=1,keepdims=True))
    @pl.when(u==0)
    def _():
        dpos_ref[0]=dpos; bias_ref[0]=bias
    @pl.when(u>0)
    def _():
        dpos_ref[0]+=dpos; bias_ref[0]+=bias
    dq=jnp.transpose(dqc+dqp)
    dq=pltpu.roll(dq,W-hs,1)
    for i,(dv,dk) in enumerate(parts):
        rows=pl.ds(i*tile,tile)
        lw=lanes((tile,W))
        dv=jnp.concatenate([dv,jnp.zeros((tile,W-V),f32)],axis=1)
        x=jnp.where(lw<hs,dv,jnp.where((lw>=off)&(lw<one),dk*(1.0/LOG2E),dq[i*tile:(i+1)*tile]))
        d_ref[0,rows,:]=jnp.where(lw<one,x,0.0).astype(bf16)

def attend_backward(qa,qb,ka,v,sb,do,mixed,st,ct,pos,tile=496):
    U,H,T,W=qa.shape; V=v.shape[3]
    hs=81
    b4=lambda w: pl.BlockSpec((1,1,T,w),lambda h,u:(u,h,0,0))
    gs=pl.GridSpec(grid=(H,U),in_specs=[b4(W),b4(W),b4(W),b4(V),
        pl.BlockSpec((T,W),lambda h,u:(0,0)),
        pl.BlockSpec((1,T,V),lambda h,u:(u,0,h)),
        pl.BlockSpec((1,T,V),lambda h,u:(u,0,h)),
        pl.BlockSpec((W,T),lambda h,u:(0,0)),
        pl.BlockSpec((W,T),lambda h,u:(0,0)),
        pl.BlockSpec((1,W,2*W),lambda h,u:(h,0,0)),
    ],out_specs=[
        pl.BlockSpec((1,T,W),lambda h,u:(u,0,h)),
        pl.BlockSpec((1,2*W,W),lambda h,u:(h,0,0)),
        pl.BlockSpec((1,W,128),lambda h,u:(h,0,0)),
    ])
    sd=jax.ShapeDtypeStruct
    return pl.pallas_call(functools.partial(attend_backward_kernel,hs=hs,tile=tile),grid_spec=gs,
        out_shape=[sd((U,T,H*W),bf16),sd((H,2*W,W),f32),sd((H,W,128),f32)],
        compiler_params=pltpu.CompilerParams(vmem_limit_bytes=VMEM,dimension_semantics=("arbitrary","arbitrary")),
        name="attend_backward")(qa,qb,ka,v,sb,do,mixed,st,ct,pos)


def fill_padded(buf,value):
    T=value.shape[0]
    zero=jnp.zeros((PAD,buf.shape[1]),f32)
    buf[0:PAD,:]=zero
    buf[T+PAD:T+2*PAD,:]=zero
    buf[PAD:T+PAD,:]=value

def conv_forward_kernel(len_ref,x_ref,w_ref,out_ref,stat_ref,xp,*,taps,step):
    u=pl.program_id(1)
    T=x_ref.shape[1]; half=(taps-1)//2
    fill_padded(xp,x_ref[0].astype(f32))
    valid=len_ref[u]
    def body(i,carry):
        s1,s2=carry
        base=pl.multiple_of(i*step,step)
        acc=None
        for o in range(taps):
            t=w_ref[o:o+1,:]*xp[pl.ds(base+PAD-half+o,step),:]
            acc=t if acc is None else acc+t
        out_ref[0,pl.ds(base,step),:]=acc
        row=lax.broadcasted_iota(jnp.int32,(step,128),0)+base
        m=jnp.where(row<valid,acc,0.0)
        s1=s1+m.reshape(step//8,8,128).sum(0)
        s2=s2+(m*acc).reshape(step//8,8,128).sum(0)
        return s1,s2
    z=jnp.zeros((8,128),f32)
    s1,s2=lax.fori_loop(0,T//step,body,(z,z))
    st=jnp.concatenate([s1,s2],axis=0)
    @pl.when(u==0)
    def _(): stat_ref[...]=st
    @pl.when(u>0)
    def _(): stat_ref[...]+=st

def conv_forward(lens,x,w,step=32):
    U,T,C=x.shape; taps=w.shape[0]
    nc=pl.cdiv(C,128)
    sd=jax.ShapeDtypeStruct
    return pl.pallas_call(functools.partial(conv_forward_kernel,taps=taps,step=step),
        grid=(nc,U),
        in_specs=[pl.BlockSpec(memory_space=pltpu.SMEM),
            pl.BlockSpec((1,T,128),lambda c,u:(u,0,c)),pl.BlockSpec((taps,128),lambda c,u:(0,c))],
        out_specs=[pl.BlockSpec((1,T,128),lambda c,u:(u,0,c)),pl.BlockSpec((16,128),lambda c,u:(0,c))],
        out_shape=[sd((U,T,C),f32),sd((16,C),f32)],
        scratch_shapes=[pltpu.VMEM((T+2*PAD,128),f32)],
        compiler_params=pltpu.CompilerParams(vmem_limit_bytes=VMEM,dimension_semantics=("arbitrary","arbitrary")),
        name="conv_forward")(lens,x,w)

def conv_backward_kernel(len_ref,x_ref,dz_ref,cv_ref,w_ref,co_ref,gs_ref,gw_ref,xp,gp,*,taps,step):
    u=pl.program_id(1)
    T=x_ref.shape[1]; half=(taps-1)//2
    valid=len_ref[u]
    row=lax.broadcasted_iota(jnp.int32,(T,128),0)
    g=dz_ref[0].astype(f32)*co_ref[0:1,:]+jnp.where(row<valid,co_ref[1:2,:]+co_ref[2:3,:]*cv_ref[0],0.0)
    fill_padded(gp,g)
    fill_padded(xp,x_ref[0].astype(f32))
    def body(i,accs):
        base=pl.multiple_of(i*step,step)
        acc=None; new=[]
        gc=gp[pl.ds(base+PAD,step),:]
        for o in range(taps):
            t=w_ref[o:o+1,:]*gp[pl.ds(base+PAD+half-o,step),:]
            acc=t if acc is None else acc+t
            new.append(accs[o]+(gc*xp[pl.ds(base+PAD-half+o,step),:]).reshape(step//8,8,128).sum(0))
        gs_ref[0,pl.ds(base,step),:]=acc
        return tuple(new)
    z=jnp.zeros((8,128),f32)
    accs=lax.fori_loop(0,T//step,body,(z,)*taps)
    gw=jnp.concatenate([a.sum(0,keepdims=True) for a in accs],axis=0)
    @pl.when(u==0)
    def _(): gw_ref[...]=gw
    @pl.when(u>0)
    def _(): gw_ref[...]+=gw

def conv_backward(lens,x,dz,cv,w,co,step=32):
    U,T,C=x.shape; taps=w.shape[0]
    nc=pl.cdiv(C,128)
    sd=jax.ShapeDtypeStruct
    blk=pl.BlockSpec((1,T,128),lambda c,u:(u,0,c))
    return pl.pallas_call(functools.partial(conv_backward_kernel,taps=taps,step=step),
        grid=(nc,U),
        in_specs=[pl.BlockSpec(memory_space=pltpu.SMEM),blk,blk,blk,
            pl.BlockSpec((taps,128),lambda c,u:(0,c)),pl.BlockSpec((3,128),lambda c,u:(0,c))],
        out_specs=[blk,pl.BlockSpec((taps,128),lambda c,u:(0,c))],
        out_shape=[sd((U,T,C),f32),sd((taps,C),f32)],
        scratch_shapes=[pltpu.VMEM((T+2*PAD,128),f32)]*2,
        compiler_params=pltpu.CompilerParams(vmem_limit_bytes=VMEM,dimension_semantics=("arbitrary","arbitrary")),
        name="conv_backward")(lens,x,dz,cv,w,co)


def swap_pairs(size, distance):
    return [(i, i ^ distance) for i in range(size)]


def hyper_steps():
    steps = []
    for axis in ("batch", "tm"):
        size = lax.axis_size(axis)
        distance = 1
        while distance < size:
            steps.append((axis, size, distance))
            distance *= 2
    return steps


def butterfly_sum(value):
    for axis, size, distance in hyper_steps():
        value = value + lax.ppermute(value, axis, swap_pairs(size, distance))
    return value


def hyper_sum(value):
    steps = hyper_steps()
    value = value.astype(f32)
    for axis, size, distance in steps:
        bit = (lax.axis_index(axis) // distance) % 2
        half = value.shape[0] // 2
        low, high = value[:half], value[half:]
        sent = jnp.where(bit == 0, high, low).astype(bf16)
        kept = jnp.where(bit == 0, low, high)
        value = kept + lax.ppermute(sent, axis, swap_pairs(size, distance)).astype(f32)
    value = value.astype(bf16)
    for axis, size, distance in steps[::-1]:
        bit = (lax.axis_index(axis) // distance) % 2
        other = lax.ppermute(value, axis, swap_pairs(size, distance))
        value = jnp.concatenate(
            [jnp.where(bit == 0, value, other), jnp.where(bit == 0, other, value)]
        )
    return value


def pack_columns(arrays, unit):
    pieces = []
    for array in arrays:
        rows, cols = array.shape
        rows_up = -(-rows // 16) * 16
        cols_up = -(-cols // 128) * 128
        padded = jnp.pad(array, ((0, rows_up - rows), (0, cols_up - cols)))
        pieces += [padded[:, c : c + 128] for c in range(0, cols_up, 128)]
    total = sum(piece.shape[0] for piece in pieces)
    spare = -total % unit
    if spare:
        pieces.append(jnp.zeros((spare, 128), pieces[0].dtype))
    return jnp.concatenate(pieces, axis=0)


def unpack_columns(packed, shapes):
    results = []
    at = 0
    for rows, cols in shapes:
        rows_up = -(-rows // 16) * 16
        count = -(-cols // 128)
        blocks = [packed[at + i * rows_up : at + i * rows_up + rows] for i in range(count)]
        results.append(jnp.concatenate(blocks, axis=1)[:, :cols].astype(f32))
        at += count * rows_up
    return results


def to_utterances(block, mine):
    parts = lax.axis_size("tm")
    seqs, rows, width = block.shape
    own = seqs // parts
    pieces = block.reshape(parts, own, rows, width)
    result = jnp.zeros((own, parts, rows, width), block.dtype)
    for shift in range(parts):
        target = lax.rem(mine + shift, parts)
        piece = lax.dynamic_index_in_dim(pieces, target, 0, keepdims=False)
        if shift:
            piece = lax.ppermute(piece, "tm", [(i, (i + shift) % parts) for i in range(parts)])
        origin = lax.rem(mine - shift + parts, parts)
        result = lax.dynamic_update_slice(result, piece[:, None], (0, origin, 0, 0))
    return result.reshape(own, parts * rows, width)


def to_frames(whole, mine):
    parts = lax.axis_size("tm")
    own, length, width = whole.shape
    rows = length // parts
    pieces = whole.reshape(own, parts, rows, width)
    result = jnp.zeros((parts, own, rows, width), whole.dtype)
    for shift in range(parts):
        target = lax.rem(mine + shift, parts)
        piece = lax.dynamic_index_in_dim(pieces, target, 1, keepdims=False)
        if shift:
            piece = lax.ppermute(piece, "tm", [(i, (i + shift) % parts) for i in range(parts)])
        origin = lax.rem(mine - shift + parts, parts)
        result = lax.dynamic_update_slice(result, piece[None], (origin, 0, 0, 0))
    return result.reshape(parts * own, rows, width)


def on_device(
    frames,
    lengths,
    cotangent,
    query_weight,
    key_weight,
    value_weight,
    position_weight,
    content_bias,
    position_bias,
    output_weight,
    attend_gain,
    attend_shift,
    inner_first,
    outer_first,
    first_gain,
    first_shift,
    glu_weight,
    depth_weight,
    batch_gain,
    batch_shift,
    point_weight,
    conv_gain,
    conv_shift,
    inner_second,
    outer_second,
    second_gain,
    second_shift,
):
    seq_local, local_rows, D = frames.shape
    H = HEADS
    hs = D // H
    half = D // 2
    parts = lax.axis_size("tm")
    mine = lax.axis_index("tm")
    U = seq_local // parts
    T = local_rows * parts
    R = U * T
    lens = lax.dynamic_slice_in_dim(lengths, mine * U, U)

    whole = to_utterances(frames, mine)
    upstream_whole = to_utterances(cotangent, mine)
    source = whole.reshape(R, D)

    def head_weight(weight, at, width):
        split = jnp.transpose(weight.reshape(D, H, hs), (1, 0, 2))
        return jnp.pad(split, ((0, 0), (0, 0), (at, width - at - hs)))

    def head_bias(bias):
        return jnp.pad(bias.reshape(H, 1, hs), ((0, 0), (0, 0), (half, WIDE - half - hs)))

    query_x = head_weight(query_weight, half, WIDE)
    key_x = head_weight(key_weight, half, WIDE)
    value_x = head_weight(value_weight, 0, 128)
    pos_x = jnp.transpose(position_weight.reshape(2, half, H, hs), (2, 3, 0, 1))
    pos_x = jnp.pad(pos_x, ((0, 0), (half, WIDE - half - hs), (0, 0), (0, WIDE - half)))
    pos_x = pos_x.reshape(H, WIDE, 2 * WIDE)
    content_x, position_x = head_bias(content_bias), head_bias(position_bias)
    output_x = jnp.pad(output_weight.reshape(H, hs, D), ((0, 0), (0, 128 - hs), (0, 0)))
    output_x = output_x.reshape(H * 128, D)
    ladder = jnp.arange(half, dtype=jnp.int32).astype(f32)
    frequency = jnp.exp(ladder * (-2.0 * math.log(10000.0) / D))
    angles = jnp.arange(T, dtype=jnp.int32).astype(f32)[:, None] * frequency[None, :]
    sines = jnp.pad(jnp.sin(angles), ((0, 0), (0, WIDE - half)))
    cosines = jnp.pad(jnp.cos(angles), ((0, 0), (0, WIDE - half)))
    sines_low = sines.astype(bf16)

    mixed, qa, qb, ka, va = attend_forward(
        lens, whole, query_x, key_x, value_x, pos_x, content_x, position_x, sines, cosines, sines_low
    )
    mixed_flat = mixed.reshape(R, H * 128)
    resid_one = source.astype(f32) + project(mixed_flat, output_x)
    hidden_one = post_norm(resid_one, attend_gain, attend_shift)
    entry_one, inner_one, active_one, outer_one = feed_forward(hidden_one, inner_first, outer_first)
    resid_two = hidden_one + outer_one
    hidden_two = post_norm(resid_two, first_gain, first_shift)
    conv_entry = hidden_two.astype(bf16)
    gated = project(conv_entry, glu_weight)
    linear_part = gated[:, :D]
    gate_sigma = jax.nn.sigmoid(gated[:, D:])
    row_mask = (
        (jnp.arange(T, dtype=jnp.int32)[None, :] < lens[:, None]).astype(f32).reshape(R, 1)
    )
    spread = (linear_part * gate_sigma * row_mask).astype(bf16).reshape(U, T, D)
    conv_out, stats = conv_forward(lens, spread, depth_weight)
    conv_flat = conv_out.reshape(R, D)
    frame_count = jnp.sum(lens).astype(f32)
    sums = jnp.stack(
        [
            jnp.sum(stats[:8], axis=0),
            jnp.sum(stats[8:], axis=0),
            jnp.broadcast_to(frame_count, (D,)),
        ]
    )
    sums = butterfly_sum(sums)
    sum_first, sum_second, frame_count = sums[0], sums[1], sums[2]
    mean_batch = sum_first / frame_count
    rstd_batch = lax.rsqrt(sum_second / frame_count - mean_batch * mean_batch + EPSILON)
    centred = (conv_flat - mean_batch) * rstd_batch
    normed = centred * batch_gain + batch_shift
    swished = jax.nn.silu(normed).astype(bf16)
    resid_three = hidden_two + project(swished, point_weight)
    hidden_three = post_norm(resid_three, conv_gain, conv_shift)
    entry_two, inner_two, active_two, outer_two = feed_forward(
        hidden_three, inner_second, outer_second
    )
    resid_four = hidden_three + outer_two
    block_out = post_norm(resid_four, second_gain, second_shift).astype(bf16)
    block_out = to_frames(block_out.reshape(U, T, D), mine)
    upstream = upstream_whole.reshape(R, D).astype(f32)
    grad_four, grad_gain_four, grad_shift_four = norm_back(resid_four, second_gain, upstream)
    grad_ffn_two, grad_inner_two, grad_outer_two = feed_back(
        grad_four, entry_two, inner_two, active_two, inner_second, outer_second
    )
    grad_three, grad_gain_three, grad_shift_three = norm_back(
        resid_three, conv_gain, grad_four + grad_ffn_two
    )
    grad_point_low = grad_three.astype(bf16)
    grad_point = weight_grad(swished, grad_point_low)
    grad_normed = project_back(grad_point_low, point_weight) * swish_slope(normed)
    grad_batch_gain = jnp.sum(grad_normed * centred, axis=0)
    grad_batch_shift = jnp.sum(grad_normed, axis=0)
    grad_centred = grad_normed * batch_gain
    part_first, part_second = butterfly_sum(
        jnp.stack([grad_batch_shift * batch_gain, grad_batch_gain * batch_gain])
    )
    grad_var = -0.5 * rstd_batch * rstd_batch * part_second
    grad_mean = -rstd_batch * part_first - 2.0 * mean_batch * grad_var
    coefs = jnp.stack([rstd_batch, grad_mean / frame_count, 2.0 * grad_var / frame_count])
    grad_spread, grad_depth = conv_backward(
        lens, spread, grad_centred.reshape(U, T, D), conv_out, depth_weight, coefs
    )
    grad_glu_out = grad_spread.reshape(R, D) * row_mask
    grad_gated = jnp.concatenate(
        [grad_glu_out * gate_sigma, grad_glu_out * linear_part * gate_sigma * (1.0 - gate_sigma)],
        axis=1,
    ).astype(bf16)
    grad_glu = weight_grad(conv_entry, grad_gated)
    grad_two, grad_gain_two, grad_shift_two = norm_back(
        resid_two, first_gain, grad_three + project_back(grad_gated, glu_weight)
    )
    grad_ffn_one, grad_inner_one, grad_outer_one = feed_back(
        grad_two, entry_one, inner_one, active_one, inner_first, outer_first
    )
    grad_one, grad_gain_one, grad_shift_one = norm_back(
        resid_one, attend_gain, grad_two + grad_ffn_one
    )
    grad_branch_low = grad_one.astype(bf16)
    grad_output = weight_grad(mixed_flat, grad_branch_low)
    grad_output = grad_output.reshape(H, 128, D)[:, :hs].reshape(D, D)
    grad_mixed = project_back(grad_branch_low, output_x).astype(bf16).reshape(U, T, H * 128)

    early = lax.psum(
        tuple(
            g.astype(bf16)
            for g in (
                grad_inner_two, grad_outer_two, grad_point, grad_glu, grad_output,
                grad_inner_one, grad_outer_one,
            )
        ),
        ("batch", "tm"),
    )
    grad_inner_two, grad_outer_two, grad_point, grad_glu, grad_output, grad_inner_one, grad_outer_one = (
        g.astype(f32) for g in early
    )

    grads, grad_pos, grad_bias = attend_backward(
        qa, qb, ka, va, sines_low, grad_mixed, mixed, sines.T, cosines.T, pos_x
    )
    grads_flat = grads.reshape(R, H * WIDE)
    weights_back = jnp.pad(
        jnp.concatenate(
            [
                jnp.transpose(w.reshape(D, H, hs), (1, 2, 0))
                for w in (value_weight, query_weight, key_weight)
            ],
            axis=1,
        ),
        ((0, 0), (0, WIDE - 3 * hs), (0, 0)),
    ).reshape(H * WIDE, D)
    frames_grad = (grad_one + project(grads_flat, weights_back)).astype(bf16).reshape(U, T, D)
    frames_grad = to_frames(frames_grad, mine)
    grad_heads = weight_grad(source, grads_flat)
    scale = LOG2E / math.sqrt(hs)
    grad_pos = grad_pos[:, :, half : half + hs] / scale + (
        grad_pos[:, :, half + hs : half + hs + 1]
        * (position_x - content_x)[:, :, half : half + hs]
    )
    grad_pos = jnp.concatenate([grad_pos[:, :half], grad_pos[:, WIDE : WIDE + half]], axis=1)
    grad_position = jnp.transpose(grad_pos, (1, 0, 2)).reshape(D, D)
    grad_content = grad_bias[:, half : half + hs, 0].reshape(D)
    grad_posbias = grad_bias[:, half : half + hs, 1].reshape(D)
    small = jnp.concatenate(
        [
            jnp.stack(
                [
                    grad_content, grad_posbias, grad_gain_one, grad_shift_one,
                    grad_gain_two, grad_shift_two, grad_batch_gain, grad_batch_shift,
                    grad_gain_three, grad_shift_three, grad_gain_four, grad_shift_four,
                ]
            ),
            grad_depth,
        ]
    )
    late = (grad_heads, grad_position, small)
    packed = hyper_sum(pack_columns(late, 1024))
    grad_heads, grad_position, small = unpack_columns(packed, [g.shape for g in late])
    grad_heads = grad_heads.reshape(D, H, WIDE)
    grad_value, grad_query, grad_key = (
        grad_heads[:, :, i * hs : (i + 1) * hs].reshape(D, D) for i in range(3)
    )
    (
        grad_content, grad_posbias, grad_gain_one, grad_shift_one,
        grad_gain_two, grad_shift_two, grad_batch_gain, grad_batch_shift,
        grad_gain_three, grad_shift_three, grad_gain_four, grad_shift_four,
    ) = (small[i] for i in range(12))
    grad_depth = small[12:]
    return (
        block_out,
        frames_grad,
        grad_query,
        grad_key,
        grad_value,
        grad_position,
        grad_content,
        grad_posbias,
        grad_output,
        grad_gain_one,
        grad_shift_one,
        grad_inner_one,
        grad_outer_one,
        grad_gain_two,
        grad_shift_two,
        grad_glu,
        grad_depth,
        grad_batch_gain,
        grad_batch_shift,
        grad_point,
        grad_gain_three,
        grad_shift_three,
        grad_inner_two,
        grad_outer_two,
        grad_gain_four,
        grad_shift_four,
    )


def solution(mesh):
    split = P("batch", "tm", None)
    return jax.shard_map(
        on_device,
        mesh=mesh,
        in_specs=(split, P("batch"), split) + (P(),) * 24,
        out_specs=(split, split) + (P(),) * 24,
        check_vma=False,
    )
```

```python
import functools
import math

import jax
import jax.numpy as jnp
from jax import lax
from jax.experimental import pallas as pl
from jax.experimental.pallas import tpu as pltpu
from jax.sharding import PartitionSpec as P

HEADS = 4
EPSILON = 1e-05
MASKED = -1e30
PAD = 16
LOG2E = 1.4426950408889634
LN2 = 0.6931471805599453
LANE = 128
WIDE = 256
VMEM = 48 * 1024 * 1024
bf16 = jnp.bfloat16
f32 = jnp.float32


def dot(a, b):
    return jnp.dot(a, b, preferred_element_type=f32)


def dot_nt(a, b):
    return lax.dot_general(a, b, (((1,), (1,)), ((), ())), preferred_element_type=f32)


def dot_tn(a, b):
    return lax.dot_general(a, b, (((0,), (0,)), ((), ())), preferred_element_type=f32)


def lanes(shape):
    return lax.broadcasted_iota(jnp.int32, shape, 1)


def sublanes(shape):
    return lax.broadcasted_iota(jnp.int32, shape, 0)


def kernel_call(kernel, name, operands, out, grid=(1,), after=(), scratch=(), flops=0):
    count = len(operands)
    extra = len(after)

    def body(*refs):
        kernel(*refs[:count], *refs[count + extra :])

    return pl.pallas_call(
        body,
        grid=grid,
        in_specs=[spec for _, spec in operands] + [pl.BlockSpec(memory_space=pl.ANY)] * extra,
        out_specs=[spec for _, _, spec in out],
        out_shape=[jax.ShapeDtypeStruct(shape, kind) for shape, kind, _ in out],
        scratch_shapes=list(scratch),
        compiler_params=pltpu.CompilerParams(
            vmem_limit_bytes=VMEM, dimension_semantics=("arbitrary",) * len(grid)
        ),
        cost_estimate=pl.CostEstimate(flops=flops, bytes_accessed=1000000, transcendentals=0)
        if flops
        else None,
        name=name,
    )(*[array for array, _ in operands], *after)


def whole_spec(shape):
    return pl.BlockSpec(tuple(shape), lambda *_: (0,) * len(shape))


SCALARS = pl.BlockSpec(memory_space=pltpu.SMEM)


def pick(rows, cols, start, at, size):
    row, col = sublanes((rows, cols)), lanes((rows, cols))
    return jnp.where((row - start == col - at) & (row >= start) & (row < start + size), 1.0, 0.0)


def prepare_kernel(
    vec_ref, wq_ref, wk_ref, wv_ref, wp_ref, wout_ref, glu_ref,
    q_ref, kv_ref, pos_ref, out_ref, bias_ref, back_ref, lin_ref, gate_ref,
    sin_ref, cos_ref, low_ref, sin_t_ref, cos_t_ref, *, length,
):
    D = wq_ref.shape[0]
    hs = D // HEADS
    half = D // 2
    at = half - LANE
    wq, wk, wv = wq_ref[...], wk_ref[...], wv_ref[...]
    vec = vec_ref[...]
    feature = sublanes((2 * WIDE, D))
    column = lanes((2 * WIDE, D))
    spread_rows = jnp.where(
        ((feature == column) & (column < half))
        | ((feature - WIDE == column - half) & (column >= half)),
        1.0, 0.0,
    ).astype(bf16)
    pos = dot(spread_rows, wp_ref[...]).astype(bf16)
    for h in range(HEADS):
        mid = pick(D, LANE, h * hs, at, hs)
        low = mid.astype(bf16)
        first = pick(D, LANE, h * hs, 0, hs).astype(bf16)
        q_ref[h] = dot(wq, low).astype(bf16)
        kv_ref[h, :, :LANE] = dot(wk, low).astype(bf16)
        kv_ref[h, :, LANE:] = dot(wv, first).astype(bf16)
        mid_t = pick(LANE, D, at, h * hs, hs).astype(bf16)
        pos_ref[h] = dot_nt(mid_t, pos).astype(bf16)
        bias_ref[h] = lax.dot_general(
            vec, mid, (((1,), (0,)), ((), ())), precision=lax.Precision.HIGHEST,
            preferred_element_type=f32,
        )
        out_ref[h * LANE : (h + 1) * LANE, :] = dot(
            pick(LANE, D, 0, h * hs, hs).astype(bf16), wout_ref[...]
        ).astype(bf16)
        back = None
        for i, w in enumerate((wv, wq, wk)):
            part = dot_nt(pick(WIDE, D, i * hs, h * hs, hs).astype(bf16), w)
            back = part if back is None else back + part
        back_ref[h * WIDE : (h + 1) * WIDE, :] = back.astype(bf16)
    lin_ref[...] = glu_ref[:D, :]
    gate_ref[...] = glu_ref[D:, :]

    rate = -2.0 * math.log(10000.0) / D

    def waves(position, index):
        angle = position.astype(f32) * jnp.exp(index.astype(f32) * rate)
        inside = index < half
        return jnp.where(inside, jnp.sin(angle), 0.0), jnp.where(inside, jnp.cos(angle), 0.0)

    shape = (32, WIDE)
    base_s, base_c = waves(sublanes(shape), lanes(shape))
    step_s, step_c = waves(sublanes(shape) * 32, lanes(shape))
    for i in range(length // 32):
        s, c = step_s[i : i + 1], step_c[i : i + 1]
        rows = pl.ds(i * 32, 32)
        sine = s * base_c + c * base_s
        sin_ref[rows, :] = sine
        cos_ref[rows, :] = c * base_c - s * base_s
        low_ref[rows, :] = sine.astype(bf16)
    shape = (WIDE, LANE)
    base_s, base_c = waves(lanes(shape), sublanes(shape))
    step_s, step_c = waves(lanes(shape) * LANE, sublanes(shape))
    for i in range(-(-length // LANE)):
        s, c = step_s[:, i : i + 1], step_c[:, i : i + 1]
        width = min(LANE, length - i * LANE)
        sin_t_ref[:, i * LANE : i * LANE + width] = (s * base_c + c * base_s)[:, :width]
        cos_t_ref[:, i * LANE : i * LANE + width] = (c * base_c - s * base_s)[:, :width]


def prepare(length, vec, wq, wk, wv, wp, wout, glu):
    D = wq.shape[0]
    arrays = (vec, wq, wk, wv, wp, wout, glu)
    shapes = (
        ((HEADS, D, LANE), bf16), ((HEADS, D, WIDE), bf16), ((HEADS, LANE, 2 * WIDE), bf16),
        ((HEADS * LANE, D), bf16), ((HEADS,) + vec.shape[:1] + (LANE,), f32),
        ((HEADS * WIDE, D), bf16), ((D, D), bf16), ((D, D), bf16),
        ((length, WIDE), f32), ((length, WIDE), f32), ((length, WIDE), bf16),
        ((WIDE, length), f32), ((WIDE, length), f32),
    )
    return kernel_call(
        functools.partial(prepare_kernel, length=length), "prepare",
        [(a, whole_spec(a.shape)) for a in arrays],
        [(s, k, whole_spec(s)) for s, k in shapes],
        flops=5_000_000_000,
    )


def attend_forward_kernel(
    len_ref, f_ref, q_ref, kv_ref, pos_ref, bias_ref, sin_ref, cos_ref, low_ref,
    mixed_ref, qa_ref, qb_ref, ka_ref, v_ref, *, hs, tile,
):
    T = f_ref.shape[1]
    one = 3 * hs - LANE
    scale = LOG2E / math.sqrt(hs)
    valid = len_ref[pl.program_id(0)]
    lane = lanes((tile, LANE))
    for r0 in range(0, T, tile):
        rows = pl.ds(r0, tile)
        kv = dot(f_ref[0, rows, :], kv_ref[0])
        k = kv[:, :LANE] + cos_ref[rows, LANE:]
        row = sublanes((tile, LANE)) + r0
        k = jnp.where(lane == one, jnp.where(row < valid, 0.0, MASKED), k)
        k = jnp.where((lane > one) & (lane < one + 4), 1.0, k)
        ka_ref[0, 0, rows, :LANE] = cos_ref[rows, :LANE].astype(bf16)
        ka_ref[0, 0, rows, LANE:] = k.astype(bf16)
        v = jnp.where((lane == hs) | (lane == hs + 1), 1.0, kv[:, LANE:])
        v_ref[0, 0, rows, :] = v.astype(bf16)
    for r0 in range(0, T, tile):
        rows = pl.ds(r0, tile)
        q = dot(f_ref[0, rows, :], q_ref[0])
        e = dot((q + bias_ref[0, 1:2, :]).astype(bf16), pos_ref[0])
        es, ec = e[:, :WIDE], e[:, WIDE:]
        s, c = sin_ref[rows, :], cos_ref[rows, :]
        qb = ((ec * s - es * c) * scale).astype(bf16)
        qb_ref[0, 0, rows, :] = qb
        a = (es * s + ec * c) * scale
        first = a[:, :LANE].astype(bf16)
        second = jnp.where(lane == one, 1.0, a[:, LANE:] + (q + bias_ref[0, 0:1, :]) * scale)
        qa = jnp.concatenate([first, second.astype(bf16)], axis=1)
        scores = dot_nt(qa, ka_ref[0, 0]) + dot_nt(qb, low_ref[...])
        peak = jnp.max(scores, axis=1, keepdims=True)
        p = jnp.exp2(scores - peak).astype(bf16)
        o = dot(p, v_ref[0, 0])
        total = o[:, hs : hs + 1]
        mixed_ref[0, rows, :] = (o / total).astype(bf16)
        log_total = -(peak + jnp.log2(total))
        hi = log_total.astype(bf16).astype(f32)
        mid = (log_total - hi).astype(bf16).astype(f32)
        rest = jnp.where(lane == one + 1, hi, jnp.where(lane == one + 2, mid, log_total - hi - mid))
        second = jnp.where((lane > one) & (lane < one + 4), rest, second)
        qa_ref[0, 0, rows, :LANE] = first
        qa_ref[0, 0, rows, LANE:] = second.astype(bf16)


def attend_forward(lens, frames, q, kv, pos, bias, sines, cosines, low, tile=496):
    U, T, D = frames.shape
    H = q.shape[0]

    def head(shape):
        return pl.BlockSpec((1,) + shape[1:], lambda u, h: (h, 0, 0))

    def four(width):
        return ((U, H, T, width), bf16, pl.BlockSpec((1, 1, T, width), lambda u, h: (u, h, 0, 0)))

    return kernel_call(
        functools.partial(attend_forward_kernel, hs=D // H, tile=tile), "attend_forward",
        [(lens, SCALARS), (frames, pl.BlockSpec((1, T, D), lambda u, h: (u, 0, 0)))]
        + [(a, head(a.shape)) for a in (q, kv, pos, bias)]
        + [(a, whole_spec(a.shape)) for a in (sines, cosines, low)],
        [((U, T, H * LANE), bf16, pl.BlockSpec((1, T, LANE), lambda u, h: (u, 0, h)))]
        + [four(w) for w in (WIDE, WIDE, WIDE, LANE)],
        grid=(U, H),
        flops=30_000_000_000,
    )


def attend_backward_kernel(
    qa_ref, qb_ref, ka_ref, v_ref, do_ref, mixed_ref, pos_ref, low_ref, sin_ref, cos_ref,
    d_ref, dpos_ref, bias_ref, *, hs, tile,
):
    u = pl.program_id(1)
    T = qa_ref.shape[2]
    at = 2 * hs - LANE
    inv = 1.0 / math.sqrt(hs)
    do = do_ref[0]
    wide = do.astype(f32)
    delta = -jnp.sum(wide * mixed_ref[0].astype(f32), axis=1, keepdims=True)
    hi = delta.astype(bf16).astype(f32)
    lane = lanes((T, LANE))
    dox = jnp.where(lane == hs, hi, jnp.where(lane == hs + 1, delta - hi, wide)).astype(bf16)
    qa = qa_ref[0, 0]
    qb = qb_ref[0, 0]
    da = db = None
    parts = []
    for r0 in range(0, T, tile):
        rows = pl.ds(r0, tile)
        ka = ka_ref[0, 0, rows, :]
        low = low_ref[rows, :]
        p = jnp.exp2(dot_nt(ka, qa) + dot_nt(low, qb))
        ds = (p * dot_nt(v_ref[0, 0, rows, :], dox)).astype(bf16)
        dv = dot(p.astype(bf16), do)
        dk = dot(ds, qa[:, LANE:])
        a, b = dot_tn(ka, ds), dot_tn(low, ds)
        da = a if da is None else da + a
        db = b if db is None else db + b
        parts.append((dv, dk))
    s, c = sin_ref[...], cos_ref[...]
    des = (da * s - db * c) * inv
    dec = (da * c + db * s) * inv
    de = jnp.concatenate([des.astype(bf16), dec.astype(bf16)], axis=0)
    dqp = dot(pos_ref[0], de)
    dpos = dot(de, qa[:, LANE:])
    sub = sublanes((LANE, T))
    dqc = jnp.where((sub >= at) & (sub < at + hs), da[LANE:] * inv, 0.0)
    ones = jnp.ones((16, T), bf16)
    bias = jnp.where(
        sublanes((16, LANE)) == 0, dot_nt(ones, dqc.astype(bf16)), dot_nt(ones, dqp.astype(bf16))
    )

    @pl.when(u == 0)
    def _():
        dpos_ref[0] = dpos
        bias_ref[0] = bias

    @pl.when(u > 0)
    def _():
        dpos_ref[0] += dpos
        bias_ref[0] += bias

    dq = jnp.transpose(dqc + dqp)
    dq = pltpu.roll(jnp.concatenate([jnp.zeros((T, LANE), f32), dq], axis=1), WIDE - hs, 1)
    lane = lanes((tile, LANE))
    for i, (dv, dk) in enumerate(parts):
        rows = pl.ds(i * tile, tile)
        dq_rows = dq[i * tile : (i + 1) * tile]
        d_ref[0, rows, :LANE] = jnp.where(lane < hs, dv, dq_rows[:, :LANE]).astype(bf16)
        inside = (lane >= at) & (lane < at + hs)
        d_ref[0, rows, LANE:] = jnp.where(inside, dk * LN2, dq_rows[:, LANE:]).astype(bf16)


def attend_backward(head_size, first, count, qa, qb, ka, v, do, mixed, pos, low, sin_t, cos_t, after, tile=496):
    U, H, T, W = qa.shape

    def four(array):
        return array, pl.BlockSpec((1, 1) + array.shape[2:], lambda h, u: (u, first + h, 0, 0))

    def lane_block(array):
        return array, pl.BlockSpec((1, T, LANE), lambda h, u: (u, 0, first + h))

    return kernel_call(
        functools.partial(attend_backward_kernel, hs=head_size, tile=tile), "attend_backward",
        [four(qa), four(qb), four(ka), four(v), lane_block(do), lane_block(mixed)]
        + [(pos, pl.BlockSpec((1,) + pos.shape[1:], lambda h, u: (first + h, 0, 0)))]
        + [(a, whole_spec(a.shape)) for a in (low, sin_t, cos_t)],
        [
            ((U, T, count * W), bf16, pl.BlockSpec((1, T, W), lambda h, u: (u, 0, h))),
            ((count, 2 * W, LANE), f32, pl.BlockSpec((1, 2 * W, LANE), lambda h, u: (h, 0, 0))),
            ((count, 16, LANE), f32, pl.BlockSpec((1, 16, LANE), lambda h, u: (h, 0, 0))),
        ],
        grid=(count, U),
        after=after,
        flops=count * U * 5_500_000_000,
    )


def fill_padded(buf, value):
    T = value.shape[0]
    zero = jnp.zeros((PAD, buf.shape[1]), f32)
    buf[0:PAD, :] = zero
    buf[T + PAD : T + 2 * PAD, :] = zero
    buf[PAD : T + PAD, :] = value


def fill_weights(wide, w_ref, taps):
    for o in range(taps):
        wide[o] = jnp.broadcast_to(w_ref[o : o + 1, :], (8, LANE))


def tall(values):
    return values.reshape(values.shape[0] // 8, 8, LANE)


def chunks(T, step, body, carry):
    full = T // step
    carry = lax.fori_loop(
        0, full, lambda i, c: body(pl.multiple_of(i * step, 8), step, c), carry
    )
    return body(full * step, T - full * step, carry) if T % step else carry


def conv_forward_kernel(len_ref, x_ref, w_ref, out_ref, stat_ref, padded, wide, *, taps, step):
    u = pl.program_id(1)
    T = x_ref.shape[1]
    half = (taps - 1) // 2
    fill_padded(padded, x_ref[0].astype(f32))
    fill_weights(wide, w_ref, taps)
    valid = len_ref[u]

    def body(base, rows, sums):
        total = None
        for o in range(taps):
            term = wide[o] * tall(padded[pl.ds(base + PAD - half + o, rows), :])
            total = term if total is None else total + term
        out_ref[0, pl.ds(base, rows), :] = total.reshape(rows, LANE)
        row = 8 * lax.broadcasted_iota(jnp.int32, (rows // 8, 8, LANE), 0)
        row = row + lax.broadcasted_iota(jnp.int32, (rows // 8, 8, LANE), 1) + base
        masked = jnp.where(row < valid, total, 0.0)
        return sums[0] + jnp.sum(masked, axis=0), sums[1] + jnp.sum(masked * total, axis=0)

    zero = jnp.zeros((8, LANE), f32)
    first, second = chunks(T, step, body, (zero, zero))
    count = jnp.full((1, LANE), valid, jnp.int32).astype(f32)
    stat = jnp.concatenate(
        [
            jnp.sum(first, axis=0, keepdims=True),
            jnp.sum(second, axis=0, keepdims=True),
            count,
            jnp.zeros((5, LANE), f32),
        ],
        axis=0,
    )

    @pl.when(u == 0)
    def _():
        stat_ref[...] = stat

    @pl.when(u > 0)
    def _():
        stat_ref[...] += stat


def conv_forward(lens, x, w, step=256):
    U, T, C = x.shape
    block = pl.BlockSpec((1, T, LANE), lambda c, u: (u, 0, c))
    return kernel_call(
        functools.partial(conv_forward_kernel, taps=w.shape[0], step=step), "conv_forward",
        [(lens, SCALARS), (x, block), (w, pl.BlockSpec((w.shape[0], LANE), lambda c, u: (0, c)))],
        [((U, T, C), f32, block), ((8, C), f32, pl.BlockSpec((8, LANE), lambda c, u: (0, c)))],
        grid=(pl.cdiv(C, LANE), U),
        scratch=[pltpu.VMEM((T + 2 * PAD, LANE), f32), pltpu.VMEM((w.shape[0], 8, LANE), f32)],
        flops=10_000_000_000,
    )


def batch_moments(stat):
    count = stat[2:3, :]
    mean = stat[0:1, :] / count
    return count, mean, lax.rsqrt(stat[1:2, :] / count - mean * mean + EPSILON)


def conv_backward_kernel(
    len_ref, x_ref, dz_ref, conv_ref, w_ref, stat_ref, sums_ref, vec_ref, gs_ref, gw_ref,
    padded_x, padded_g, wide, *, taps, step, gain_row,
):
    u = pl.program_id(1)
    T = x_ref.shape[1]
    half = (taps - 1) // 2
    valid = len_ref[u]
    count, mean, rstd = batch_moments(stat_ref[...])
    gain = vec_ref[gain_row : gain_row + 1, :]
    grad_var = -0.5 * rstd * rstd * (sums_ref[0:1, :] * gain)
    grad_mean = -rstd * (sums_ref[1:2, :] * gain) - 2.0 * mean * grad_var
    shift = grad_mean / count
    slope = 2.0 * grad_var / count
    row = sublanes((T, LANE))
    g = dz_ref[0] * rstd + jnp.where(row < valid, shift + slope * conv_ref[0], 0.0)
    fill_padded(padded_g, g)
    fill_padded(padded_x, x_ref[0].astype(f32))

    fill_weights(wide, w_ref, taps)

    def spread(base, rows, carry):
        total = None
        for o in range(taps):
            term = wide[o] * tall(padded_g[pl.ds(base + PAD + half - o, rows), :])
            total = term if total is None else total + term
        gs_ref[0, pl.ds(base, rows), :] = total.reshape(rows, LANE)
        return carry

    chunks(T, step, spread, 0)

    zero = jnp.zeros((8, LANE), f32)

    def relate(base, rows, carry):
        centre = tall(padded_g[pl.ds(base + PAD, rows), :])
        new = []
        for o, kept in enumerate(carry):
            moved = tall(padded_x[pl.ds(base + PAD - half + o, rows), :])
            new.append(kept + jnp.sum(centre * moved, axis=0))
        return tuple(new)

    sums = chunks(T, step // 2, relate, (zero,) * taps)
    rows = [jnp.sum(s, axis=0, keepdims=True) for s in sums]
    gw = jnp.concatenate(rows + [jnp.zeros((-taps % 8, LANE), f32)], axis=0)

    @pl.when(u == 0)
    def _():
        gw_ref[...] = gw

    @pl.when(u > 0)
    def _():
        gw_ref[...] += gw


def conv_backward(lens, x, dz, conv, w, stat, sums, vec, gain_row, step=256):
    U, T, C = x.shape
    taps = w.shape[0]
    block = pl.BlockSpec((1, T, LANE), lambda c, u: (u, 0, c))

    def channel(array):
        return array, pl.BlockSpec((array.shape[0], LANE), lambda c, u: (0, c))

    return kernel_call(
        functools.partial(conv_backward_kernel, taps=taps, step=step, gain_row=gain_row),
        "conv_backward",
        [(lens, SCALARS), (x, block), (dz, block), (conv, block)]
        + [channel(a) for a in (w, stat, sums, vec)],
        [((U, T, C), f32, block), ((taps + -taps % 8, C), f32, pl.BlockSpec((taps + -taps % 8, LANE), lambda c, u: (0, c)))],
        grid=(pl.cdiv(C, LANE), U),
        scratch=[pltpu.VMEM((T + 2 * PAD, LANE), f32)] * 2 + [pltpu.VMEM((taps, 8, LANE), f32)],
        flops=20_000_000_000,
    )


CONTENT, POSITION, GAIN1, SHIFT1, GAIN2, SHIFT2, BGAIN, BSHIFT, GAIN3, SHIFT3, GAIN4, SHIFT4 = range(12)


def vector(ref, index):
    return ref[index : index + 1, :]


def sigmoid(x):
    return 0.5 * jnp.tanh(0.5 * x) + 0.5


def unit_norm(values):
    centred = values - jnp.mean(values, axis=-1, keepdims=True)
    inv_std = lax.rsqrt(jnp.mean(centred * centred, axis=-1, keepdims=True) + EPSILON)
    return centred * inv_std, inv_std


def unit_norm_back(unit, inv_std, gain, upstream):
    scaled = upstream * gain
    return inv_std * (
        scaled
        - jnp.mean(scaled, axis=-1, keepdims=True)
        - unit * jnp.mean(scaled * unit, axis=-1, keepdims=True)
    )


def col_sum(values):
    return jnp.sum(values, axis=0, keepdims=True)


def accumulate(step, refs, values):
    @pl.when(step == 0)
    def _():
        for ref, value in zip(refs, values):
            ref[...] = value

    @pl.when(step > 0)
    def _():
        for ref, value in zip(refs, values):
            ref[...] += value


def add_into(step, ref, value):
    rows, cols = value.shape

    @pl.when(step == 0)
    def _():
        ref[...] = jnp.zeros(ref.shape, f32)
        ref[:rows, :cols] = value

    @pl.when(step > 0)
    def _():
        ref[:rows, :cols] += value


def up(value, unit):
    return -(-value // unit) * unit


def put_blocks(packed_ref, at, value):
    rows, cols = value.shape
    for c in range(0, cols, LANE):
        packed_ref[at : at + rows, :] = value[:, c : c + LANE].astype(bf16)
        at += rows
    return at


def row_valid(len_ref, step, tile, length):
    per = length // tile
    row = sublanes((tile, 1)) + lax.rem(step, per) * tile
    return row < len_ref[lax.div(step, per)]


def first_kernel(
    len_ref, f_ref, mixed_ref, vec_ref, wout_ref, wi_ref, wo_ref, wl_ref, wg_ref,
    x1_ref, r1_ref, u_ref, x2_ref, r2_ref, lin_ref, sig_ref, spread_ref, *, tile, length,
):
    resid = f_ref[...].astype(f32) + dot(mixed_ref[...], wout_ref[...])
    unit, inv_std = unit_norm(resid)
    x1_ref[...] = unit
    r1_ref[...] = inv_std
    hidden = unit * vector(vec_ref, GAIN1) + vector(vec_ref, SHIFT1)
    inner = dot(hidden.astype(bf16), wi_ref[...])
    u_ref[...] = inner.astype(bf16)
    active = (inner * sigmoid(inner)).astype(bf16)
    resid = hidden + dot_nt(active, wo_ref[...])
    unit, inv_std = unit_norm(resid)
    x2_ref[...] = unit
    r2_ref[...] = inv_std
    entry = (unit * vector(vec_ref, GAIN2) + vector(vec_ref, SHIFT2)).astype(bf16)
    lin = dot_nt(entry, wl_ref[...])
    sig = sigmoid(dot_nt(entry, wg_ref[...]))
    lin_ref[...] = lin.astype(bf16)
    sig_ref[...] = sig.astype(bf16)
    valid = row_valid(len_ref, pl.program_id(0), tile, length)
    spread_ref[...] = jnp.where(valid, lin * sig, 0.0).astype(bf16)


def second_kernel(
    x2_ref, conv_ref, cot_ref, stat_ref, vec_ref, wp_ref, wi_ref, wo_ref,
    out_ref, dz_ref, g3_ref, small_ref, dwp_ref, dwi_ref, dwo_ref, sum_p, sum_i, sum_o,
):
    step = pl.program_id(0)
    _, mean, rstd = batch_moments(stat_ref[...])
    centred = (conv_ref[...] - mean) * rstd
    batch_gain = vector(vec_ref, BGAIN)
    normed = centred * batch_gain + vector(vec_ref, BSHIFT)
    sig_n = sigmoid(normed)
    swished = (normed * sig_n).astype(bf16)
    hidden_two = x2_ref[...] * vector(vec_ref, GAIN2) + vector(vec_ref, SHIFT2)
    unit3, inv3 = unit_norm(hidden_two + dot(swished, wp_ref[...]))
    gain3 = vector(vec_ref, GAIN3)
    hidden = unit3 * gain3 + vector(vec_ref, SHIFT3)
    entry = hidden.astype(bf16)
    inner = dot(entry, wi_ref[...])
    sig = sigmoid(inner)
    active = (inner * sig).astype(bf16)
    unit4, inv4 = unit_norm(hidden + dot_nt(active, wo_ref[...]))
    gain4 = vector(vec_ref, GAIN4)
    out_ref[...] = (unit4 * gain4 + vector(vec_ref, SHIFT4)).astype(bf16)
    upstream = cot_ref[...].astype(f32)
    grad4 = unit_norm_back(unit4, inv4, gain4, upstream)
    low4 = grad4.astype(bf16)
    dwo = dot_tn(low4, active)
    dinner = (dot(low4, wo_ref[...]) * (sig * (1.0 + inner * (1.0 - sig)))).astype(bf16)
    dwi = dot_tn(entry, dinner)
    up3 = grad4 + dot_nt(dinner, wi_ref[...])
    grad3 = unit_norm_back(unit3, inv3, gain3, up3)
    g3_ref[...] = grad3
    low3 = grad3.astype(bf16)
    dwp = dot_tn(swished, low3)
    dnormed = dot_nt(low3, wp_ref[...]) * (sig_n * (1.0 + normed * (1.0 - sig_n)))
    dz_ref[...] = dnormed * batch_gain
    small = jnp.concatenate(
        [
            col_sum(dnormed * centred), col_sum(dnormed),
            col_sum(up3 * unit3), col_sum(up3),
            col_sum(upstream * unit4), col_sum(upstream),
            jnp.zeros((2, centred.shape[1]), f32),
        ],
        axis=0,
    )
    accumulate(step, (small_ref, sum_p, sum_i, sum_o), (small, dwp, dwi, dwo))

    @pl.when(step == pl.num_programs(0) - 1)
    def _():
        dwp_ref[...] = sum_p[...].astype(bf16)
        dwi_ref[...] = sum_i[...].astype(bf16)
        dwo_ref[...] = sum_o[...].astype(bf16)


def third_kernel(
    len_ref, gs_ref, lin_ref, sig_ref, x2_ref, r2_ref, g3_ref, u_ref, x1_ref, r1_ref, mixed_ref,
    vec_ref, wl_ref, wg_ref, wi_ref, wo_ref, wout_ref,
    g1_ref, gm_ref, small_ref, packed_ref, sum_i, sum_o, sum_l, sum_g, sum_out, *, tile, length,
):
    step = pl.program_id(0)
    valid = row_valid(len_ref, step, tile, length)
    sig_g = sig_ref[...].astype(f32)
    gated = jnp.where(valid, gs_ref[...], 0.0) * sig_g
    low_l = gated.astype(bf16)
    low_g = (gated * lin_ref[...].astype(f32) * (1.0 - sig_g)).astype(bf16)
    unit2 = x2_ref[...]
    gain2 = vector(vec_ref, GAIN2)
    entry2 = (unit2 * gain2 + vector(vec_ref, SHIFT2)).astype(bf16)
    dwl = dot_tn(low_l, entry2)
    dwg = dot_tn(low_g, entry2)
    up2 = g3_ref[...] + dot(low_l, wl_ref[...]) + dot(low_g, wg_ref[...])
    grad2 = unit_norm_back(unit2, r2_ref[...], gain2, up2)
    low2 = grad2.astype(bf16)
    inner = u_ref[...].astype(f32)
    sig = sigmoid(inner)
    active = (inner * sig).astype(bf16)
    dwo = dot_tn(low2, active)
    dinner = (dot(low2, wo_ref[...]) * (sig * (1.0 + inner * (1.0 - sig)))).astype(bf16)
    unit1 = x1_ref[...]
    gain1 = vector(vec_ref, GAIN1)
    entry1 = (unit1 * gain1 + vector(vec_ref, SHIFT1)).astype(bf16)
    dwi = dot_tn(entry1, dinner)
    up1 = grad2 + dot_nt(dinner, wi_ref[...])
    grad1 = unit_norm_back(unit1, r1_ref[...], gain1, up1)
    g1_ref[...] = grad1
    low1 = grad1.astype(bf16)
    dwout = dot_tn(mixed_ref[...], low1)
    gm_ref[...] = dot_nt(low1, wout_ref[...]).astype(bf16)
    small = jnp.concatenate(
        [
            col_sum(up1 * unit1), col_sum(up1),
            col_sum(up2 * unit2), col_sum(up2),
            jnp.zeros((4, unit1.shape[1]), f32),
        ],
        axis=0,
    )
    accumulate(step, (small_ref, sum_out), (small, dwout))
    for ref, value in ((sum_i, dwi), (sum_o, dwo), (sum_l, dwl), (sum_g, dwg)):
        add_into(step, ref, value)

    @pl.when(step == pl.num_programs(0) - 1)
    def _():
        D = unit1.shape[1]
        hs = D // HEADS
        at = 0
        for ref in (sum_i, sum_o, sum_l, sum_g):
            at = put_blocks(packed_ref, at, ref[...])
        rows = sum_l.shape[0]
        compact = jnp.zeros(sum_l.shape, f32)
        for h in range(HEADS):
            chosen = pick(rows, LANE, h * hs, 0, hs).astype(bf16)
            part = dot(chosen, sum_out[h * LANE : (h + 1) * LANE, :].astype(bf16))
            compact += jnp.concatenate(
                [part, jnp.zeros((rows, sum_l.shape[1] - D), f32)], axis=1
            )
        at = put_blocks(packed_ref, at, compact)
        if at < packed_ref.shape[0]:
            packed_ref[at:, :] = jnp.zeros((packed_ref.shape[0] - at, LANE), bf16)


def last_kernel(*refs, heads):
    d_refs, pos_refs, bias_refs = refs[:heads], refs[heads + 2 : 2 * heads + 2], refs[2 * heads + 2 : 3 * heads + 2]
    f_ref, g1_ref = refs[heads : heads + 2]
    back_ref, small_ref, depth_ref, out_ref, packed_ref, sum_w = refs[3 * heads + 2 :]
    step = pl.program_id(0)
    grads = jnp.concatenate([ref[...] for ref in d_refs], axis=1)
    out_ref[...] = (g1_ref[...] + dot(grads, back_ref[...])).astype(bf16)
    add_into(step, sum_w, dot_tn(f_ref[...], grads))

    @pl.when(step == pl.num_programs(0) - 1)
    def _():
        D = out_ref.shape[1]
        wide = up(D, LANE)
        spare = jnp.zeros((16, wide - D), f32)
        at = put_blocks(packed_ref, 0, sum_w[...])
        kept = up(D // 2, 16)
        for ref in pos_refs:
            for half in range(2):
                at = put_blocks(packed_ref, at, ref[0, half * WIDE : half * WIDE + kept, :])
        for ref in bias_refs:
            at = put_blocks(packed_ref, at, ref[0])
        small = jnp.concatenate([small_ref[...], jnp.zeros((8, D), f32)], axis=0)
        at = put_blocks(packed_ref, at, jnp.concatenate([small, spare], axis=1))
        depth = depth_ref[...]
        spare = jnp.zeros((depth.shape[0], wide - D), f32)
        at = put_blocks(packed_ref, at, jnp.concatenate([depth, spare], axis=1))
        if at < packed_ref.shape[0]:
            packed_ref[at:, :] = jnp.zeros((packed_ref.shape[0] - at, LANE), bf16)


def middle_rows(D, F, unit):
    blocks = 2 * (up(F, LANE) // LANE) + 3 * (up(D, LANE) // LANE)
    return up(blocks * up(D, 16), unit)


def late_rows(D, taps, unit):
    blocks = up(D, LANE) // LANE
    rows = HEADS * WIDE // LANE * up(D, 16) + HEADS * (2 * up(D // 2, 16) + 16)
    return up(rows + blocks * (16 + up(taps, 16)), unit)


def unpack_kernel(
    bit_ref, value_ref, other_ref, bias_ref,
    wi1_ref, wo1_ref, glu_ref, wout_ref, q_ref, k_ref, v_ref, pos_ref, vec_ref, depth_ref, buf, *, middle, late,
):
    n = value_ref.shape[0]
    bit = bit_ref[0]
    buf[pl.ds(pl.multiple_of(bit * n, 16), n), :] = value_ref[...]
    buf[pl.ds(pl.multiple_of((1 - bit) * n, 16), n), :] = other_ref[...]
    D, F = wi1_ref.shape
    hs = D // HEADS
    half = D // 2
    at = half - LANE
    one = 3 * hs - LANE
    place = {"middle": 0, "late": 0}

    def fetch(kind, rows):
        cut = middle if kind == "middle" else late
        start = place[kind]
        place[kind] += rows
        parts = []
        while rows:
            shard, offset = divmod(start, cut)
            count = min(rows, cut - offset)
            base = shard * (middle + late) + offset + (0 if kind == "middle" else middle)
            parts.append(buf[base : base + count, :])
            start += count
            rows -= count
        return jnp.concatenate(parts, axis=0) if len(parts) > 1 else parts[0]

    def spread_blocks(ref, first, kind, rows, cols):
        for c in range(0, cols, LANE):
            width = min(LANE, cols - c)
            block = fetch(kind, up(rows, 16))[:rows, :width].astype(f32)
            ref[first : first + rows, c : c + width] = block

    spread_blocks(wi1_ref, 0, "middle", D, F)
    spread_blocks(wo1_ref, 0, "middle", D, F)
    spread_blocks(glu_ref, 0, "middle", D, D)
    spread_blocks(glu_ref, D, "middle", D, D)
    spread_blocks(wout_ref, 0, "middle", D, D)
    sums = [None, None, None]
    for h in range(HEADS):
        block = jnp.concatenate([fetch("late", up(D, 16)), fetch("late", up(D, 16))], axis=1)
        for i in range(3):
            part = dot(block, pick(WIDE, D, i * hs, h * hs, hs).astype(bf16))
            sums[i] = part if sums[i] is None else sums[i] + part
    v_ref[...] = sums[0][:D]
    q_ref[...] = sums[1][:D]
    k_ref[...] = sums[2][:D]
    halves = [None, None]
    scale = math.sqrt(hs) / LOG2E
    for h in range(HEADS):
        change = bias_ref[h, 1:2, :] - bias_ref[h, 0:1, :]
        chosen = pick(LANE, D, at, h * hs, hs)
        for i in range(2):
            raw = fetch("late", up(half, 16)).astype(f32)
            full = raw * scale + raw[:, one : one + 1] * change
            part = lax.dot_general(
                full, chosen, (((1,), (0,)), ((), ())), precision=lax.Precision.HIGHEST,
                preferred_element_type=f32,
            )
            halves[i] = part if halves[i] is None else halves[i] + part
    pos_ref[:half, :] = halves[0][:half]
    pos_ref[half:, :] = halves[1][:half]
    total = None
    for h in range(HEADS):
        part = dot(fetch("late", 16), pick(LANE, D, at, h * hs, hs).astype(bf16))
        total = part if total is None else total + part
    vec_ref[0:8, :] = total[:8]
    spread_blocks(vec_ref.at[8:16], 0, "late", 8, D)
    spread_blocks(depth_ref, 0, "late", depth_ref.shape[0], D)


def unpack(bit, value, other, bias, D, F, taps, middle, late, after):
    arrays = (value, other, bias)
    shapes = (
        (D, F), (D, F), (2 * D, D), (D, D), (D, D), (D, D), (D, D), (D, D),
        (16, D), (up(taps, 8), D),
    )
    return kernel_call(
        functools.partial(unpack_kernel, middle=middle, late=late), "unpack",
        [(bit, SCALARS)] + [(a, whole_spec(a.shape)) for a in arrays],
        [(s, f32, whole_spec(s)) for s in shapes],
        after=after, scratch=[pltpu.VMEM((2 * value.shape[0], LANE), bf16)], flops=1000,
    )


def widen_kernel(*refs):
    count = len(refs) // 2
    for source, target in zip(refs[:count], refs[count:]):
        target[...] = source[...].astype(f32)


def widen(arrays):
    return kernel_call(
        widen_kernel, "widen", [(a, whole_spec(a.shape)) for a in arrays],
        [(a.shape, f32, whole_spec(a.shape)) for a in arrays], flops=1000,
    )


def row_call(kernel, name, rows, tile, scalars, tiled, fixed, tiled_out, fixed_out, after=(), scratch=(), flops=0):
    def block(width):
        return pl.BlockSpec((tile, width), lambda i: (i, 0))

    return kernel_call(
        kernel, name,
        [(a, SCALARS) for a in scalars]
        + [(a, block(a.shape[1])) for a in tiled]
        + [(a, whole_spec(a.shape)) for a in fixed],
        [((rows, w), d, block(w)) for w, d in tiled_out]
        + [(s, k, whole_spec(s)) for s, k in fixed_out],
        grid=(rows // tile,),
        after=after,
        scratch=[pltpu.VMEM(s, f32) for s in scratch],
        flops=flops,
    )


def first_block(lens, length, tiled, fixed, tile=496):
    rows, D = tiled[0].shape
    F = fixed[2].shape[1]
    return row_call(
        functools.partial(first_kernel, tile=tile, length=length), "first_block", rows, tile,
        (lens,), tiled, fixed,
        ((D, f32), (1, f32), (F, bf16), (D, f32), (1, f32), (D, bf16), (D, bf16), (D, bf16)), (),
        flops=15_000_000_000,
    )


def second_block(tiled, fixed, tile=496):
    rows, D = tiled[0].shape
    F = fixed[3].shape[1]
    return row_call(
        second_kernel, "second_block", rows, tile, (), tiled, fixed,
        ((D, bf16), (D, f32), (D, f32)),
        (((8, D), f32), ((D, D), bf16), ((D, F), bf16), ((D, F), bf16)),
        scratch=((D, D), (D, F), (D, F)),
        flops=30_000_000_000,
    )


def third_block(lens, length, unit, tiled, fixed, after, tile=496):
    rows, D = tiled[0].shape
    M = tiled[-1].shape[1]
    F = fixed[3].shape[1]
    tall, wide, square = up(D, 16), up(F, LANE), up(D, LANE)
    return row_call(
        functools.partial(third_kernel, tile=tile, length=length), "third_block", rows, tile,
        (lens,), tiled, fixed, ((D, f32), (M, bf16)),
        (((8, D), f32), ((middle_rows(D, F, unit), LANE), bf16)),
        scratch=((tall, wide), (tall, wide), (tall, square), (tall, square), (M, D)),
        after=after, flops=30_000_000_000,
    )


def last_block(unit, heads, source, g1, pos, bias, fixed, taps, after, tile=496):
    rows, D = source.shape
    return row_call(
        functools.partial(last_kernel, heads=len(heads)), "last_block", rows, tile,
        (), (*heads, source, g1), (*pos, *bias, *fixed),
        ((D, bf16),), (((late_rows(D, taps, unit), LANE), bf16),),
        scratch=((up(D, 16), fixed[0].shape[0]),),
        after=after, flops=7_000_000_000,
    )


def swap_pairs(size, distance):
    return [(i, i ^ distance) for i in range(size)]


def axis_steps(axis, first=1):
    size = lax.axis_size(axis)
    steps = []
    distance = first
    while distance < size:
        steps.append((axis, size, distance))
        distance *= 2
    return steps


def butterfly_sum(value):
    for axis, size, distance in axis_steps("batch") + axis_steps("tm"):
        value = value + lax.ppermute(value, axis, swap_pairs(size, distance))
    return value


def scatter_step(value, step):
    axis, size, distance = step
    bit = (lax.axis_index(axis) // distance) % 2
    half = value.shape[0] // 2
    sent = lax.dynamic_slice_in_dim(value, (1 - bit) * half, half, 0).astype(bf16)
    kept = lax.dynamic_slice_in_dim(value, bit * half, half, 0).astype(f32)
    got = lax.ppermute(sent, axis, swap_pairs(size, distance))
    return kept + got.astype(f32), got


def gather_step(value, step):
    axis, size, distance = step
    bit = (lax.axis_index(axis) // distance) % 2
    other = lax.ppermute(value, axis, swap_pairs(size, distance))
    return jnp.concatenate(
        [jnp.where(bit == 0, value, other), jnp.where(bit == 0, other, value)]
    )


def ring_plan():
    batch = axis_steps("batch")
    return batch[:1], batch[1:2], axis_steps("tm"), batch[2:]


def exchange_sum(value, step):
    axis, size, distance = step
    low = value.astype(bf16)
    got = lax.ppermute(low, axis, swap_pairs(size, distance))
    return low.astype(f32) + got.astype(f32), got


def scatter_sum(value, after=()):
    core, across, tm, rest = ring_plan()
    arrived = []
    for step in core:
        value, got = scatter_step(value, step)
        arrived.append([got])
    half = value.shape[0] // 2
    streams = [value[:half], value[half:]]
    for steps in zip(across + tm, tm + across):
        pair = [scatter_step(v, s) for v, s in zip(streams, steps)]
        streams = [p[0] for p in pair]
        arrived.append([p[1] for p in pair])
    value = jnp.concatenate(streams)
    for index, step in enumerate(rest):
        if after and index == len(rest) - 1:
            value = hold(value, after)
        value, got = exchange_sum(value, step)
        arrived.append([got])
    return value.astype(bf16), arrived


def gather_all(streams):
    core, across, tm, rest = ring_plan()
    for steps in list(zip(across + tm, tm + across))[::-1]:
        streams = [gather_step(v, s) for v, s in zip(streams, steps)]
    value = jnp.concatenate(streams)
    for step in core[:0:-1]:
        value = gather_step(value, step)
    axis, size, distance = core[0]
    bit = (lax.axis_index(axis) // distance) % 2
    return bit, value, lax.ppermute(value, axis, swap_pairs(size, distance))


def scatter_parts():
    core, across, tm, rest = ring_plan()
    return 2 ** (len(core) + 1 + len(across) + len(tm))


def hold_kernel(a_ref, out_ref):
    out_ref[...] = a_ref[...]


def hold(value, after):
    spec = whole_spec(value.shape)
    return kernel_call(
        hold_kernel, "hold", [(value, spec)], [(value.shape, value.dtype, spec)], after=after,
        flops=1000,
    )[0]


def join_kernel(a_ref, b_ref, first_ref, second_ref):
    a, b = a_ref.shape[0] // 2, b_ref.shape[0] // 2
    for i, ref in enumerate((first_ref, second_ref)):
        ref[:a, :] = a_ref[i * a : (i + 1) * a, :]
        ref[a:, :] = b_ref[i * b : (i + 1) * b, :]


def join_shards(a, b, after):
    shape = ((a.shape[0] + b.shape[0]) // 2, LANE)
    return kernel_call(
        join_kernel, "join_shards", [(x, whole_spec(x.shape)) for x in (a, b)],
        [(shape, a.dtype, whole_spec(shape))] * 2, after=after, flops=1000,
    )


def rotation(size, shift):
    return [(i, (i + shift) % size) for i in range(size)]


def arrange(pieces, mine):
    parts = len(pieces)
    ordered = []
    for place in range(parts):
        shift = lax.rem(mine - place + parts, parts)
        chosen = pieces[0]
        for k in range(1, parts):
            chosen = jnp.where(shift == k, pieces[k], chosen)
        ordered.append(chosen)
    return ordered


def to_utterances(block, mine):
    parts = lax.axis_size("tm")
    own = block.shape[0] // parts
    pieces = []
    for shift in range(parts):
        piece = lax.dynamic_slice_in_dim(block, lax.rem(mine + shift, parts) * own, own, 0)
        pieces.append(lax.ppermute(piece, "tm", rotation(parts, shift)) if shift else piece)
    return jnp.concatenate(arrange(pieces, mine), axis=1)


def send_frames(whole, mine):
    parts = lax.axis_size("tm")
    rows = whole.shape[1] // parts
    pieces = []
    for shift in range(1, parts):
        piece = lax.dynamic_slice_in_dim(whole, lax.rem(mine + shift, parts) * rows, rows, 1)
        pieces.append(lax.ppermute(piece, "tm", rotation(parts, shift)))
    return pieces


def assemble_kernel(mine_ref, whole_ref, *refs):
    out_ref = refs[-1]
    parts = len(refs)
    mine = mine_ref[0]
    place = pl.program_id(0)
    rows = out_ref.shape[1]
    shift = lax.rem(mine - place + parts, parts)

    @pl.when(shift == 0)
    def _():
        out_ref[...] = whole_ref[:, pl.ds(pl.multiple_of(mine * rows, 8), rows), :]

    for k in range(1, parts):

        @pl.when(shift == k)
        def _():
            out_ref[...] = refs[k - 1][...]


def assemble(whole, pieces, mine):
    U, T, D = whole.shape
    parts = len(pieces) + 1
    rows = T // parts
    return kernel_call(
        assemble_kernel, "assemble",
        [(mine.astype(jnp.int32).reshape(1), SCALARS), (whole, whole_spec(whole.shape))]
        + [(p, whole_spec(p.shape)) for p in pieces],
        [((parts * U, rows, D), whole.dtype, pl.BlockSpec((U, rows, D), lambda p: (p, 0, 0)))],
        grid=(parts,), flops=1000,
    )[0]


def on_device(
    frames,
    lengths,
    cotangent,
    query_weight,
    key_weight,
    value_weight,
    position_weight,
    content_bias,
    position_bias,
    output_weight,
    attend_gain,
    attend_shift,
    inner_first,
    outer_first,
    first_gain,
    first_shift,
    glu_weight,
    depth_weight,
    batch_gain,
    batch_shift,
    point_weight,
    conv_gain,
    conv_shift,
    inner_second,
    outer_second,
    second_gain,
    second_shift,
):
    seq_local, local_rows, D = frames.shape
    H = HEADS
    hs = D // H
    F = inner_first.shape[1]
    taps = depth_weight.shape[0]
    half = D // 2
    at = half - LANE
    parts = lax.axis_size("tm")
    mine = lax.axis_index("tm")
    unit = 16 * scatter_parts()
    U = seq_local // parts
    T = local_rows * parts
    R = U * T
    lens = lax.dynamic_slice_in_dim(lengths, mine * U, U)

    whole = to_utterances(frames, mine)
    source = whole.reshape(R, D)
    zero = jnp.zeros((D,), f32)
    vec = jnp.stack(
        [
            content_bias, position_bias, attend_gain, attend_shift, first_gain, first_shift,
            batch_gain, batch_shift, conv_gain, conv_shift, second_gain, second_shift,
            zero, zero, zero, zero,
        ]
    )
    outer_first_t, outer_second_t = outer_first.T, outer_second.T
    (
        query_x, kv_x, pos_x, output_x, bias_x, back_x, lin_t, gate_t,
        sines, cosines, sines_low, sines_t, cosines_t,
    ) = prepare(
        T, vec, query_weight, key_weight, value_weight, position_weight, output_weight, glu_weight.T
    )

    mixed, qa, qb, ka, va = attend_forward(
        lens, whole, query_x, kv_x, pos_x, bias_x, sines, cosines, sines_low
    )
    place, _ = lax.optimization_barrier((mine, mixed[0, :16, :LANE]))
    upstream = to_utterances(cotangent, place).reshape(R, D)
    mixed_flat = mixed.reshape(R, H * LANE)
    unit_one, inv_one, inner_one, unit_two, inv_two, linear, sigma, spread = first_block(
        lens, T, (source, mixed_flat),
        (vec, output_x, inner_first, outer_first_t, lin_t, gate_t),
    )
    spread = spread.reshape(U, T, D)
    conv_out, stat = conv_forward(lens, spread, depth_weight)
    stat = butterfly_sum(stat)
    block_out, grad_centred, grad_three, sums, grad_point, grad_inner_two, grad_outer_two = (
        second_block(
            (unit_two, conv_out.reshape(R, D), upstream),
            (stat, vec, point_weight, inner_second, outer_second_t),
        )
    )
    early = lax.psum((grad_inner_two, grad_outer_two, grad_point), ("batch", "tm"))
    block_out = block_out.reshape(U, T, D)
    out_pieces = send_frames(block_out, mine)
    sums = butterfly_sum(sums)
    def backward(stat, sums, grad_centred, grad_three):
        grad_spread, grad_depth = conv_backward(
            lens, spread, grad_centred.reshape(U, T, D), conv_out, depth_weight, stat, sums, vec, BGAIN
        )
        grad_one, grad_mixed, small_one, middle = (
            third_block(
                lens, T, unit,
                (
                    grad_spread.reshape(R, D), linear, sigma, unit_two, inv_two, grad_three,
                    inner_one, unit_one, inv_one, mixed_flat,
                ),
                (vec, lin_t, gate_t, inner_first, outer_first_t, output_x),
                after=tuple(out_pieces),
            )
        )
        grad_mixed = grad_mixed.reshape(U, T, H * LANE)
        middle_shard, arrived = scatter_sum(middle)
        back = []
        for h in range(H):
            back.append(
                attend_backward(
                    hs, h, 1, qa, qb, ka, va, grad_mixed, mixed, pos_x, sines_low, sines_t, cosines_t,
                    after=tuple(arrived[h]),
                )
            )
        frames_grad, late = last_block(
            unit, [b[0].reshape(R, -1) for b in back], source, grad_one,
            [b[1] for b in back], [b[2] for b in back], (back_x, small_one, grad_depth), taps,
            after=tuple(arrived[H]),
        )
        frames_grad = frames_grad.reshape(U, T, D)
        grad_pieces = send_frames(frames_grad, mine)
        late_shard, _ = scatter_sum(late, after=tuple(grad_pieces))
        return frames_grad, grad_pieces, middle_shard, late_shard

    shapes = jax.eval_shape(backward, stat, sums, grad_centred, grad_three)
    frames_grad, grad_pieces, middle_shard, late_shard = lax.cond(
        stat[2, 0] > 0.0,
        backward,
        lambda *_: jax.tree.map(lambda s: jnp.zeros(s.shape, s.dtype), shapes),
        stat, sums, grad_centred, grad_three,
    )
    frames_grad = assemble(frames_grad, grad_pieces, mine)
    block_out = assemble(block_out, out_pieces, mine)
    cuts = [s.shape[0] // 2 for s in (middle_shard, late_shard)]
    bit, value, other = gather_all(join_shards(middle_shard, late_shard, early[2:]))
    grad_inner_two, grad_outer_two, grad_point = widen(early)
    (
        grad_inner_one, grad_outer_one, grad_glu, grad_output, grad_query, grad_key, grad_value, grad_position, small, grad_depth,
    ) = unpack(
        bit.astype(jnp.int32).reshape(1), value, other, bias_x, D, F, taps, *cuts,
        after=(grad_point, frames_grad, block_out),
    )
    return (
        block_out,
        frames_grad,
        grad_query,
        grad_key,
        grad_value,
        grad_position,
        small[0],
        small[1],
        grad_output,
        small[8],
        small[9],
        grad_inner_one,
        grad_outer_one.T,
        small[10],
        small[11],
        grad_glu.T,
        grad_depth[:taps],
        sums[0],
        sums[1],
        grad_point,
        sums[2],
        sums[3],
        grad_inner_two,
        grad_outer_two.T,
        sums[4],
        sums[5],
    )


def solution(mesh):
    split = P("batch", "tm", None)
    return jax.shard_map(
        on_device,
        mesh=mesh,
        in_specs=(split, P("batch"), split) + (P(),) * 24,
        out_specs=(split, split) + (P(),) * 24,
        check_vma=False,
    )
```

```python
import functools
import math

import jax
import jax.numpy as jnp
from jax import lax
from jax.experimental import pallas as pl
from jax.experimental.pallas import tpu as pltpu
from jax.sharding import PartitionSpec as P

HEADS = 4
EPSILON = 1e-05
MASKED = -1e30
PAD = 16
LOG2E = 1.4426950408889634
LN2 = 0.6931471805599453
LANE = 128
WIDE = 256
FULL = 384
VMEM = 28 * 1024 * 1024
MOST = 56 * 1024 * 1024
bf16 = jnp.bfloat16
f32 = jnp.float32


def dot(a, b):
    return jnp.dot(a, b, preferred_element_type=f32)


def dot_nt(a, b):
    return lax.dot_general(a, b, (((1,), (1,)), ((), ())), preferred_element_type=f32)


def dot_tn(a, b):
    return lax.dot_general(a, b, (((0,), (0,)), ((), ())), preferred_element_type=f32)


def lanes(shape):
    return lax.broadcasted_iota(jnp.int32, shape, 1)


def sublanes(shape):
    return lax.broadcasted_iota(jnp.int32, shape, 0)


def kernel_call(kernel, name, operands, out, grid=(1,), after=(), scratch=(), flops=0, vmem=VMEM):
    count = len(operands)
    extra = len(after)

    def body(*refs):
        kernel(*refs[:count], *refs[count + extra :])

    return pl.pallas_call(
        body,
        grid=grid,
        in_specs=[spec for _, spec in operands] + [pl.BlockSpec(memory_space=pl.ANY)] * extra,
        out_specs=[spec for _, _, spec in out],
        out_shape=[jax.ShapeDtypeStruct(shape, kind) for shape, kind, _ in out],
        scratch_shapes=list(scratch),
        compiler_params=pltpu.CompilerParams(
            vmem_limit_bytes=vmem, dimension_semantics=("arbitrary",) * len(grid)
        ),
        cost_estimate=pl.CostEstimate(flops=flops, bytes_accessed=1000000, transcendentals=0)
        if flops
        else None,
        name=name,
    )(*[array for array, _ in operands], *after)


def whole_spec(shape):
    return pl.BlockSpec(tuple(shape), lambda *_: (0,) * len(shape))


SCALARS = pl.BlockSpec(memory_space=pltpu.SMEM)


def split_kernel(mine_ref, x_ref, *out_refs, parts, own, seqs):
    mine = mine_ref[0]
    D = x_ref.shape[0]
    for place in range(parts):
        shift = lax.rem(place - mine + parts, parts)
        for i, u in enumerate(seqs):
            rows = jnp.transpose(x_ref[:, place * own + u, :].astype(f32)).astype(bf16)
            spare = jnp.zeros((rows.shape[0], FULL - D), bf16)
            rows = jnp.concatenate([rows, spare], axis=1)
            for k in range(parts):

                @pl.when(shift == k)
                def _():
                    out_refs[k * len(seqs) + i][...] = rows


def split_frames(frames, mine, seqs, after=()):
    count, rows, D = frames.shape
    parts = lax.axis_size("tm")
    across = jnp.transpose(frames, (2, 0, 1))
    pieces = kernel_call(
        functools.partial(split_kernel, parts=parts, own=count // parts, seqs=seqs),
        "split_frames",
        [(mine, SCALARS), (across, whole_spec(across.shape))],
        [((rows, FULL), bf16, whole_spec((rows, FULL)))] * (parts * len(seqs)),
        after=after, flops=3_000_000_000,
    )
    return [pieces[k * len(seqs) : (k + 1) * len(seqs)] for k in range(parts)]


def at_place(mine, place, pieces):
    parts = len(pieces)
    shift = lax.rem(mine - place + parts, parts)
    chosen = pieces[0]
    for k in range(1, parts):
        chosen = jnp.where(shift == k, pieces[k], chosen)
    return chosen


def pick(rows, cols, start, at, size):
    row, col = sublanes((rows, cols)), lanes((rows, cols))
    return jnp.where((row - start == col - at) & (row >= start) & (row < start + size), 1.0, 0.0)


def prepare_kernel(
    vec_ref, wq_ref, wk_ref, wv_ref, wp_ref, wout_ref, glu_ref,
    q_ref, kv_ref, pos_ref, out_ref, bias_ref, back_ref, lin_ref, gate_ref,
    sin_ref, cos_ref, low_ref, sin_t_ref, cos_t_ref, *, length,
):
    D = wq_ref.shape[0]
    hs = D // HEADS
    half = D // 2
    at = half - LANE
    wq, wk, wv = wq_ref[...], wk_ref[...], wv_ref[...]
    vec = vec_ref[...]
    feature = sublanes((2 * WIDE, D))
    column = lanes((2 * WIDE, D))
    spread_rows = jnp.where(
        ((feature == column) & (column < half))
        | ((feature - WIDE == column - half) & (column >= half)),
        1.0, 0.0,
    ).astype(bf16)
    pos = dot(spread_rows, wp_ref[...]).astype(bf16)
    for h in range(HEADS):
        mid = pick(D, LANE, h * hs, at, hs)
        low = mid.astype(bf16)
        first = pick(D, LANE, h * hs, 0, hs).astype(bf16)
        spare = jnp.zeros((FULL - D, LANE), f32)
        q_ref[h] = jnp.concatenate([dot(wq, low), spare], axis=0).astype(bf16)
        kv_ref[h, :, :LANE] = jnp.concatenate([dot(wk, low), spare], axis=0).astype(bf16)
        kv_ref[h, :, LANE:] = jnp.concatenate([dot(wv, first), spare], axis=0).astype(bf16)
        mid_t = pick(LANE, D, at, h * hs, hs).astype(bf16)
        pos_ref[h] = dot_nt(mid_t, pos).astype(bf16)
        bias_ref[h] = lax.dot_general(
            vec, mid, (((1,), (0,)), ((), ())), precision=lax.Precision.HIGHEST,
            preferred_element_type=f32,
        )
        out_ref[h * LANE : (h + 1) * LANE, :] = dot(
            pick(LANE, D, 0, h * hs, hs).astype(bf16), wout_ref[...]
        ).astype(bf16)
        back = None
        for i, w in enumerate((wv, wq, wk)):
            part = dot_nt(pick(WIDE, D, i * hs, h * hs, hs).astype(bf16), w)
            back = part if back is None else back + part
        back_ref[h * WIDE : (h + 1) * WIDE, :] = back.astype(bf16)
    lin_ref[...] = glu_ref[:D, :]
    gate_ref[...] = glu_ref[D:, :]

    rate = -2.0 * math.log(10000.0) / D

    def waves(position, index):
        angle = position.astype(f32) * jnp.exp(index.astype(f32) * rate)
        inside = index < half
        return jnp.where(inside, jnp.sin(angle), 0.0), jnp.where(inside, jnp.cos(angle), 0.0)

    shape = (32, WIDE)
    base_s, base_c = waves(sublanes(shape), lanes(shape))
    step_s, step_c = waves(sublanes(shape) * 32, lanes(shape))
    for i in range(length // 32):
        s, c = step_s[i : i + 1], step_c[i : i + 1]
        rows = pl.ds(i * 32, 32)
        sine = s * base_c + c * base_s
        sin_ref[rows, :] = sine
        cos_ref[rows, :] = c * base_c - s * base_s
        low_ref[rows, :] = sine.astype(bf16)
    shape = (WIDE, LANE)
    base_s, base_c = waves(lanes(shape), sublanes(shape))
    step_s, step_c = waves(lanes(shape) * LANE, sublanes(shape))
    for i in range(-(-length // LANE)):
        s, c = step_s[:, i : i + 1], step_c[:, i : i + 1]
        width = min(LANE, length - i * LANE)
        sin_t_ref[:, i * LANE : i * LANE + width] = (s * base_c + c * base_s)[:, :width]
        cos_t_ref[:, i * LANE : i * LANE + width] = (c * base_c - s * base_s)[:, :width]


def prepare(length, vec, wq, wk, wv, wp, wout, glu):
    D = wq.shape[0]
    arrays = (vec, wq, wk, wv, wp, wout, glu)
    shapes = (
        ((HEADS, FULL, LANE), bf16), ((HEADS, FULL, WIDE), bf16), ((HEADS, LANE, 2 * WIDE), bf16),
        ((HEADS * LANE, D), bf16), ((HEADS,) + vec.shape[:1] + (LANE,), f32),
        ((HEADS * WIDE, D), bf16), ((D, D), bf16), ((D, D), bf16),
        ((length, WIDE), f32), ((length, WIDE), f32), ((length, WIDE), bf16),
        ((WIDE, length), f32), ((WIDE, length), f32),
    )
    return kernel_call(
        functools.partial(prepare_kernel, length=length), "prepare",
        [(a, whole_spec(a.shape)) for a in arrays],
        [(s, k, whole_spec(s)) for s, k in shapes],
        flops=5_000_000_000, vmem=MOST,
    )


def attend_forward_kernel(
    len_ref, mine_ref, *refs, parts, seq, hs, tile,
):
    pieces = refs[:parts]
    q_ref, kv_ref, pos_ref, bias_ref, sin_ref, cos_ref, low_ref = refs[parts : parts + 7]
    mixed_ref, qa_ref, qb_ref, ka_ref, v_ref, f_ref = refs[parts + 7 :]
    T = f_ref.shape[0]
    count = pieces[0].shape[0]

    @pl.when(pl.program_id(0) == 0)
    def _():
        for place in range(parts):
            f_ref[place * count : (place + 1) * count, :] = at_place(
                mine_ref[0], place, [p[...] for p in pieces]
            )

    one = 3 * hs - LANE
    scale = LOG2E / math.sqrt(hs)
    valid = len_ref[seq]
    lane = lanes((tile, LANE))

    def key_rows(h, r0):
        rows = pl.ds(r0, tile)
        kv = dot(f_ref[rows, :], kv_ref[h])
        k = kv[:, :LANE] + cos_ref[rows, LANE:]
        row = sublanes((tile, LANE)) + r0
        k = jnp.where(lane == one, jnp.where(row < valid, 0.0, MASKED), k)
        k = jnp.where((lane > one) & (lane < one + 4), 1.0, k)
        ka_ref[h, rows, :LANE] = cos_ref[rows, :LANE].astype(bf16)
        ka_ref[h, rows, LANE:] = k.astype(bf16)
        v = jnp.where((lane == hs) | (lane == hs + 1), 1.0, kv[:, LANE:])
        v_ref[h, rows, :] = v.astype(bf16)

    def score_rows(h, r0):
        rows = pl.ds(r0, tile)
        q = dot(f_ref[rows, :], q_ref[h])
        e = dot((q + bias_ref[h, 1:2, :]).astype(bf16), pos_ref[h])
        es, ec = e[:, :WIDE], e[:, WIDE:]
        s, c = sin_ref[rows, :], cos_ref[rows, :]
        qb = ((ec * s - es * c) * scale).astype(bf16)
        qb_ref[h, rows, :] = qb
        a = (es * s + ec * c) * scale
        first = a[:, :LANE].astype(bf16)
        second = jnp.where(lane == one, 1.0, a[:, LANE:] + (q + bias_ref[h, 0:1, :]) * scale)
        second = second.astype(bf16)
        qa_ref[h, rows, :LANE] = first
        qa = jnp.concatenate([first, second], axis=1)
        return second, dot_nt(qa, ka_ref[h]) + dot_nt(qb, low_ref[...])

    def mix_rows(h, r0, second, scores):
        rows = pl.ds(r0, tile)
        peak = jnp.max(scores, axis=1, keepdims=True)
        p = jnp.exp2(scores - peak).astype(bf16)
        o = dot(p, v_ref[h])
        total = o[:, hs : hs + 1]
        mixed_ref[rows, h * LANE : (h + 1) * LANE] = (o / total).astype(bf16)
        log_total = -(peak + jnp.log2(total))
        hi = log_total.astype(bf16).astype(f32)
        mid = (log_total - hi).astype(bf16).astype(f32)
        rest = jnp.where(lane == one + 1, hi, jnp.where(lane == one + 2, mid, log_total - hi - mid))
        second = jnp.where((lane > one) & (lane < one + 4), rest, second.astype(f32))
        qa_ref[h, rows, LANE:] = second.astype(bf16)

    tasks = [(h, r0) for h in range(q_ref.shape[0]) for r0 in range(0, T, tile)]
    for task in tasks:
        key_rows(*task)
    waiting = None
    for task in tasks:
        current = (*task, *score_rows(*task))
        if waiting is not None:
            mix_rows(*waiting)
        waiting = current
    mix_rows(*waiting)


def attend_forward(seq, head_size, lens, mine, pieces, q, kv, pos, bias, sines, cosines, low, tile=496):
    T = sines.shape[0]
    H = q.shape[0]
    group = 2

    def head(shape):
        return pl.BlockSpec((group,) + shape[1:], lambda h: (h, 0, 0))

    def three(width):
        return ((H, T, width), bf16, pl.BlockSpec((group, T, width), lambda h: (h, 0, 0)))

    return kernel_call(
        functools.partial(
            attend_forward_kernel, parts=len(pieces), seq=seq, hs=head_size, tile=tile
        ),
        "attend_forward",
        [(lens, SCALARS), (mine, SCALARS)]
        + [(p, whole_spec(p.shape)) for p in pieces]
        + [(a, head(a.shape)) for a in (q, kv, pos, bias)]
        + [(a, whole_spec(a.shape)) for a in (sines, cosines, low)],
        [((T, H * LANE), bf16, pl.BlockSpec((T, group * LANE), lambda h: (0, h)))]
        + [three(w) for w in (WIDE, WIDE, WIDE, LANE)]
        + [((T, FULL), bf16, whole_spec((T, FULL)))],
        grid=(H // group,),
        flops=15_000_000_000, vmem=40 * 1024 * 1024,
    )


def attend_backward_kernel(
    qa_ref, qb_ref, ka_ref, v_ref, do_ref, mixed_ref, pos_ref, low_ref, sin_ref, cos_ref,
    d_ref, dpos_ref, bias_ref, *, hs, tile,
):
    T = qa_ref.shape[1]
    at = 2 * hs - LANE
    inv = 1.0 / math.sqrt(hs)
    do = do_ref[...]
    wide = do.astype(f32)
    delta = -jnp.sum(wide * mixed_ref[...].astype(f32), axis=1, keepdims=True)
    hi = delta.astype(bf16).astype(f32)
    lane = lanes((T, LANE))
    dox = jnp.where(lane == hs, hi, jnp.where(lane == hs + 1, delta - hi, wide)).astype(bf16)
    qa = qa_ref[0]
    qb = qb_ref[0]
    da = db = None
    parts = []
    for r0 in range(0, T, tile):
        rows = pl.ds(r0, tile)
        ka = ka_ref[0, rows, :]
        low = low_ref[rows, :]
        p = jnp.exp2(dot_nt(ka, qa) + dot_nt(low, qb))
        ds = (p * dot_nt(v_ref[0, rows, :], dox)).astype(bf16)
        dv = dot(p.astype(bf16), do)
        dk = dot(ds, qa[:, LANE:])
        a, b = dot_tn(ka, ds), dot_tn(low, ds)
        da = a if da is None else da + a
        db = b if db is None else db + b
        parts.append((dv, dk))
    s, c = sin_ref[...], cos_ref[...]
    des = (da * s - db * c) * inv
    dec = (da * c + db * s) * inv
    de = jnp.concatenate([des.astype(bf16), dec.astype(bf16)], axis=0)
    dqp = dot(pos_ref[0], de)
    dpos = dot(de, qa[:, LANE:])
    sub = sublanes((LANE, T))
    dqc = jnp.where((sub >= at) & (sub < at + hs), da[LANE:] * inv, 0.0)
    ones = jnp.ones((16, T), bf16)
    bias = jnp.where(
        sublanes((16, LANE)) == 0, dot_nt(ones, dqc.astype(bf16)), dot_nt(ones, dqp.astype(bf16))
    )

    dpos_ref[0] = dpos
    bias_ref[0] = bias
    dq = jnp.transpose(dqc + dqp)
    dq = pltpu.roll(jnp.concatenate([jnp.zeros((T, LANE), f32), dq], axis=1), WIDE - hs, 1)
    lane = lanes((tile, LANE))
    for i, (dv, dk) in enumerate(parts):
        rows = pl.ds(i * tile, tile)
        dq_rows = dq[i * tile : (i + 1) * tile]
        d_ref[rows, :LANE] = jnp.where(lane < hs, dv, dq_rows[:, :LANE]).astype(bf16)
        inside = (lane >= at) & (lane < at + hs)
        d_ref[rows, LANE:] = jnp.where(inside, dk * LN2, dq_rows[:, LANE:]).astype(bf16)


def attend_backward(
    seq, head_size, first, count, qa, qb, ka, v, do, mixed, pos, low, sin_t, cos_t, after, tile=496,
):
    H, T, W = qa.shape

    def three(array):
        return array, pl.BlockSpec((1,) + array.shape[1:], lambda h: (first + h, 0, 0))

    def lane_block(array, u):
        return array, pl.BlockSpec((T, LANE), lambda h: (u, first + h))

    return kernel_call(
        functools.partial(attend_backward_kernel, hs=head_size, tile=tile), "attend_backward",
        [three(qa), three(qb), three(ka), three(v), lane_block(do, seq), lane_block(mixed, 0)]
        + [three(pos)]
        + [(a, whole_spec(a.shape)) for a in (low, sin_t, cos_t)],
        [
            ((T, count * W), bf16, pl.BlockSpec((T, W), lambda h: (0, h))),
            ((count, 2 * W, LANE), f32, pl.BlockSpec((1, 2 * W, LANE), lambda h: (h, 0, 0))),
            ((count, 16, LANE), f32, pl.BlockSpec((1, 16, LANE), lambda h: (h, 0, 0))),
        ],
        grid=(count,),
        after=after,
        flops=count * 5_500_000_000,
    )


def fill_padded(buf, value):
    T = value.shape[0]
    zero = jnp.zeros((PAD, buf.shape[1]), f32)
    buf[0:PAD, :] = zero
    buf[T + PAD : T + 2 * PAD, :] = zero
    buf[PAD : T + PAD, :] = value


def fill_weights(wide, w_ref, taps):
    for o in range(taps):
        wide[o] = jnp.broadcast_to(w_ref[o : o + 1, :], (8, LANE))


def tall(values):
    return values.reshape(values.shape[0] // 8, 8, LANE)


def chunks(T, step, body, carry):
    full = T // step
    carry = lax.fori_loop(
        0, full, lambda i, c: body(pl.multiple_of(i * step, 8), step, c), carry
    )
    return body(full * step, T - full * step, carry) if T % step else carry


def conv_forward_kernel(len_ref, x_ref, w_ref, out_ref, stat_ref, padded, wide, *, taps, step):
    u = pl.program_id(1)
    T = x_ref.shape[1]
    half = (taps - 1) // 2
    fill_padded(padded, x_ref[0].astype(f32))
    fill_weights(wide, w_ref, taps)
    valid = len_ref[u]

    def body(base, rows, sums):
        total = None
        for o in range(taps):
            term = wide[o] * tall(padded[pl.ds(base + PAD - half + o, rows), :])
            total = term if total is None else total + term
        out_ref[0, pl.ds(base, rows), :] = total.reshape(rows, LANE)
        row = 8 * lax.broadcasted_iota(jnp.int32, (rows // 8, 8, LANE), 0)
        row = row + lax.broadcasted_iota(jnp.int32, (rows // 8, 8, LANE), 1) + base
        masked = jnp.where(row < valid, total, 0.0)
        return sums[0] + jnp.sum(masked, axis=0), sums[1] + jnp.sum(masked * total, axis=0)

    zero = jnp.zeros((8, LANE), f32)
    first, second = chunks(T, step, body, (zero, zero))
    count = jnp.full((1, LANE), valid, jnp.int32).astype(f32)
    stat = jnp.concatenate(
        [
            jnp.sum(first, axis=0, keepdims=True),
            jnp.sum(second, axis=0, keepdims=True),
            count,
            jnp.zeros((5, LANE), f32),
        ],
        axis=0,
    )

    @pl.when(u == 0)
    def _():
        stat_ref[...] = stat

    @pl.when(u > 0)
    def _():
        stat_ref[...] += stat


def conv_forward(lens, x, w, step=256):
    U, T, C = x.shape
    block = pl.BlockSpec((1, T, LANE), lambda c, u: (u, 0, c))
    return kernel_call(
        functools.partial(conv_forward_kernel, taps=w.shape[0], step=step), "conv_forward",
        [(lens, SCALARS), (x, block), (w, pl.BlockSpec((w.shape[0], LANE), lambda c, u: (0, c)))],
        [((U, T, C), f32, block), ((8, C), f32, pl.BlockSpec((8, LANE), lambda c, u: (0, c)))],
        grid=(pl.cdiv(C, LANE), U),
        scratch=[pltpu.VMEM((T + 2 * PAD, LANE), f32), pltpu.VMEM((w.shape[0], 8, LANE), f32)],
        flops=10_000_000_000,
    )


def batch_moments(stat):
    count = stat[2:3, :]
    mean = stat[0:1, :] / count
    return count, mean, lax.rsqrt(stat[1:2, :] / count - mean * mean + EPSILON)


def conv_backward_kernel(
    len_ref, x_ref, dz_ref, conv_ref, w_ref, stat_ref, sums_ref, vec_ref, gs_ref, gw_ref,
    padded_x, padded_g, wide, *, taps, step, gain_row,
):
    u = pl.program_id(1)
    T = x_ref.shape[1]
    half = (taps - 1) // 2
    valid = len_ref[u]
    count, mean, rstd = batch_moments(stat_ref[...])
    gain = vec_ref[gain_row : gain_row + 1, :]
    grad_var = -0.5 * rstd * rstd * (sums_ref[0:1, :] * gain)
    grad_mean = -rstd * (sums_ref[1:2, :] * gain) - 2.0 * mean * grad_var
    shift = grad_mean / count
    slope = 2.0 * grad_var / count
    row = sublanes((T, LANE))
    g = dz_ref[0] * rstd + jnp.where(row < valid, shift + slope * conv_ref[0], 0.0)
    fill_padded(padded_g, g)
    fill_padded(padded_x, x_ref[0].astype(f32))

    fill_weights(wide, w_ref, taps)

    def spread(base, rows, carry):
        total = None
        for o in range(taps):
            term = wide[o] * tall(padded_g[pl.ds(base + PAD + half - o, rows), :])
            total = term if total is None else total + term
        gs_ref[0, pl.ds(base, rows), :] = total.reshape(rows, LANE)
        return carry

    chunks(T, step, spread, 0)

    zero = jnp.zeros((8, LANE), f32)

    def relate(base, rows, carry):
        centre = tall(padded_g[pl.ds(base + PAD, rows), :])
        new = []
        for o, kept in enumerate(carry):
            moved = tall(padded_x[pl.ds(base + PAD - half + o, rows), :])
            new.append(kept + jnp.sum(centre * moved, axis=0))
        return tuple(new)

    sums = chunks(T, step // 2, relate, (zero,) * taps)
    rows = [jnp.sum(s, axis=0, keepdims=True) for s in sums]
    gw = jnp.concatenate(rows + [jnp.zeros((-taps % 8, LANE), f32)], axis=0)

    @pl.when(u == 0)
    def _():
        gw_ref[...] = gw

    @pl.when(u > 0)
    def _():
        gw_ref[...] += gw


def conv_backward(lens, x, dz, conv, w, stat, sums, vec, gain_row, step=256):
    U, T, C = x.shape
    taps = w.shape[0]
    block = pl.BlockSpec((1, T, LANE), lambda c, u: (u, 0, c))

    def channel(array):
        return array, pl.BlockSpec((array.shape[0], LANE), lambda c, u: (0, c))

    return kernel_call(
        functools.partial(conv_backward_kernel, taps=taps, step=step, gain_row=gain_row),
        "conv_backward",
        [(lens, SCALARS), (x, block), (dz, block), (conv, block)]
        + [channel(a) for a in (w, stat, sums, vec)],
        [((U, T, C), f32, block), ((taps + -taps % 8, C), f32, pl.BlockSpec((taps + -taps % 8, LANE), lambda c, u: (0, c)))],
        grid=(pl.cdiv(C, LANE), U),
        scratch=[pltpu.VMEM((T + 2 * PAD, LANE), f32)] * 2 + [pltpu.VMEM((taps, 8, LANE), f32)],
        flops=20_000_000_000,
    )


CONTENT, POSITION, GAIN1, SHIFT1, GAIN2, SHIFT2, BGAIN, BSHIFT, GAIN3, SHIFT3, GAIN4, SHIFT4 = range(12)


def vector(ref, index):
    return ref[index : index + 1, :]


def sigmoid(x):
    return 0.5 * jnp.tanh(0.5 * x) + 0.5


def unit_norm(values):
    centred = values - jnp.mean(values, axis=-1, keepdims=True)
    inv_std = lax.rsqrt(jnp.mean(centred * centred, axis=-1, keepdims=True) + EPSILON)
    return centred * inv_std, inv_std


def unit_norm_back(unit, inv_std, gain, upstream):
    scaled = upstream * gain
    return inv_std * (
        scaled
        - jnp.mean(scaled, axis=-1, keepdims=True)
        - unit * jnp.mean(scaled * unit, axis=-1, keepdims=True)
    )


def col_sum(values):
    return jnp.sum(values, axis=0, keepdims=True)


def clear(refs):
    @pl.when(pl.program_id(0) == 0)
    def _():
        for ref in refs:
            ref[...] = jnp.zeros(ref.shape, ref.dtype)


def add_into(ref, value):
    rows, cols = value.shape
    ref[:rows, :cols] += value


def up(value, unit):
    return -(-value // unit) * unit


def put_blocks(packed_ref, at, value):
    rows, cols = value.shape
    for c in range(0, cols, LANE):
        packed_ref[at : at + rows, :] = value[:, c : c + LANE].astype(bf16)
        at += rows
    return at


def row_valid(len_ref, step, tile, length):
    per = length // tile
    row = sublanes((tile, 1)) + lax.rem(step, per) * tile
    return row < len_ref[lax.div(step, per)]


def first_kernel(
    len_ref, f_ref, mixed_ref, vec_ref, wout_ref, wi_ref, wo_ref, wl_ref, wg_ref,
    x1_ref, r1_ref, u_ref, x2_ref, r2_ref, lin_ref, sig_ref, spread_ref, *, tile, length,
):
    D = x1_ref.shape[1]
    resid = f_ref[...][:, :D].astype(f32) + dot(mixed_ref[...], wout_ref[...])
    unit, inv_std = unit_norm(resid)
    x1_ref[...] = unit
    r1_ref[...] = inv_std
    hidden = unit * vector(vec_ref, GAIN1) + vector(vec_ref, SHIFT1)
    inner = dot(hidden.astype(bf16), wi_ref[...])
    u_ref[...] = inner.astype(bf16)
    active = (inner * sigmoid(inner)).astype(bf16)
    resid = hidden + dot_nt(active, wo_ref[...])
    unit, inv_std = unit_norm(resid)
    x2_ref[...] = unit
    r2_ref[...] = inv_std
    entry = (unit * vector(vec_ref, GAIN2) + vector(vec_ref, SHIFT2)).astype(bf16)
    lin = dot_nt(entry, wl_ref[...])
    sig = sigmoid(dot_nt(entry, wg_ref[...]))
    lin_ref[...] = lin.astype(bf16)
    sig_ref[...] = sig.astype(bf16)
    valid = row_valid(len_ref, pl.program_id(0), tile, length)
    spread_ref[...] = jnp.where(valid, lin * sig, 0.0).astype(bf16)


def second_kernel(
    mine_ref, x2_ref, conv_ref, cot_ref, stat_ref, vec_ref, wp_ref, wi_ref, wo_ref,
    out_ref, dz_ref, g3_ref, small_ref, dwp_ref, dwi_ref, dwo_ref, sum_p, sum_i, sum_o,
):
    clear((small_ref, sum_p, sum_i, sum_o))
    _, mean, rstd = batch_moments(stat_ref[...])
    centred = (conv_ref[...] - mean) * rstd
    batch_gain = vector(vec_ref, BGAIN)
    normed = centred * batch_gain + vector(vec_ref, BSHIFT)
    sig_n = sigmoid(normed)
    swished = (normed * sig_n).astype(bf16)
    slope_n = (sig_n * (1.0 + normed * (1.0 - sig_n))).astype(bf16)
    hidden_two = x2_ref[...] * vector(vec_ref, GAIN2) + vector(vec_ref, SHIFT2)
    unit3, inv3 = unit_norm(hidden_two + dot(swished, wp_ref[...]))
    gain3 = vector(vec_ref, GAIN3)
    hidden = unit3 * gain3 + vector(vec_ref, SHIFT3)
    entry = hidden.astype(bf16)
    inner = dot(entry, wi_ref[...])
    sig = sigmoid(inner)
    active = (inner * sig).astype(bf16)
    slope = (sig * (1.0 + inner * (1.0 - sig))).astype(bf16)
    unit4, inv4 = unit_norm(hidden + dot_nt(active, wo_ref[...]))
    gain4 = vector(vec_ref, GAIN4)
    D = unit4.shape[1]
    out_ref[:, :D] = (unit4 * gain4 + vector(vec_ref, SHIFT4)).astype(bf16)
    out_ref[:, D:] = jnp.zeros((unit4.shape[0], FULL - D), bf16)
    upstream = cot_ref.value(mine_ref[0])[:, :D].astype(f32)
    grad4 = unit_norm_back(unit4, inv4, gain4, upstream)
    low4 = grad4.astype(bf16)
    add_into(sum_o, dot_tn(low4, active))
    dinner = (dot(low4, wo_ref[...]) * slope.astype(f32)).astype(bf16)
    add_into(sum_i, dot_tn(entry, dinner))
    up3 = grad4 + dot_nt(dinner, wi_ref[...])
    grad3 = unit_norm_back(unit3, inv3, gain3, up3)
    g3_ref[...] = grad3
    low3 = grad3.astype(bf16)
    add_into(sum_p, dot_tn(swished, low3))
    dnormed = dot_nt(low3, wp_ref[...]) * slope_n.astype(f32)
    dz_ref[...] = dnormed * batch_gain
    small = jnp.concatenate(
        [
            col_sum(dnormed * centred), col_sum(dnormed),
            col_sum(up3 * unit3), col_sum(up3),
            col_sum(upstream * unit4), col_sum(upstream),
            jnp.zeros((2, centred.shape[1]), f32),
        ],
        axis=0,
    )
    add_into(small_ref, small)

    @pl.when(pl.program_id(0) == pl.num_programs(0) - 1)
    def _():
        dwp_ref[...] = sum_p[...].astype(bf16)
        dwi_ref[...] = sum_i[...].astype(bf16)
        dwo_ref[...] = sum_o[...].astype(bf16)


def third_kernel(
    len_ref, gs_ref, lin_ref, sig_ref, x2_ref, r2_ref, g3_ref, u_ref, x1_ref, r1_ref, mixed_ref,
    vec_ref, wl_ref, wg_ref, wi_ref, wo_ref, wout_ref,
    g1_ref, gm_ref, small_ref, packed_ref, sum_i, sum_o, sum_l, sum_g, sum_out, *, tile, length,
):
    step = pl.program_id(0)
    clear((small_ref, sum_i, sum_o, sum_l, sum_g, sum_out))
    valid = row_valid(len_ref, step, tile, length)
    sig_g = sig_ref[...].astype(f32)
    gated = jnp.where(valid, gs_ref[...], 0.0) * sig_g
    low_l = gated.astype(bf16)
    low_g = (gated * lin_ref[...].astype(f32) * (1.0 - sig_g)).astype(bf16)
    unit2 = x2_ref[...]
    gain2 = vector(vec_ref, GAIN2)
    entry2 = (unit2 * gain2 + vector(vec_ref, SHIFT2)).astype(bf16)
    add_into(sum_l, dot_tn(low_l, entry2))
    add_into(sum_g, dot_tn(low_g, entry2))
    up2 = g3_ref[...] + dot(low_l, wl_ref[...]) + dot(low_g, wg_ref[...])
    grad2 = unit_norm_back(unit2, r2_ref[...], gain2, up2)
    low2 = grad2.astype(bf16)
    inner = u_ref[...].astype(f32)
    sig = sigmoid(inner)
    active = (inner * sig).astype(bf16)
    slope = (sig * (1.0 + inner * (1.0 - sig))).astype(bf16)
    add_into(sum_o, dot_tn(low2, active))
    dinner = (dot(low2, wo_ref[...]) * slope.astype(f32)).astype(bf16)
    unit1 = x1_ref[...]
    gain1 = vector(vec_ref, GAIN1)
    entry1 = (unit1 * gain1 + vector(vec_ref, SHIFT1)).astype(bf16)
    add_into(sum_i, dot_tn(entry1, dinner))
    up1 = grad2 + dot_nt(dinner, wi_ref[...])
    grad1 = unit_norm_back(unit1, r1_ref[...], gain1, up1)
    g1_ref[...] = grad1
    low1 = grad1.astype(bf16)
    add_into(sum_out, dot_tn(mixed_ref[...], low1))
    gm_ref[...] = dot_nt(low1, wout_ref[...]).astype(bf16)
    small = jnp.concatenate(
        [
            col_sum(up1 * unit1), col_sum(up1),
            col_sum(up2 * unit2), col_sum(up2),
            jnp.zeros((4, unit1.shape[1]), f32),
        ],
        axis=0,
    )
    add_into(small_ref, small)

    @pl.when(step == pl.num_programs(0) - 1)
    def _():
        D = unit1.shape[1]
        hs = D // HEADS
        at = 0
        for ref in (sum_i, sum_o, sum_l, sum_g):
            at = put_blocks(packed_ref, at, ref[...])
        rows = sum_l.shape[0]
        compact = jnp.zeros(sum_l.shape, f32)
        for h in range(HEADS):
            chosen = pick(rows, LANE, h * hs, 0, hs).astype(bf16)
            part = dot(chosen, sum_out[h * LANE : (h + 1) * LANE, :].astype(bf16))
            compact += jnp.concatenate(
                [part, jnp.zeros((rows, sum_l.shape[1] - D), f32)], axis=1
            )
        at = put_blocks(packed_ref, at, compact)
        if at < packed_ref.shape[0]:
            packed_ref[at:, :] = jnp.zeros((packed_ref.shape[0] - at, LANE), bf16)


def frames_kernel(*refs):
    heads = refs[:-3]
    g1_ref, back_ref, out_ref = refs[-3:]
    grads = jnp.concatenate([ref[...] for ref in heads], axis=1)
    D = g1_ref.shape[1]
    out_ref[:, :D] = (g1_ref[...] + dot(grads, back_ref[...])).astype(bf16)
    out_ref[:, D:] = jnp.zeros((out_ref.shape[0], FULL - D), bf16)


def frames_block(seq, heads, g1, back, after=(), tile=496):
    rows = heads[0].shape[0]
    per = rows // tile
    return kernel_call(
        frames_kernel, "frames_block",
        [(a, pl.BlockSpec((tile, a.shape[1]), lambda i: (i, 0))) for a in heads]
        + [(g1, pl.BlockSpec((tile, g1.shape[1]), lambda i: (seq * per + i, 0)))]
        + [(back, whole_spec(back.shape))],
        [((rows, FULL), bf16, pl.BlockSpec((tile, FULL), lambda i: (i, 0)))],
        grid=(per,), after=after, flops=3_000_000_000, vmem=MOST,
    )[0]


def pack_kernel(*refs, groups, seqs):
    d_refs = refs[:groups]
    f_ref = refs[groups]
    rest = refs[groups + 1 :]
    pos_refs, bias_refs = rest[: groups * seqs], rest[groups * seqs : 2 * groups * seqs]
    small_ref, depth_ref, packed_ref, sum_w = rest[2 * groups * seqs :]
    clear((sum_w,))
    grads = jnp.concatenate([ref[...] for ref in d_refs], axis=1)
    sum_w[...] += dot_tn(f_ref[...], grads)

    @pl.when(pl.program_id(0) == pl.num_programs(0) - 1)
    def _():
        D = small_ref.shape[1]
        wide = up(D, LANE)
        spare = jnp.zeros((16, wide - D), f32)
        at = put_blocks(packed_ref, 0, sum_w[: up(D, 16), :])
        kept = up(D // 2, 16)

        def over_seqs(items, group, take):
            total = None
            for s in range(seqs):
                value = take(items[s * groups + group])
                total = value if total is None else total + value
            return total

        for group in range(groups):
            for h in range(pos_refs[group].shape[0]):
                for half in range(2):
                    rows = slice(half * WIDE, half * WIDE + kept)
                    value = over_seqs(pos_refs, group, lambda ref: ref[h, rows, :])
                    at = put_blocks(packed_ref, at, value)
        for group in range(groups):
            for h in range(bias_refs[group].shape[0]):
                at = put_blocks(packed_ref, at, over_seqs(bias_refs, group, lambda ref: ref[h]))
        small = jnp.concatenate([small_ref[...], jnp.zeros((8, D), f32)], axis=0)
        at = put_blocks(packed_ref, at, jnp.concatenate([small, spare], axis=1))
        depth = depth_ref[...]
        spare = jnp.zeros((depth.shape[0], wide - D), f32)
        at = put_blocks(packed_ref, at, jnp.concatenate([depth, spare], axis=1))
        if at < packed_ref.shape[0]:
            packed_ref[at:, :] = jnp.zeros((packed_ref.shape[0] - at, LANE), bf16)


def middle_rows(D, F, unit):
    blocks = 2 * (up(F, LANE) // LANE) + 3 * (up(D, LANE) // LANE)
    return up(blocks * up(D, 16), unit)


def late_rows(D, taps, unit):
    blocks = up(D, LANE) // LANE
    rows = HEADS * WIDE // LANE * up(D, 16) + HEADS * (2 * up(D // 2, 16) + 16)
    return up(rows + blocks * (16 + up(taps, 16)), unit)


def unpack_kernel(
    bit_ref, value_ref, other_ref, bias_ref,
    wi1_ref, wo1_ref, glu_ref, wout_ref, q_ref, k_ref, v_ref, pos_ref, vec_ref, depth_ref, buf, *, middle, late,
):
    n = value_ref.shape[0]
    bit = bit_ref[0]
    buf[pl.ds(pl.multiple_of(bit * n, 16), n), :] = value_ref[...]
    buf[pl.ds(pl.multiple_of((1 - bit) * n, 16), n), :] = other_ref[...]
    D, F = wi1_ref.shape
    hs = D // HEADS
    half = D // 2
    at = half - LANE
    one = 3 * hs - LANE
    place = {"middle": 0, "late": 0}

    def fetch(kind, rows):
        cut = middle if kind == "middle" else late
        start = place[kind]
        place[kind] += rows
        parts = []
        while rows:
            shard, offset = divmod(start, cut)
            count = min(rows, cut - offset)
            base = shard * (middle + late) + offset + (0 if kind == "middle" else middle)
            parts.append(buf[base : base + count, :])
            start += count
            rows -= count
        return jnp.concatenate(parts, axis=0) if len(parts) > 1 else parts[0]

    def spread_blocks(ref, first, kind, rows, cols):
        for c in range(0, cols, LANE):
            width = min(LANE, cols - c)
            block = fetch(kind, up(rows, 16))[:rows, :width].astype(f32)
            ref[first : first + rows, c : c + width] = block

    spread_blocks(wi1_ref, 0, "middle", D, F)
    spread_blocks(wo1_ref, 0, "middle", D, F)
    spread_blocks(glu_ref, 0, "middle", D, D)
    spread_blocks(glu_ref, D, "middle", D, D)
    spread_blocks(wout_ref, 0, "middle", D, D)
    sums = [None, None, None]
    for h in range(HEADS):
        block = jnp.concatenate([fetch("late", up(D, 16)), fetch("late", up(D, 16))], axis=1)
        for i in range(3):
            part = dot(block, pick(WIDE, D, i * hs, h * hs, hs).astype(bf16))
            sums[i] = part if sums[i] is None else sums[i] + part
    v_ref[...] = sums[0][:D]
    q_ref[...] = sums[1][:D]
    k_ref[...] = sums[2][:D]
    halves = [None, None]
    scale = math.sqrt(hs) / LOG2E
    for h in range(HEADS):
        change = bias_ref[h, 1:2, :] - bias_ref[h, 0:1, :]
        chosen = pick(LANE, D, at, h * hs, hs)
        for i in range(2):
            raw = fetch("late", up(half, 16)).astype(f32)
            full = raw * scale + raw[:, one : one + 1] * change
            part = lax.dot_general(
                full, chosen, (((1,), (0,)), ((), ())), precision=lax.Precision.HIGHEST,
                preferred_element_type=f32,
            )
            halves[i] = part if halves[i] is None else halves[i] + part
    pos_ref[:half, :] = halves[0][:half]
    pos_ref[half:, :] = halves[1][:half]
    total = None
    for h in range(HEADS):
        part = dot(fetch("late", 16), pick(LANE, D, at, h * hs, hs).astype(bf16))
        total = part if total is None else total + part
    vec_ref[0:8, :] = total[:8]
    spread_blocks(vec_ref.at[8:16], 0, "late", 8, D)
    spread_blocks(depth_ref, 0, "late", depth_ref.shape[0], D)


def unpack(bit, value, other, bias, D, F, taps, middle, late, after):
    arrays = (value, other, bias)
    shapes = (
        (D, F), (D, F), (2 * D, D), (D, D), (D, D), (D, D), (D, D), (D, D),
        (16, D), (up(taps, 8), D),
    )
    return kernel_call(
        functools.partial(unpack_kernel, middle=middle, late=late), "unpack",
        [(bit, SCALARS)] + [(a, whole_spec(a.shape)) for a in arrays],
        [(s, f32, whole_spec(s)) for s in shapes],
        after=after, scratch=[pltpu.VMEM((2 * value.shape[0], LANE), bf16)], flops=1000,
    )


def widen_kernel(*refs):
    count = len(refs) // 2
    for source, target in zip(refs[:count], refs[count:]):
        target[...] = source[...].astype(f32)


def widen(arrays):
    return kernel_call(
        widen_kernel, "widen", [(a, whole_spec(a.shape)) for a in arrays],
        [(a.shape, f32, whole_spec(a.shape)) for a in arrays], flops=1000,
    )


class Rows:
    def __init__(self, refs, per):
        self.refs, self.per, self.shape = refs, per, refs[0].shape

    def __getitem__(self, _):
        step = pl.program_id(0)
        value = self.refs[0][...]
        for u in range(1, len(self.refs)):
            value = jnp.where(step >= u * self.per, self.refs[u][...], value)
        return value


class Places:
    def __init__(self, refs, per, parts, tile):
        self.refs, self.per, self.parts = refs, per, parts

    def value(self, mine):
        step = pl.program_id(0)
        found = []
        own = len(self.refs) // self.parts
        count = self.parts // self.per
        for k in range(count):
            place = lax.rem(step, self.per) * count + k
            chosen = None
            for u in range(own):
                here = at_place(mine, place, [self.refs[s * own + u][...] for s in range(self.parts)])
                chosen = here if chosen is None else jnp.where(step >= u * self.per, here, chosen)
            found.append(chosen)
        return jnp.concatenate(found, axis=0) if count > 1 else found[0]


def row_call(kernel, name, rows, tile, scalars, tiled, fixed, tiled_out, fixed_out, after=(), scratch=(), flops=0):
    def block(width):
        return pl.BlockSpec((tile, width), lambda i: (i, 0))

    operands = [(a, SCALARS) for a in scalars]
    wraps = []
    for a in tiled:
        start = len(operands)
        if isinstance(a, list):
            parts = len(a)
            length = parts * a[0][0].shape[0]
            per = length // tile
            operands += [(p, whole_spec(p.shape)) for row in a for p in row]
            wraps.append((start, len(operands), lambda r, n=per, k=parts: Places(r, n, k, tile)))
        elif isinstance(a, tuple):
            per = a[0].shape[0] // tile
            for u, array in enumerate(a):
                spec = pl.BlockSpec(
                    (tile, array.shape[1]), lambda i, u=u: (jnp.clip(i - u * per, 0, per - 1), 0)
                )
                operands.append((array, spec))
            wraps.append((start, len(operands), lambda r, n=per: Rows(r, n)))
        else:
            operands.append((a, block(a.shape[1])))
            wraps.append((start, start + 1, lambda r: r[0]))
    first = len(scalars)
    last = len(operands)

    def body(*refs):
        kernel(*refs[:first], *[wrap(refs[i:j]) for i, j, wrap in wraps], *refs[last:])

    return kernel_call(
        body, name,
        operands + [(a, whole_spec(a.shape)) for a in fixed],
        [((rows, w), d, block(w)) for w, d in tiled_out]
        + [(s, k, whole_spec(s)) for s, k in fixed_out],
        grid=(rows // tile,),
        after=after,
        scratch=[pltpu.VMEM(s, f32) for s in scratch],
        flops=flops,
    )


def first_block(lens, length, tiled, fixed, tile=496):
    D, F = fixed[2].shape
    rows = len(tiled[0]) * length
    return row_call(
        functools.partial(first_kernel, tile=tile, length=length), "first_block", rows, tile,
        (lens,), tiled, fixed,
        ((D, f32), (1, f32), (F, bf16), (D, f32), (1, f32), (D, bf16), (D, bf16), (D, bf16)), (),
        flops=15_000_000_000,
    )


def second_block(mine, tiled, fixed, tile=496):
    rows, D = tiled[0].shape
    F = fixed[3].shape[1]
    return row_call(
        second_kernel, "second_block", rows, tile, (mine,), tiled, fixed,
        ((FULL, bf16), (D, f32), (D, f32)),
        (((8, D), f32), ((D, D), bf16), ((D, F), bf16), ((D, F), bf16)),
        scratch=((D, D), (D, F), (D, F)),
        flops=30_000_000_000,
    )


def third_block(lens, length, unit, tiled, fixed, after, tile=496):
    rows, D = tiled[0].shape
    M = tiled[-1][0].shape[1]
    F = fixed[3].shape[1]
    tall, wide, square = up(D, 16), up(F, LANE), up(D, LANE)
    return row_call(
        functools.partial(third_kernel, tile=tile, length=length), "third_block", rows, tile,
        (lens,), tiled, fixed, ((D, f32), (M, bf16)),
        (((8, D), f32), ((middle_rows(D, F, unit), LANE), bf16)),
        scratch=((tall, wide), (tall, wide), (tall, square), (tall, square), (M, D)),
        after=after, flops=30_000_000_000,
    )


def pack_block(unit, groups, whole, pos, bias, small, depth, taps, after, tile=496):
    seqs = len(whole)
    D = small.shape[1]
    rows = seqs * whole[0].shape[0]
    width = sum(g[0].shape[1] for g in groups)
    return row_call(
        functools.partial(pack_kernel, groups=len(groups), seqs=seqs), "pack_block", rows, tile,
        (), (*groups, whole), (*pos, *bias, small, depth),
        (), (((late_rows(D, taps, unit), LANE), bf16),),
        scratch=((FULL, width),), after=after, flops=5_000_000_000,
    )[0]


def swap_pairs(size, distance):
    return [(i, i ^ distance) for i in range(size)]


def axis_steps(axis, first=1):
    size = lax.axis_size(axis)
    steps = []
    distance = first
    while distance < size:
        steps.append((axis, size, distance))
        distance *= 2
    return steps


def butterfly_sum(value):
    for axis, size, distance in axis_steps("batch") + axis_steps("tm"):
        value = value + lax.ppermute(value, axis, swap_pairs(size, distance))
    return value


def scatter_step(value, step):
    axis, size, distance = step
    bit = (lax.axis_index(axis) // distance) % 2
    half = value.shape[0] // 2
    sent = lax.dynamic_slice_in_dim(value, (1 - bit) * half, half, 0).astype(bf16)
    kept = lax.dynamic_slice_in_dim(value, bit * half, half, 0).astype(f32)
    got = lax.ppermute(sent, axis, swap_pairs(size, distance))
    return kept + got.astype(f32), got


def gather_step(value, step):
    axis, size, distance = step
    bit = (lax.axis_index(axis) // distance) % 2
    other = lax.ppermute(value, axis, swap_pairs(size, distance))
    return jnp.concatenate(
        [jnp.where(bit == 0, value, other), jnp.where(bit == 0, other, value)]
    )


def ring_plan():
    batch = axis_steps("batch")
    return batch[:1], batch[1:2], axis_steps("tm"), batch[2:]


def exchange_sum(value, step):
    axis, size, distance = step
    low = value.astype(bf16)
    got = lax.ppermute(low, axis, swap_pairs(size, distance))
    return low.astype(f32) + got.astype(f32), got


def scatter_sum(value, after=(), split=False):
    core, across, tm, rest = ring_plan()
    arrived = []
    for step in core:
        value, got = scatter_step(value, step)
        arrived.append([got])
    half = value.shape[0] // 2
    streams = [value[:half], value[half:]]
    for steps in zip(across + tm, tm + across):
        pair = [scatter_step(v, s) for v, s in zip(streams, steps)]
        streams = [p[0] for p in pair]
        arrived.append([p[1] for p in pair])
    value = jnp.concatenate(streams)
    if split:
        for step in rest:
            value, got = scatter_step(value, step)
            arrived.append([got])
        value = value.astype(bf16)
        for step in rest[::-1]:
            value = gather_step(value, step)
        return value, arrived
    for index, step in enumerate(rest):
        if after and index == len(rest) - 1:
            value = hold(value, after)
        value, got = exchange_sum(value, step)
        arrived.append([got])
    return value.astype(bf16), arrived


def merge_kernel(bits_ref, *refs, joined):
    count = bits_ref.shape[0]
    out_refs = refs[2 * count :]
    at = 0
    for i in range(count):
        value, other = refs[i], refs[count + i]
        rows = value.shape[0]
        out_ref = out_refs[0] if joined else out_refs[i]
        for ref, place in ((value, bits_ref[i]), (other, 1 - bits_ref[i])):
            out_ref[pl.ds(pl.multiple_of(at + place * rows, 16), rows), :] = ref[...]
        at += 2 * rows if joined else 0


def merge(bits, values, others, joined, after):
    arrays = list(values) + list(others)
    shapes = [(2 * v.shape[0], LANE) for v in values]
    if joined:
        shapes = [(sum(s[0] for s in shapes), LANE)]
    return kernel_call(
        functools.partial(merge_kernel, joined=joined), "merge",
        [(jnp.stack(bits).astype(jnp.int32), SCALARS)]
        + [(a, whole_spec(a.shape)) for a in arrays],
        [(s, bf16, whole_spec(s)) for s in shapes], after=after, flops=1000,
    )


def gather_all(streams, after):
    core, across, tm, _ = ring_plan()
    stages = list(zip(across + tm, tm + across))[::-1]
    for index, steps in enumerate(stages):
        last = index == len(stages) - 1
        bits = [(lax.axis_index(a) // d) % 2 for a, _, d in steps]
        others = [lax.ppermute(v, a, swap_pairs(n, d)) for v, (a, n, d) in zip(streams, steps)]
        streams = merge(bits, streams, others, last, after if last else ())
    value = streams[0]
    axis, size, distance = core[0]
    bit = (lax.axis_index(axis) // distance) % 2
    return bit, value, lax.ppermute(value, axis, swap_pairs(size, distance))


def scatter_parts():
    core, across, tm, rest = ring_plan()
    return 2 ** (len(core) + 1 + len(across) + len(tm))


def hold_kernel(a_ref, out_ref):
    out_ref[...] = a_ref[...]


def hold(value, after):
    spec = whole_spec(value.shape)
    return kernel_call(
        hold_kernel, "hold", [(value, spec)], [(value.shape, value.dtype, spec)], after=after,
        flops=1000,
    )[0]


def join_kernel(a_ref, b_ref, first_ref, second_ref):
    a, b = a_ref.shape[0] // 2, b_ref.shape[0] // 2
    for i, ref in enumerate((first_ref, second_ref)):
        ref[:a, :] = a_ref[i * a : (i + 1) * a, :]
        ref[a:, :] = b_ref[i * b : (i + 1) * b, :]


def join_shards(a, b, after):
    shape = ((a.shape[0] + b.shape[0]) // 2, LANE)
    return kernel_call(
        join_kernel, "join_shards", [(x, whole_spec(x.shape)) for x in (a, b)],
        [(shape, a.dtype, whole_spec(shape))] * 2, after=after, flops=1000,
    )


def rotation(size, shift):
    return [(i, (i + shift) % size) for i in range(size)]


def assemble_kernel(mine_ref, *refs, parts, own):
    out_ref = refs[-1]
    D, _, rows = out_ref.shape
    mine = mine_ref[0]
    base = pl.multiple_of(mine * rows, 8)
    for u in range(own):
        pieces = [refs[u][pl.ds(base, rows), :]]
        pieces += [refs[own + k * own + u][...] for k in range(parts - 1)]
        for place in range(parts):
            value = at_place(mine, place, pieces)[:, :D].astype(f32)
            out_ref[:, place * own + u, :] = jnp.transpose(value).astype(bf16)


def assemble(whole, pieces, mine, D, after=()):
    own = len(whole)
    parts = len(pieces) + 1
    arrays = list(whole) + [p for row in pieces for p in row]
    shape = (D, parts * own, whole[0].shape[0] // parts)
    out = kernel_call(
        functools.partial(assemble_kernel, parts=parts, own=own), "assemble",
        [(mine, SCALARS)] + [(a, whole_spec(a.shape)) for a in arrays],
        [(shape, bf16, whole_spec(shape))], after=after, flops=1000, vmem=MOST,
    )[0]
    return out


def send_pieces(pieces):
    parts = len(pieces)
    return [pieces[0]] + [
        [lax.ppermute(p, "tm", rotation(parts, shift)) for p in pieces[shift]]
        for shift in range(1, parts)
    ]


def send_frames(whole, mine):
    parts = lax.axis_size("tm")
    rows = whole.shape[0] // parts
    pieces = []
    for shift in range(1, parts):
        piece = lax.dynamic_slice_in_dim(whole, lax.rem(mine + shift, parts) * rows, rows, 0)
        pieces.append(lax.ppermute(piece, "tm", rotation(parts, shift)))
    return pieces


def on_device(
    frames,
    lengths,
    cotangent,
    query_weight,
    key_weight,
    value_weight,
    position_weight,
    content_bias,
    position_bias,
    output_weight,
    attend_gain,
    attend_shift,
    inner_first,
    outer_first,
    first_gain,
    first_shift,
    glu_weight,
    depth_weight,
    batch_gain,
    batch_shift,
    point_weight,
    conv_gain,
    conv_shift,
    inner_second,
    outer_second,
    second_gain,
    second_shift,
):
    seq_local, local_rows, D = frames.shape
    H = HEADS
    hs = D // H
    F = inner_first.shape[1]
    taps = depth_weight.shape[0]
    half = D // 2
    at = half - LANE
    parts = lax.axis_size("tm")
    mine = lax.axis_index("tm")
    unit = 16 * scatter_parts()
    U = seq_local // parts
    T = local_rows * parts
    R = U * T
    lens = lax.dynamic_slice_in_dim(lengths, mine * U, U)

    place = mine.astype(jnp.int32).reshape(1)
    pieces = []
    for u in range(U):
        earlier = tuple(p[0] for p in pieces[-1][1:]) if pieces else ()
        pieces.append(send_pieces(split_frames(frames, place, (u,), after=earlier)))
    zero = jnp.zeros((D,), f32)
    vec = jnp.stack(
        [
            content_bias, position_bias, attend_gain, attend_shift, first_gain, first_shift,
            batch_gain, batch_shift, conv_gain, conv_shift, second_gain, second_shift,
            zero, zero, zero, zero,
        ]
    )
    outer_first_t, outer_second_t = outer_first.T, outer_second.T
    (
        query_x, kv_x, pos_x, output_x, bias_x, back_x, lin_t, gate_t,
        sines, cosines, sines_low, sines_t, cosines_t,
    ) = prepare(
        T, vec, query_weight, key_weight, value_weight, position_weight, output_weight, glu_weight.T
    )

    attended = [
        attend_forward(
            u, hs, lens, place, [row[0] for row in pieces[u]],
            query_x, kv_x, pos_x, bias_x, sines, cosines, sines_low,
        )
        for u in range(U)
    ]
    mixed = tuple(a[0] for a in attended)
    whole = tuple(a[5] for a in attended)
    upstream = send_pieces(split_frames(cotangent, place, tuple(range(U)), after=mixed[-1:]))
    unit_one, inv_one, inner_one, unit_two, inv_two, linear, sigma, spread = first_block(
        lens, T, (whole, mixed),
        (vec, output_x, inner_first, outer_first_t, lin_t, gate_t),
    )
    spread = spread.reshape(U, T, D)
    conv_out, stat = conv_forward(lens, spread, depth_weight)
    stat = butterfly_sum(stat)
    block_out, grad_centred, grad_three, sums, grad_point, grad_inner_two, grad_outer_two = (
        second_block(
            place, (unit_two, conv_out.reshape(R, D), upstream),
            (stat, vec, point_weight, inner_second, outer_second_t),
        )
    )
    early = lax.psum((grad_inner_two, grad_outer_two, grad_point), ("batch", "tm"))
    block_out = [block_out[u * T : (u + 1) * T] for u in range(U)]
    out_pieces = [send_frames(b, mine) for b in block_out]
    sums = butterfly_sum(sums)
    def backward(stat, sums, grad_centred, grad_three):
        grad_spread, grad_depth = conv_backward(
            lens, spread, grad_centred.reshape(U, T, D), conv_out, depth_weight, stat, sums, vec, BGAIN
        )
        grad_one, grad_mixed, small_one, middle = (
            third_block(
                lens, T, unit,
                (
                    grad_spread.reshape(R, D), linear, sigma, unit_two, inv_two, grad_three,
                    inner_one, unit_one, inv_one, mixed,
                ),
                (vec, lin_t, gate_t, inner_first, outer_first_t, output_x),
                after=tuple(p for row in out_pieces for p in row),
            )
        )
        middle_shard, arrived = scatter_sum(middle, split=True)
        waits = iter([()] + arrived)
        groups = 2
        count = H // groups
        back, frames_grad, grad_pieces = [], [], []
        for u in range(U):
            for g in range(groups):
                back.append(
                    attend_backward(
                        u, hs, g * count, count, *attended[u][1:5], grad_mixed, mixed[u], pos_x,
                        sines_low, sines_t, cosines_t, after=tuple(next(waits, ())),
                    )
                )
            if u < U - 1:
                frames_grad.append(
                    frames_block(u, [b[0] for b in back[-groups:]], grad_one, back_x)
                )
                grad_pieces.append(send_frames(frames_grad[-1], mine))
        earlier = tuple(p for row in grad_pieces for p in row)
        late = pack_block(
            unit, [tuple(b[0] for b in back[g::groups]) for g in range(groups)], whole,
            [b[1] for b in back], [b[2] for b in back], small_one, grad_depth, taps,
            after=tuple(next(waits, ())) + earlier,
        )
        frames_grad.append(
            frames_block(U - 1, [b[0] for b in back[-groups:]], grad_one, back_x, after=(late,))
        )
        grad_pieces.append(send_frames(frames_grad[-1], mine))
        block_raw = assemble(block_out, list(zip(*out_pieces)), place, D)
        late_shard, _ = scatter_sum(late, after=tuple(grad_pieces[-1]) + (block_raw,))
        return block_raw, frames_grad, grad_pieces, middle_shard, late_shard

    shapes = jax.eval_shape(backward, stat, sums, grad_centred, grad_three)
    block_out, frames_grad, grad_pieces, middle_shard, late_shard = lax.cond(
        stat[2, 0] > 0.0,
        backward,
        lambda *_: jax.tree.map(lambda s: jnp.zeros(s.shape, s.dtype), shapes),
        stat, sums, grad_centred, grad_three,
    )
    frames_grad = assemble(frames_grad, list(zip(*grad_pieces)), place, D)
    cuts = [s.shape[0] // 2 for s in (middle_shard, late_shard)]
    grad_inner_two, grad_outer_two, grad_point = widen(early)
    bit, value, other = gather_all(
        join_shards(middle_shard, late_shard, early[2:]), after=(frames_grad, grad_point)
    )
    (
        grad_inner_one, grad_outer_one, grad_glu, grad_output, grad_query, grad_key, grad_value, grad_position, small, grad_depth,
    ) = unpack(
        bit.astype(jnp.int32).reshape(1), value, other, bias_x, D, F, taps, *cuts, after=()
    )
    return (
        jnp.transpose(block_out, (1, 2, 0)),
        jnp.transpose(frames_grad, (1, 2, 0)),
        grad_query,
        grad_key,
        grad_value,
        grad_position,
        small[0],
        small[1],
        grad_output,
        small[8],
        small[9],
        grad_inner_one,
        grad_outer_one.T,
        small[10],
        small[11],
        grad_glu.T,
        grad_depth[:taps],
        sums[0],
        sums[1],
        grad_point,
        sums[2],
        sums[3],
        grad_inner_two,
        grad_outer_two.T,
        sums[4],
        sums[5],
    )


def solution(mesh):
    split = P("batch", "tm", None)
    return jax.shard_map(
        on_device,
        mesh=mesh,
        in_specs=(split, P("batch"), split) + (P(),) * 24,
        out_specs=(split, split) + (P(),) * 24,
        check_vma=False,
    )
```

```python
import functools
import math

import jax
import jax.numpy as jnp
from jax import lax
from jax.experimental import pallas as pl
from jax.experimental.pallas import tpu as pltpu
from jax.sharding import PartitionSpec as P

HEADS = 4
EPSILON = 1e-05
MASKED = -1e30
PAD = 16
LOG2E = 1.4426950408889634
LN2 = 0.6931471805599453
LANE = 128
WIDE = 256
FULL = 384
VMEM = 28 * 1024 * 1024
MOST = 56 * 1024 * 1024
bf16 = jnp.bfloat16
f32 = jnp.float32


def dot(a, b):
    return jnp.dot(a, b, preferred_element_type=f32)


def dot_nt(a, b):
    return lax.dot_general(a, b, (((1,), (1,)), ((), ())), preferred_element_type=f32)


def dot_tn(a, b):
    return lax.dot_general(a, b, (((0,), (0,)), ((), ())), preferred_element_type=f32)


def lanes(shape):
    return lax.broadcasted_iota(jnp.int32, shape, 1)


def sublanes(shape):
    return lax.broadcasted_iota(jnp.int32, shape, 0)


def kernel_call(kernel, name, operands, out, grid=(1,), after=(), scratch=(), flops=0, vmem=VMEM):
    count = len(operands)
    extra = len(after)

    def body(*refs):
        kernel(*refs[:count], *refs[count + extra :])

    return pl.pallas_call(
        body,
        grid=grid,
        in_specs=[spec for _, spec in operands] + [pl.BlockSpec(memory_space=pl.ANY)] * extra,
        out_specs=[spec for _, _, spec in out],
        out_shape=[jax.ShapeDtypeStruct(shape, kind) for shape, kind, _ in out],
        scratch_shapes=list(scratch),
        compiler_params=pltpu.CompilerParams(
            vmem_limit_bytes=vmem, dimension_semantics=("arbitrary",) * len(grid)
        ),
        cost_estimate=pl.CostEstimate(flops=flops, bytes_accessed=1000000, transcendentals=0)
        if flops
        else None,
        name=name,
    )(*[array for array, _ in operands], *after)


def whole_spec(shape):
    return pl.BlockSpec(tuple(shape), lambda *_: (0,) * len(shape))


SCALARS = pl.BlockSpec(memory_space=pltpu.SMEM)


def split_kernel(mine_ref, x_ref, *out_refs, parts, own, seqs):
    mine = mine_ref[0]
    D = x_ref.shape[0]
    for place in range(parts):
        shift = lax.rem(place - mine + parts, parts)
        for i, u in enumerate(seqs):
            rows = jnp.transpose(x_ref[:, place * own + u, :].astype(f32)).astype(bf16)
            spare = jnp.zeros((rows.shape[0], FULL - D), bf16)
            rows = jnp.concatenate([rows, spare], axis=1)
            for k in range(parts):

                @pl.when(shift == k)
                def _():
                    out_refs[k][i * rows.shape[0] : (i + 1) * rows.shape[0], :] = rows


def split_frames(frames, mine, seqs, after=()):
    count, rows, D = frames.shape
    parts = lax.axis_size("tm")
    across = jnp.transpose(frames, (2, 0, 1))
    pieces = kernel_call(
        functools.partial(split_kernel, parts=parts, own=count // parts, seqs=seqs),
        "split_frames",
        [(mine, SCALARS), (across, whole_spec(across.shape))],
        [((len(seqs) * rows, FULL), bf16, whole_spec((len(seqs) * rows, FULL)))] * parts,
        after=after, flops=3_000_000_000,
    )
    return pieces


def at_place(mine, place, pieces):
    parts = len(pieces)
    shift = lax.rem(mine - place + parts, parts)
    chosen = pieces[0]
    for k in range(1, parts):
        chosen = jnp.where(shift == k, pieces[k], chosen)
    return chosen


def pick(rows, cols, start, at, size):
    row, col = sublanes((rows, cols)), lanes((rows, cols))
    return jnp.where((row - start == col - at) & (row >= start) & (row < start + size), 1.0, 0.0)


def prepare_kernel(
    vec_ref, wq_ref, wk_ref, wv_ref, wp_ref, wout_ref, glu_ref,
    q_ref, kv_ref, pos_ref, out_ref, bias_ref, back_ref, lin_ref, gate_ref,
    sin_ref, cos_ref, low_ref, sin_t_ref, cos_t_ref, *, length,
):
    D = wq_ref.shape[0]
    hs = D // HEADS
    half = D // 2
    at = half - LANE
    wq, wk, wv = wq_ref[...], wk_ref[...], wv_ref[...]
    vec = vec_ref[...]
    feature = sublanes((2 * WIDE, D))
    column = lanes((2 * WIDE, D))
    spread_rows = jnp.where(
        ((feature == column) & (column < half))
        | ((feature - WIDE == column - half) & (column >= half)),
        1.0, 0.0,
    ).astype(bf16)
    pos = dot(spread_rows, wp_ref[...]).astype(bf16)
    for h in range(HEADS):
        mid = pick(D, LANE, h * hs, at, hs)
        low = mid.astype(bf16)
        first = pick(D, LANE, h * hs, 0, hs).astype(bf16)
        spare = jnp.zeros((FULL - D, LANE), f32)
        q_ref[h] = jnp.concatenate([dot(wq, low), spare], axis=0).astype(bf16)
        kv_ref[h, :, :LANE] = jnp.concatenate([dot(wk, low), spare], axis=0).astype(bf16)
        kv_ref[h, :, LANE:] = jnp.concatenate([dot(wv, first), spare], axis=0).astype(bf16)
        mid_t = pick(LANE, D, at, h * hs, hs).astype(bf16)
        pos_ref[h] = dot_nt(mid_t, pos).astype(bf16)
        bias_ref[h] = lax.dot_general(
            vec, mid, (((1,), (0,)), ((), ())), precision=lax.Precision.HIGHEST,
            preferred_element_type=f32,
        )
        out_ref[h * LANE : (h + 1) * LANE, :] = dot(
            pick(LANE, D, 0, h * hs, hs).astype(bf16), wout_ref[...]
        ).astype(bf16)
        back = None
        for i, w in enumerate((wv, wq, wk)):
            part = dot_nt(pick(WIDE, D, i * hs, h * hs, hs).astype(bf16), w)
            back = part if back is None else back + part
        back_ref[h * WIDE : (h + 1) * WIDE, :] = back.astype(bf16)
    lin_ref[...] = glu_ref[:D, :]
    gate_ref[...] = glu_ref[D:, :]

    rate = -2.0 * math.log(10000.0) / D

    def waves(position, index):
        angle = position.astype(f32) * jnp.exp(index.astype(f32) * rate)
        inside = index < half
        return jnp.where(inside, jnp.sin(angle), 0.0), jnp.where(inside, jnp.cos(angle), 0.0)

    shape = (32, WIDE)
    base_s, base_c = waves(sublanes(shape), lanes(shape))
    step_s, step_c = waves(sublanes(shape) * 32, lanes(shape))
    for i in range(length // 32):
        s, c = step_s[i : i + 1], step_c[i : i + 1]
        rows = pl.ds(i * 32, 32)
        sine = s * base_c + c * base_s
        sin_ref[rows, :] = sine
        cos_ref[rows, :] = c * base_c - s * base_s
        low_ref[rows, :] = sine.astype(bf16)
    shape = (WIDE, LANE)
    base_s, base_c = waves(lanes(shape), sublanes(shape))
    step_s, step_c = waves(lanes(shape) * LANE, sublanes(shape))
    for i in range(-(-length // LANE)):
        s, c = step_s[:, i : i + 1], step_c[:, i : i + 1]
        width = min(LANE, length - i * LANE)
        sin_t_ref[:, i * LANE : i * LANE + width] = (s * base_c + c * base_s)[:, :width]
        cos_t_ref[:, i * LANE : i * LANE + width] = (c * base_c - s * base_s)[:, :width]


def prepare(length, vec, wq, wk, wv, wp, wout, glu):
    D = wq.shape[0]
    arrays = (vec, wq, wk, wv, wp, wout, glu)
    shapes = (
        ((HEADS, FULL, LANE), bf16), ((HEADS, FULL, WIDE), bf16), ((HEADS, LANE, 2 * WIDE), bf16),
        ((HEADS * LANE, D), bf16), ((HEADS,) + vec.shape[:1] + (LANE,), f32),
        ((HEADS * WIDE, D), bf16), ((D, D), bf16), ((D, D), bf16),
        ((length, WIDE), f32), ((length, WIDE), f32), ((length, WIDE), bf16),
        ((WIDE, length), f32), ((WIDE, length), f32),
    )
    return kernel_call(
        functools.partial(prepare_kernel, length=length), "prepare",
        [(a, whole_spec(a.shape)) for a in arrays],
        [(s, k, whole_spec(s)) for s, k in shapes],
        flops=5_000_000_000, vmem=MOST,
    )


def attend_forward_kernel(
    len_ref, mine_ref, *refs, parts, seq, hs, tile,
):
    pieces = refs[:parts]
    q_ref, kv_ref, pos_ref, bias_ref, sin_ref, cos_ref, low_ref = refs[parts : parts + 7]
    mixed_ref, qa_ref, qb_ref, ka_ref, v_ref, f_ref = refs[parts + 7 :]
    T = f_ref.shape[0]
    count = pieces[0].shape[0]

    @pl.when(pl.program_id(0) == 0)
    def _():
        for place in range(parts):
            f_ref[place * count : (place + 1) * count, :] = at_place(
                mine_ref[0], place, [p[...] for p in pieces]
            )

    one = 3 * hs - LANE
    scale = LOG2E / math.sqrt(hs)
    valid = len_ref[seq]
    lane = lanes((tile, LANE))

    def key_rows(h, r0):
        rows = pl.ds(r0, tile)
        kv = dot(f_ref[rows, :], kv_ref[h])
        k = kv[:, :LANE] + cos_ref[rows, LANE:]
        row = sublanes((tile, LANE)) + r0
        k = jnp.where(lane == one, jnp.where(row < valid, 0.0, MASKED), k)
        k = jnp.where((lane > one) & (lane < one + 4), 1.0, k)
        ka_ref[h, rows, :LANE] = cos_ref[rows, :LANE].astype(bf16)
        ka_ref[h, rows, LANE:] = k.astype(bf16)
        v = jnp.where((lane == hs) | (lane == hs + 1), 1.0, kv[:, LANE:])
        v_ref[h, rows, :] = v.astype(bf16)

    def score_rows(h, r0):
        rows = pl.ds(r0, tile)
        q = dot(f_ref[rows, :], q_ref[h])
        e = dot((q + bias_ref[h, 1:2, :]).astype(bf16), pos_ref[h])
        es, ec = e[:, :WIDE], e[:, WIDE:]
        s, c = sin_ref[rows, :], cos_ref[rows, :]
        qb = ((ec * s - es * c) * scale).astype(bf16)
        qb_ref[h, rows, :] = qb
        a = (es * s + ec * c) * scale
        first = a[:, :LANE].astype(bf16)
        second = jnp.where(lane == one, 1.0, a[:, LANE:] + (q + bias_ref[h, 0:1, :]) * scale)
        second = second.astype(bf16)
        qa_ref[h, rows, :LANE] = first
        qa = jnp.concatenate([first, second], axis=1)
        return second, dot_nt(qa, ka_ref[h]) + dot_nt(qb, low_ref[...])

    def mix_rows(h, r0, second, scores):
        rows = pl.ds(r0, tile)
        peak = jnp.max(scores, axis=1, keepdims=True)
        p = jnp.exp2(scores - peak).astype(bf16)
        o = dot(p, v_ref[h])
        total = o[:, hs : hs + 1]
        mixed_ref[rows, h * LANE : (h + 1) * LANE] = (o / total).astype(bf16)
        log_total = -(peak + jnp.log2(total))
        hi = log_total.astype(bf16).astype(f32)
        mid = (log_total - hi).astype(bf16).astype(f32)
        rest = jnp.where(lane == one + 1, hi, jnp.where(lane == one + 2, mid, log_total - hi - mid))
        second = jnp.where((lane > one) & (lane < one + 4), rest, second.astype(f32))
        qa_ref[h, rows, LANE:] = second.astype(bf16)

    tasks = [(h, r0) for h in range(q_ref.shape[0]) for r0 in range(0, T, tile)]
    for task in tasks:
        key_rows(*task)
    waiting = None
    for task in tasks:
        current = (*task, *score_rows(*task))
        if waiting is not None:
            mix_rows(*waiting)
        waiting = current
    mix_rows(*waiting)


def attend_forward(seq, head_size, lens, mine, pieces, q, kv, pos, bias, sines, cosines, low, tile=496):
    T = sines.shape[0]
    H = q.shape[0]
    group = 2

    def head(shape):
        return pl.BlockSpec((group,) + shape[1:], lambda h: (h, 0, 0))

    def three(width):
        return ((H, T, width), bf16, pl.BlockSpec((group, T, width), lambda h: (h, 0, 0)))

    return kernel_call(
        functools.partial(
            attend_forward_kernel, parts=len(pieces), seq=seq, hs=head_size, tile=tile
        ),
        "attend_forward",
        [(lens, SCALARS), (mine, SCALARS)]
        + [(p, whole_spec(p.shape)) for p in pieces]
        + [(a, head(a.shape)) for a in (q, kv, pos, bias)]
        + [(a, whole_spec(a.shape)) for a in (sines, cosines, low)],
        [((T, H * LANE), bf16, pl.BlockSpec((T, group * LANE), lambda h: (0, h)))]
        + [three(w) for w in (WIDE, WIDE, WIDE, LANE)]
        + [((T, FULL), bf16, whole_spec((T, FULL)))],
        grid=(H // group,),
        flops=15_000_000_000, vmem=40 * 1024 * 1024,
    )


def attend_backward_kernel(
    qa_ref, qb_ref, ka_ref, v_ref, do_ref, mixed_ref, pos_ref, low_ref, sin_ref, cos_ref,
    d_ref, dpos_ref, bias_ref, *, hs, tile,
):
    T = qa_ref.shape[1]
    at = 2 * hs - LANE
    inv = 1.0 / math.sqrt(hs)
    do = do_ref[...]
    wide = do.astype(f32)
    delta = -jnp.sum(wide * mixed_ref[...].astype(f32), axis=1, keepdims=True)
    hi = delta.astype(bf16).astype(f32)
    lane = lanes((T, LANE))
    dox = jnp.where(lane == hs, hi, jnp.where(lane == hs + 1, delta - hi, wide)).astype(bf16)
    qa = qa_ref[0]
    qb = qb_ref[0]
    da = db = None
    parts = []
    for r0 in range(0, T, tile):
        rows = pl.ds(r0, tile)
        ka = ka_ref[0, rows, :]
        low = low_ref[rows, :]
        p = jnp.exp2(dot_nt(ka, qa) + dot_nt(low, qb))
        ds = (p * dot_nt(v_ref[0, rows, :], dox)).astype(bf16)
        dv = dot(p.astype(bf16), do)
        dk = dot(ds, qa[:, LANE:])
        a, b = dot_tn(ka, ds), dot_tn(low, ds)
        da = a if da is None else da + a
        db = b if db is None else db + b
        parts.append((dv, dk))
    s, c = sin_ref[...], cos_ref[...]
    des = (da * s - db * c) * inv
    dec = (da * c + db * s) * inv
    de = jnp.concatenate([des.astype(bf16), dec.astype(bf16)], axis=0)
    dqp = dot(pos_ref[0], de)
    dpos = dot(de, qa[:, LANE:])
    sub = sublanes((LANE, T))
    dqc = jnp.where((sub >= at) & (sub < at + hs), da[LANE:] * inv, 0.0)
    ones = jnp.ones((16, T), bf16)
    bias = jnp.where(
        sublanes((16, LANE)) == 0, dot_nt(ones, dqc.astype(bf16)), dot_nt(ones, dqp.astype(bf16))
    )

    dpos_ref[0] = dpos
    bias_ref[0] = bias
    dq = jnp.transpose(dqc + dqp)
    dq = pltpu.roll(jnp.concatenate([jnp.zeros((T, LANE), f32), dq], axis=1), WIDE - hs, 1)
    lane = lanes((tile, LANE))
    for i, (dv, dk) in enumerate(parts):
        rows = pl.ds(i * tile, tile)
        dq_rows = dq[i * tile : (i + 1) * tile]
        d_ref[rows, :LANE] = jnp.where(lane < hs, dv, dq_rows[:, :LANE]).astype(bf16)
        inside = (lane >= at) & (lane < at + hs)
        d_ref[rows, LANE:] = jnp.where(inside, dk * LN2, dq_rows[:, LANE:]).astype(bf16)


def attend_backward(
    seq, head_size, first, count, qa, qb, ka, v, do, mixed, pos, low, sin_t, cos_t, after, vmem=VMEM, tile=496,
):
    H, T, W = qa.shape

    def three(array):
        return array, pl.BlockSpec((1,) + array.shape[1:], lambda h: (first + h, 0, 0))

    def lane_block(array, u):
        return array, pl.BlockSpec((T, LANE), lambda h: (u, first + h))

    return kernel_call(
        functools.partial(attend_backward_kernel, hs=head_size, tile=tile), "attend_backward",
        [three(qa), three(qb), three(ka), three(v), lane_block(do, seq), lane_block(mixed, 0)]
        + [three(pos)]
        + [(a, whole_spec(a.shape)) for a in (low, sin_t, cos_t)],
        [
            ((T, count * W), bf16, pl.BlockSpec((T, W), lambda h: (0, h))),
            ((count, 2 * W, LANE), f32, pl.BlockSpec((1, 2 * W, LANE), lambda h: (h, 0, 0))),
            ((count, 16, LANE), f32, pl.BlockSpec((1, 16, LANE), lambda h: (h, 0, 0))),
        ],
        grid=(count,),
        after=after, vmem=vmem,
        flops=count * 5_500_000_000,
    )


def fill_padded(buf, value):
    T = value.shape[0]
    zero = jnp.zeros((PAD, buf.shape[1]), f32)
    buf[0:PAD, :] = zero
    buf[T + PAD : T + 2 * PAD, :] = zero
    buf[PAD : T + PAD, :] = value


def fill_weights(wide, w_ref, taps):
    for o in range(taps):
        wide[o] = jnp.broadcast_to(w_ref[o : o + 1, :], (8, LANE))


def tall(values):
    return values.reshape(values.shape[0] // 8, 8, LANE)


def chunks(T, step, body, carry):
    full = T // step
    carry = lax.fori_loop(
        0, full, lambda i, c: body(pl.multiple_of(i * step, 8), step, c), carry
    )
    return body(full * step, T - full * step, carry) if T % step else carry


def conv_forward_kernel(len_ref, x_ref, w_ref, out_ref, stat_ref, padded, wide, *, taps, step):
    u = pl.program_id(1)
    T = x_ref.shape[1]
    half = (taps - 1) // 2
    fill_padded(padded, x_ref[0].astype(f32))
    fill_weights(wide, w_ref, taps)
    valid = len_ref[u]

    def body(base, rows, sums):
        total = None
        for o in range(taps):
            term = wide[o] * tall(padded[pl.ds(base + PAD - half + o, rows), :])
            total = term if total is None else total + term
        out_ref[0, pl.ds(base, rows), :] = total.reshape(rows, LANE)
        row = 8 * lax.broadcasted_iota(jnp.int32, (rows // 8, 8, LANE), 0)
        row = row + lax.broadcasted_iota(jnp.int32, (rows // 8, 8, LANE), 1) + base
        masked = jnp.where(row < valid, total, 0.0)
        return sums[0] + jnp.sum(masked, axis=0), sums[1] + jnp.sum(masked * total, axis=0)

    zero = jnp.zeros((8, LANE), f32)
    first, second = chunks(T, step, body, (zero, zero))
    count = jnp.full((1, LANE), valid, jnp.int32).astype(f32)
    stat = jnp.concatenate(
        [
            jnp.sum(first, axis=0, keepdims=True),
            jnp.sum(second, axis=0, keepdims=True),
            count,
            jnp.zeros((5, LANE), f32),
        ],
        axis=0,
    )

    @pl.when(u == 0)
    def _():
        stat_ref[...] = stat

    @pl.when(u > 0)
    def _():
        stat_ref[...] += stat


def conv_forward(lens, x, w, step=256):
    U, T, C = x.shape
    block = pl.BlockSpec((1, T, LANE), lambda c, u: (u, 0, c))
    return kernel_call(
        functools.partial(conv_forward_kernel, taps=w.shape[0], step=step), "conv_forward",
        [(lens, SCALARS), (x, block), (w, pl.BlockSpec((w.shape[0], LANE), lambda c, u: (0, c)))],
        [((U, T, C), f32, block), ((8, C), f32, pl.BlockSpec((8, LANE), lambda c, u: (0, c)))],
        grid=(pl.cdiv(C, LANE), U),
        scratch=[pltpu.VMEM((T + 2 * PAD, LANE), f32), pltpu.VMEM((w.shape[0], 8, LANE), f32)],
        flops=10_000_000_000,
    )


def batch_moments(stat):
    count = stat[2:3, :]
    mean = stat[0:1, :] / count
    return count, mean, lax.rsqrt(stat[1:2, :] / count - mean * mean + EPSILON)


def conv_backward_kernel(
    len_ref, x_ref, dz_ref, conv_ref, w_ref, stat_ref, sums_ref, vec_ref, gs_ref, gw_ref,
    padded_x, padded_g, wide, *, taps, step, gain_row,
):
    u = pl.program_id(1)
    T = x_ref.shape[1]
    half = (taps - 1) // 2
    valid = len_ref[u]
    count, mean, rstd = batch_moments(stat_ref[...])
    gain = vec_ref[gain_row : gain_row + 1, :]
    grad_var = -0.5 * rstd * rstd * (sums_ref[0:1, :] * gain)
    grad_mean = -rstd * (sums_ref[1:2, :] * gain) - 2.0 * mean * grad_var
    shift = grad_mean / count
    slope = 2.0 * grad_var / count
    row = sublanes((T, LANE))
    g = dz_ref[0] * rstd + jnp.where(row < valid, shift + slope * conv_ref[0], 0.0)
    fill_padded(padded_g, g)
    fill_padded(padded_x, x_ref[0].astype(f32))

    fill_weights(wide, w_ref, taps)

    def spread(base, rows, carry):
        total = None
        for o in range(taps):
            term = wide[o] * tall(padded_g[pl.ds(base + PAD + half - o, rows), :])
            total = term if total is None else total + term
        gs_ref[0, pl.ds(base, rows), :] = total.reshape(rows, LANE)
        return carry

    chunks(T, step, spread, 0)

    zero = jnp.zeros((8, LANE), f32)

    def relate(base, rows, carry):
        centre = tall(padded_g[pl.ds(base + PAD, rows), :])
        new = []
        for o, kept in enumerate(carry):
            moved = tall(padded_x[pl.ds(base + PAD - half + o, rows), :])
            new.append(kept + jnp.sum(centre * moved, axis=0))
        return tuple(new)

    sums = chunks(T, step // 2, relate, (zero,) * taps)
    rows = [jnp.sum(s, axis=0, keepdims=True) for s in sums]
    gw = jnp.concatenate(rows + [jnp.zeros((-taps % 8, LANE), f32)], axis=0)

    @pl.when(u == 0)
    def _():
        gw_ref[...] = gw

    @pl.when(u > 0)
    def _():
        gw_ref[...] += gw


def conv_backward(lens, x, dz, conv, w, stat, sums, vec, gain_row, step=256):
    U, T, C = x.shape
    taps = w.shape[0]
    block = pl.BlockSpec((1, T, LANE), lambda c, u: (u, 0, c))

    def channel(array):
        return array, pl.BlockSpec((array.shape[0], LANE), lambda c, u: (0, c))

    return kernel_call(
        functools.partial(conv_backward_kernel, taps=taps, step=step, gain_row=gain_row),
        "conv_backward",
        [(lens, SCALARS), (x, block), (dz, block), (conv, block)]
        + [channel(a) for a in (w, stat, sums, vec)],
        [((U, T, C), f32, block), ((taps + -taps % 8, C), f32, pl.BlockSpec((taps + -taps % 8, LANE), lambda c, u: (0, c)))],
        grid=(pl.cdiv(C, LANE), U),
        scratch=[pltpu.VMEM((T + 2 * PAD, LANE), f32)] * 2 + [pltpu.VMEM((taps, 8, LANE), f32)],
        flops=20_000_000_000,
    )


CONTENT, POSITION, GAIN1, SHIFT1, GAIN2, SHIFT2, BGAIN, BSHIFT, GAIN3, SHIFT3, GAIN4, SHIFT4 = range(12)


def vector(ref, index):
    return ref[index : index + 1, :]


def sigmoid(x):
    return 0.5 * jnp.tanh(0.5 * x) + 0.5


def unit_norm(values):
    centred = values - jnp.mean(values, axis=-1, keepdims=True)
    inv_std = lax.rsqrt(jnp.mean(centred * centred, axis=-1, keepdims=True) + EPSILON)
    return centred * inv_std, inv_std


def unit_norm_back(unit, inv_std, gain, upstream):
    scaled = upstream * gain
    return inv_std * (
        scaled
        - jnp.mean(scaled, axis=-1, keepdims=True)
        - unit * jnp.mean(scaled * unit, axis=-1, keepdims=True)
    )


def col_sum(values):
    return jnp.sum(values, axis=0, keepdims=True)


def clear(refs):
    @pl.when(pl.program_id(0) == 0)
    def _():
        for ref in refs:
            ref[...] = jnp.zeros(ref.shape, ref.dtype)


def add_into(ref, value):
    rows, cols = value.shape
    ref[:rows, :cols] += value


def up(value, unit):
    return -(-value // unit) * unit


def put_blocks(packed_ref, at, value):
    rows, cols = value.shape
    for c in range(0, cols, LANE):
        packed_ref[at : at + rows, :] = value[:, c : c + LANE].astype(bf16)
        at += rows
    return at


def row_valid(len_ref, step, tile, length):
    per = length // tile
    row = sublanes((tile, 1)) + lax.rem(step, per) * tile
    return row < len_ref[lax.div(step, per)]


def first_kernel(
    len_ref, f_ref, mixed_ref, vec_ref, wout_ref, wi_ref, wo_ref, wl_ref, wg_ref,
    x1_ref, r1_ref, u_ref, x2_ref, r2_ref, lin_ref, sig_ref, spread_ref, *, tile, length,
):
    D = x1_ref.shape[1]
    resid = f_ref[...][:, :D].astype(f32) + dot(mixed_ref[...], wout_ref[...])
    unit, inv_std = unit_norm(resid)
    x1_ref[...] = unit
    r1_ref[...] = inv_std
    hidden = unit * vector(vec_ref, GAIN1) + vector(vec_ref, SHIFT1)
    inner = dot(hidden.astype(bf16), wi_ref[...])
    u_ref[...] = inner.astype(bf16)
    active = (inner * sigmoid(inner)).astype(bf16)
    resid = hidden + dot_nt(active, wo_ref[...])
    unit, inv_std = unit_norm(resid)
    x2_ref[...] = unit
    r2_ref[...] = inv_std
    entry = (unit * vector(vec_ref, GAIN2) + vector(vec_ref, SHIFT2)).astype(bf16)
    lin = dot_nt(entry, wl_ref[...])
    sig = sigmoid(dot_nt(entry, wg_ref[...]))
    lin_ref[...] = lin.astype(bf16)
    sig_ref[...] = sig.astype(bf16)
    valid = row_valid(len_ref, pl.program_id(0), tile, length)
    spread_ref[...] = jnp.where(valid, lin * sig, 0.0).astype(bf16)


def second_kernel(
    mine_ref, x2_ref, conv_ref, cot_ref, stat_ref, vec_ref, wp_ref, wi_ref, wo_ref,
    out_ref, dz_ref, g3_ref, small_ref, dwp_ref, dwi_ref, dwo_ref, sum_p, sum_i, sum_o,
):
    clear((small_ref, sum_p, sum_i, sum_o))
    _, mean, rstd = batch_moments(stat_ref[...])
    centred = (conv_ref[...] - mean) * rstd
    batch_gain = vector(vec_ref, BGAIN)
    normed = centred * batch_gain + vector(vec_ref, BSHIFT)
    sig_n = sigmoid(normed)
    swished = (normed * sig_n).astype(bf16)
    slope_n = (sig_n * (1.0 + normed * (1.0 - sig_n))).astype(bf16)
    hidden_two = x2_ref[...] * vector(vec_ref, GAIN2) + vector(vec_ref, SHIFT2)
    unit3, inv3 = unit_norm(hidden_two + dot(swished, wp_ref[...]))
    gain3 = vector(vec_ref, GAIN3)
    hidden = unit3 * gain3 + vector(vec_ref, SHIFT3)
    entry = hidden.astype(bf16)
    inner = dot(entry, wi_ref[...])
    sig = sigmoid(inner)
    active = (inner * sig).astype(bf16)
    slope = (sig * (1.0 + inner * (1.0 - sig))).astype(bf16)
    unit4, inv4 = unit_norm(hidden + dot_nt(active, wo_ref[...]))
    gain4 = vector(vec_ref, GAIN4)
    D = unit4.shape[1]
    out_ref[:, :D] = (unit4 * gain4 + vector(vec_ref, SHIFT4)).astype(bf16)
    out_ref[:, D:] = jnp.zeros((unit4.shape[0], FULL - D), bf16)
    upstream = cot_ref.value(mine_ref[0])[:, :D].astype(f32)
    grad4 = unit_norm_back(unit4, inv4, gain4, upstream)
    low4 = grad4.astype(bf16)
    add_into(sum_o, dot_tn(low4, active))
    dinner = (dot(low4, wo_ref[...]) * slope.astype(f32)).astype(bf16)
    add_into(sum_i, dot_tn(entry, dinner))
    up3 = grad4 + dot_nt(dinner, wi_ref[...])
    grad3 = unit_norm_back(unit3, inv3, gain3, up3)
    g3_ref[...] = grad3
    low3 = grad3.astype(bf16)
    add_into(sum_p, dot_tn(swished, low3))
    dnormed = dot_nt(low3, wp_ref[...]) * slope_n.astype(f32)
    dz_ref[...] = dnormed * batch_gain
    small = jnp.concatenate(
        [
            col_sum(dnormed * centred), col_sum(dnormed),
            col_sum(up3 * unit3), col_sum(up3),
            col_sum(upstream * unit4), col_sum(upstream),
            jnp.zeros((2, centred.shape[1]), f32),
        ],
        axis=0,
    )
    add_into(small_ref, small)

    @pl.when(pl.program_id(0) == pl.num_programs(0) - 1)
    def _():
        dwp_ref[...] = sum_p[...].astype(bf16)
        dwi_ref[...] = sum_i[...].astype(bf16)
        dwo_ref[...] = sum_o[...].astype(bf16)


def third_kernel(
    len_ref, gs_ref, lin_ref, sig_ref, x2_ref, r2_ref, g3_ref, u_ref, x1_ref, r1_ref, mixed_ref,
    vec_ref, wl_ref, wg_ref, wi_ref, wo_ref, wout_ref,
    g1_ref, gm_ref, small_ref, packed_ref, sum_i, sum_o, sum_l, sum_g, sum_out, *, tile, length,
):
    step = pl.program_id(0)
    clear((small_ref, sum_i, sum_o, sum_l, sum_g, sum_out))
    valid = row_valid(len_ref, step, tile, length)
    sig_g = sig_ref[...].astype(f32)
    gated = jnp.where(valid, gs_ref[...], 0.0) * sig_g
    low_l = gated.astype(bf16)
    low_g = (gated * lin_ref[...].astype(f32) * (1.0 - sig_g)).astype(bf16)
    unit2 = x2_ref[...]
    gain2 = vector(vec_ref, GAIN2)
    entry2 = (unit2 * gain2 + vector(vec_ref, SHIFT2)).astype(bf16)
    add_into(sum_l, dot_tn(low_l, entry2))
    add_into(sum_g, dot_tn(low_g, entry2))
    up2 = g3_ref[...] + dot(low_l, wl_ref[...]) + dot(low_g, wg_ref[...])
    grad2 = unit_norm_back(unit2, r2_ref[...], gain2, up2)
    low2 = grad2.astype(bf16)
    inner = u_ref[...].astype(f32)
    sig = sigmoid(inner)
    active = (inner * sig).astype(bf16)
    slope = (sig * (1.0 + inner * (1.0 - sig))).astype(bf16)
    add_into(sum_o, dot_tn(low2, active))
    dinner = (dot(low2, wo_ref[...]) * slope.astype(f32)).astype(bf16)
    unit1 = x1_ref[...]
    gain1 = vector(vec_ref, GAIN1)
    entry1 = (unit1 * gain1 + vector(vec_ref, SHIFT1)).astype(bf16)
    add_into(sum_i, dot_tn(entry1, dinner))
    up1 = grad2 + dot_nt(dinner, wi_ref[...])
    grad1 = unit_norm_back(unit1, r1_ref[...], gain1, up1)
    g1_ref[...] = grad1
    low1 = grad1.astype(bf16)
    add_into(sum_out, dot_tn(mixed_ref[...], low1))
    gm_ref[...] = dot_nt(low1, wout_ref[...]).astype(bf16)
    small = jnp.concatenate(
        [
            col_sum(up1 * unit1), col_sum(up1),
            col_sum(up2 * unit2), col_sum(up2),
            jnp.zeros((4, unit1.shape[1]), f32),
        ],
        axis=0,
    )
    add_into(small_ref, small)

    @pl.when(step == pl.num_programs(0) - 1)
    def _():
        D = unit1.shape[1]
        hs = D // HEADS
        at = 0
        for ref in (sum_i, sum_o, sum_l, sum_g):
            at = put_blocks(packed_ref, at, ref[...])
        rows = sum_l.shape[0]
        compact = jnp.zeros(sum_l.shape, f32)
        for h in range(HEADS):
            chosen = pick(rows, LANE, h * hs, 0, hs).astype(bf16)
            part = dot(chosen, sum_out[h * LANE : (h + 1) * LANE, :].astype(bf16))
            compact += jnp.concatenate(
                [part, jnp.zeros((rows, sum_l.shape[1] - D), f32)], axis=1
            )
        at = put_blocks(packed_ref, at, compact)
        if at < packed_ref.shape[0]:
            packed_ref[at:, :] = jnp.zeros((packed_ref.shape[0] - at, LANE), bf16)


def frames_kernel(*refs):
    heads = refs[:-3]
    g1_ref, back_ref, out_ref = refs[-3:]
    grads = jnp.concatenate([ref[...] for ref in heads], axis=1)
    D = g1_ref.shape[1]
    out_ref[:, :D] = (g1_ref[...] + dot(grads, back_ref[...])).astype(bf16)
    out_ref[:, D:] = jnp.zeros((out_ref.shape[0], FULL - D), bf16)


def frames_block(seq, heads, g1, back, after=(), tile=496):
    rows = heads[0].shape[0]
    per = rows // tile
    return kernel_call(
        frames_kernel, "frames_block",
        [(a, pl.BlockSpec((tile, a.shape[1]), lambda i: (i, 0))) for a in heads]
        + [(g1, pl.BlockSpec((tile, g1.shape[1]), lambda i: (seq * per + i, 0)))]
        + [(back, whole_spec(back.shape))],
        [((rows, FULL), bf16, pl.BlockSpec((tile, FULL), lambda i: (i, 0)))],
        grid=(per,), after=after, flops=3_000_000_000,
    )[0]


def pack_kernel(*refs, groups, seqs):
    d_refs = refs[:groups]
    f_ref = refs[groups]
    rest = refs[groups + 1 :]
    pos_refs, bias_refs = rest[: groups * seqs], rest[groups * seqs : 2 * groups * seqs]
    small_ref, depth_ref, packed_ref, sum_w = rest[2 * groups * seqs :]
    clear((sum_w,))
    grads = jnp.concatenate([ref[...] for ref in d_refs], axis=1)
    sum_w[...] += dot_tn(f_ref[...], grads)

    @pl.when(pl.program_id(0) == pl.num_programs(0) - 1)
    def _():
        D = small_ref.shape[1]
        wide = up(D, LANE)
        spare = jnp.zeros((16, wide - D), f32)
        at = put_blocks(packed_ref, 0, sum_w[: up(D, 16), :])
        kept = up(D // 2, 16)

        def over_seqs(items, group, take):
            total = None
            for s in range(seqs):
                value = take(items[s * groups + group])
                total = value if total is None else total + value
            return total

        for group in range(groups):
            for h in range(pos_refs[group].shape[0]):
                for half in range(2):
                    rows = slice(half * WIDE, half * WIDE + kept)
                    value = over_seqs(pos_refs, group, lambda ref: ref[h, rows, :])
                    at = put_blocks(packed_ref, at, value)
        for group in range(groups):
            for h in range(bias_refs[group].shape[0]):
                at = put_blocks(packed_ref, at, over_seqs(bias_refs, group, lambda ref: ref[h]))
        small = jnp.concatenate([small_ref[...], jnp.zeros((8, D), f32)], axis=0)
        at = put_blocks(packed_ref, at, jnp.concatenate([small, spare], axis=1))
        depth = depth_ref[...]
        spare = jnp.zeros((depth.shape[0], wide - D), f32)
        at = put_blocks(packed_ref, at, jnp.concatenate([depth, spare], axis=1))
        if at < packed_ref.shape[0]:
            packed_ref[at:, :] = jnp.zeros((packed_ref.shape[0] - at, LANE), bf16)


def middle_rows(D, F, unit):
    blocks = 2 * (up(F, LANE) // LANE) + 3 * (up(D, LANE) // LANE)
    return up(blocks * up(D, 16), unit)


def late_rows(D, taps, unit):
    blocks = up(D, LANE) // LANE
    rows = HEADS * WIDE // LANE * up(D, 16) + HEADS * (2 * up(D // 2, 16) + 16)
    return up(rows + blocks * (16 + up(taps, 16)), unit)


def unpack_kernel(
    bit_ref, value_ref, other_ref, bias_ref,
    wi1_ref, wo1_ref, glu_ref, wout_ref, q_ref, k_ref, v_ref, pos_ref, vec_ref, depth_ref, buf, *, middle, late,
):
    n = value_ref.shape[0]
    bit = bit_ref[0]
    buf[pl.ds(pl.multiple_of(bit * n, 16), n), :] = value_ref[...]
    buf[pl.ds(pl.multiple_of((1 - bit) * n, 16), n), :] = other_ref[...]
    D, F = wi1_ref.shape
    hs = D // HEADS
    half = D // 2
    at = half - LANE
    one = 3 * hs - LANE
    place = {"middle": 0, "late": 0}

    def fetch(kind, rows):
        cut = middle if kind == "middle" else late
        start = place[kind]
        place[kind] += rows
        parts = []
        while rows:
            shard, offset = divmod(start, cut)
            count = min(rows, cut - offset)
            base = shard * (middle + late) + offset + (0 if kind == "middle" else middle)
            parts.append(buf[base : base + count, :])
            start += count
            rows -= count
        return jnp.concatenate(parts, axis=0) if len(parts) > 1 else parts[0]

    def spread_blocks(ref, first, kind, rows, cols):
        for c in range(0, cols, LANE):
            width = min(LANE, cols - c)
            block = fetch(kind, up(rows, 16))[:rows, :width].astype(f32)
            ref[first : first + rows, c : c + width] = block

    spread_blocks(wi1_ref, 0, "middle", D, F)
    spread_blocks(wo1_ref, 0, "middle", D, F)
    spread_blocks(glu_ref, 0, "middle", D, D)
    spread_blocks(glu_ref, D, "middle", D, D)
    spread_blocks(wout_ref, 0, "middle", D, D)
    sums = [None, None, None]
    for h in range(HEADS):
        block = jnp.concatenate([fetch("late", up(D, 16)), fetch("late", up(D, 16))], axis=1)
        for i in range(3):
            part = dot(block, pick(WIDE, D, i * hs, h * hs, hs).astype(bf16))
            sums[i] = part if sums[i] is None else sums[i] + part
    v_ref[...] = sums[0][:D]
    q_ref[...] = sums[1][:D]
    k_ref[...] = sums[2][:D]
    halves = [None, None]
    scale = math.sqrt(hs) / LOG2E
    for h in range(HEADS):
        change = bias_ref[h, 1:2, :] - bias_ref[h, 0:1, :]
        chosen = pick(LANE, D, at, h * hs, hs)
        for i in range(2):
            raw = fetch("late", up(half, 16)).astype(f32)
            full = raw * scale + raw[:, one : one + 1] * change
            part = lax.dot_general(
                full, chosen, (((1,), (0,)), ((), ())), precision=lax.Precision.HIGHEST,
                preferred_element_type=f32,
            )
            halves[i] = part if halves[i] is None else halves[i] + part
    pos_ref[:half, :] = halves[0][:half]
    pos_ref[half:, :] = halves[1][:half]
    total = None
    for h in range(HEADS):
        part = dot(fetch("late", 16), pick(LANE, D, at, h * hs, hs).astype(bf16))
        total = part if total is None else total + part
    vec_ref[0:8, :] = total[:8]
    spread_blocks(vec_ref.at[8:16], 0, "late", 8, D)
    spread_blocks(depth_ref, 0, "late", depth_ref.shape[0], D)


def unpack(bit, value, other, bias, D, F, taps, middle, late, after):
    arrays = (value, other, bias)
    shapes = (
        (D, F), (D, F), (2 * D, D), (D, D), (D, D), (D, D), (D, D), (D, D),
        (16, D), (up(taps, 8), D),
    )
    return kernel_call(
        functools.partial(unpack_kernel, middle=middle, late=late), "unpack",
        [(bit, SCALARS)] + [(a, whole_spec(a.shape)) for a in arrays],
        [(s, f32, whole_spec(s)) for s in shapes],
        after=after, scratch=[pltpu.VMEM((2 * value.shape[0], LANE), bf16)], flops=1000,
    )


def widen_kernel(*refs):
    count = len(refs) // 2
    for source, target in zip(refs[:count], refs[count:]):
        target[...] = source[...].astype(f32)


def widen(arrays):
    return kernel_call(
        widen_kernel, "widen", [(a, whole_spec(a.shape)) for a in arrays],
        [(a.shape, f32, whole_spec(a.shape)) for a in arrays], flops=1000,
    )


class Rows:
    def __init__(self, refs, per):
        self.refs, self.per, self.shape = refs, per, refs[0].shape

    def __getitem__(self, _):
        step = pl.program_id(0)
        value = self.refs[0][...]
        for u in range(1, len(self.refs)):
            value = jnp.where(step >= u * self.per, self.refs[u][...], value)
        return value


class Shifts(list):
    def __init__(self, arrays, rows):
        super().__init__(arrays)
        self.rows = rows


class Places:
    def __init__(self, refs, per, rows):
        self.refs, self.per, self.rows = refs, per, rows

    def value(self, mine):
        step = pl.program_id(0)
        parts = len(self.refs)
        count = parts // self.per
        found = []
        for k in range(count):
            place = lax.rem(step, self.per) * count + k
            chosen = None
            for u in range(self.refs[0].shape[0] // self.rows):
                rows = slice(u * self.rows, (u + 1) * self.rows)
                here = at_place(mine, place, [ref[rows, :] for ref in self.refs])
                chosen = here if chosen is None else jnp.where(step >= u * self.per, here, chosen)
            found.append(chosen)
        return jnp.concatenate(found, axis=0) if count > 1 else found[0]


def row_call(kernel, name, rows, tile, scalars, tiled, fixed, tiled_out, fixed_out, after=(), scratch=(), flops=0):
    def block(width):
        return pl.BlockSpec((tile, width), lambda i: (i, 0))

    operands = [(a, SCALARS) for a in scalars]
    wraps = []
    for a in tiled:
        start = len(operands)
        if isinstance(a, list):
            count = a.rows
            per = len(a) * count // tile
            operands += [(p, whole_spec(p.shape)) for p in a]
            wraps.append((start, len(operands), lambda r, n=per, k=count: Places(r, n, k)))
        elif isinstance(a, tuple):
            per = a[0].shape[0] // tile
            for u, array in enumerate(a):
                spec = pl.BlockSpec(
                    (tile, array.shape[1]), lambda i, u=u: (jnp.clip(i - u * per, 0, per - 1), 0)
                )
                operands.append((array, spec))
            wraps.append((start, len(operands), lambda r, n=per: Rows(r, n)))
        else:
            operands.append((a, block(a.shape[1])))
            wraps.append((start, start + 1, lambda r: r[0]))
    first = len(scalars)
    last = len(operands)

    def body(*refs):
        kernel(*refs[:first], *[wrap(refs[i:j]) for i, j, wrap in wraps], *refs[last:])

    return kernel_call(
        body, name,
        operands + [(a, whole_spec(a.shape)) for a in fixed],
        [((rows, w), d, block(w)) for w, d in tiled_out]
        + [(s, k, whole_spec(s)) for s, k in fixed_out],
        grid=(rows // tile,),
        after=after,
        scratch=[pltpu.VMEM(s, f32) for s in scratch],
        flops=flops,
    )


def first_block(lens, length, tiled, fixed, tile=496):
    D, F = fixed[2].shape
    rows = len(tiled[0]) * length
    return row_call(
        functools.partial(first_kernel, tile=tile, length=length), "first_block", rows, tile,
        (lens,), tiled, fixed,
        ((D, f32), (1, f32), (F, bf16), (D, f32), (1, f32), (D, bf16), (D, bf16), (D, bf16)), (),
        flops=15_000_000_000,
    )


def second_block(mine, tiled, fixed, tile=496):
    rows, D = tiled[0].shape
    F = fixed[3].shape[1]
    return row_call(
        second_kernel, "second_block", rows, tile, (mine,), tiled, fixed,
        ((FULL, bf16), (D, f32), (D, f32)),
        (((8, D), f32), ((D, D), bf16), ((D, F), bf16), ((D, F), bf16)),
        scratch=((D, D), (D, F), (D, F)),
        flops=30_000_000_000,
    )


def third_block(lens, length, unit, tiled, fixed, after, tile=496):
    rows, D = tiled[0].shape
    M = tiled[-1][0].shape[1]
    F = fixed[3].shape[1]
    tall, wide, square = up(D, 16), up(F, LANE), up(D, LANE)
    return row_call(
        functools.partial(third_kernel, tile=tile, length=length), "third_block", rows, tile,
        (lens,), tiled, fixed, ((D, f32), (M, bf16)),
        (((8, D), f32), ((middle_rows(D, F, unit), LANE), bf16)),
        scratch=((tall, wide), (tall, wide), (tall, square), (tall, square), (M, D)),
        after=after, flops=30_000_000_000,
    )


def pack_block(unit, groups, whole, pos, bias, small, depth, taps, after, tile=496):
    seqs = len(whole)
    D = small.shape[1]
    rows = seqs * whole[0].shape[0]
    width = sum(g[0].shape[1] for g in groups)
    return row_call(
        functools.partial(pack_kernel, groups=len(groups), seqs=seqs), "pack_block", rows, tile,
        (), (*groups, whole), (*pos, *bias, small, depth),
        (), (((late_rows(D, taps, unit), LANE), bf16),),
        scratch=((FULL, width),), after=after, flops=5_000_000_000,
    )[0]


def swap_pairs(size, distance):
    return [(i, i ^ distance) for i in range(size)]


def axis_steps(axis, first=1):
    size = lax.axis_size(axis)
    steps = []
    distance = first
    while distance < size:
        steps.append((axis, size, distance))
        distance *= 2
    return steps


def butterfly_sum(value):
    for axis, size, distance in axis_steps("batch") + axis_steps("tm"):
        value = value + lax.ppermute(value, axis, swap_pairs(size, distance))
    return value


def scatter_step(value, step):
    axis, size, distance = step
    bit = (lax.axis_index(axis) // distance) % 2
    half = value.shape[0] // 2
    sent = lax.dynamic_slice_in_dim(value, (1 - bit) * half, half, 0).astype(bf16)
    kept = lax.dynamic_slice_in_dim(value, bit * half, half, 0).astype(f32)
    got = lax.ppermute(sent, axis, swap_pairs(size, distance))
    return kept + got.astype(f32), got


def gather_step(value, step):
    axis, size, distance = step
    bit = (lax.axis_index(axis) // distance) % 2
    other = lax.ppermute(value, axis, swap_pairs(size, distance))
    return jnp.concatenate(
        [jnp.where(bit == 0, value, other), jnp.where(bit == 0, other, value)]
    )


def ring_plan():
    batch = axis_steps("batch")
    return batch[:1], batch[1:2], axis_steps("tm"), batch[2:]


def exchange_sum(value, step):
    axis, size, distance = step
    low = value.astype(bf16)
    got = lax.ppermute(low, axis, swap_pairs(size, distance))
    return low.astype(f32) + got.astype(f32), got


def scatter_sum(value, after=(), split=False):
    core, across, tm, rest = ring_plan()
    arrived = []
    for step in core:
        value, got = scatter_step(value, step)
        arrived.append([got])
    half = value.shape[0] // 2
    streams = [value[:half], value[half:]]
    for steps in zip(across + tm, tm + across):
        pair = [scatter_step(v, s) for v, s in zip(streams, steps)]
        streams = [p[0] for p in pair]
        arrived.append([p[1] for p in pair])
    value = jnp.concatenate(streams)
    if split:
        for step in rest:
            value, got = scatter_step(value, step)
            arrived.append([got])
        value = value.astype(bf16)
        for step in rest[::-1]:
            value = gather_step(value, step)
        return value, arrived
    for index, step in enumerate(rest):
        if after and index == len(rest) - 1:
            value = hold(value, after)
        value, got = exchange_sum(value, step)
        arrived.append([got])
    return value.astype(bf16), arrived


def merge_kernel(bits_ref, *refs, joined):
    count = bits_ref.shape[0]
    out_refs = refs[2 * count :]
    at = 0
    for i in range(count):
        value, other = refs[i], refs[count + i]
        rows = value.shape[0]
        out_ref = out_refs[0] if joined else out_refs[i]
        for ref, place in ((value, bits_ref[i]), (other, 1 - bits_ref[i])):
            out_ref[pl.ds(pl.multiple_of(at + place * rows, 16), rows), :] = ref[...]
        at += 2 * rows if joined else 0


def merge(bits, values, others, joined, after):
    arrays = list(values) + list(others)
    shapes = [(2 * v.shape[0], LANE) for v in values]
    if joined:
        shapes = [(sum(s[0] for s in shapes), LANE)]
    return kernel_call(
        functools.partial(merge_kernel, joined=joined), "merge",
        [(jnp.stack(bits).astype(jnp.int32), SCALARS)]
        + [(a, whole_spec(a.shape)) for a in arrays],
        [(s, bf16, whole_spec(s)) for s in shapes], after=after, flops=1000,
    )


def gather_all(streams, after):
    core, across, tm, _ = ring_plan()
    stages = list(zip(across + tm, tm + across))[::-1]
    for index, steps in enumerate(stages):
        last = index == len(stages) - 1
        bits = [(lax.axis_index(a) // d) % 2 for a, _, d in steps]
        others = [lax.ppermute(v, a, swap_pairs(n, d)) for v, (a, n, d) in zip(streams, steps)]
        streams = merge(bits, streams, others, last, after if last else ())
    value = streams[0]
    axis, size, distance = core[0]
    bit = (lax.axis_index(axis) // distance) % 2
    return bit, value, lax.ppermute(value, axis, swap_pairs(size, distance))


def scatter_parts():
    core, across, tm, rest = ring_plan()
    return 2 ** (len(core) + 1 + len(across) + len(tm))


def hold_kernel(a_ref, out_ref):
    out_ref[...] = a_ref[...]


def hold(value, after):
    spec = whole_spec(value.shape)
    return kernel_call(
        hold_kernel, "hold", [(value, spec)], [(value.shape, value.dtype, spec)], after=after,
        flops=1000,
    )[0]


def join_kernel(a_ref, b_ref, first_ref, second_ref):
    a, b = a_ref.shape[0] // 2, b_ref.shape[0] // 2
    for i, ref in enumerate((first_ref, second_ref)):
        ref[:a, :] = a_ref[i * a : (i + 1) * a, :]
        ref[a:, :] = b_ref[i * b : (i + 1) * b, :]


def join_shards(a, b, after):
    shape = ((a.shape[0] + b.shape[0]) // 2, LANE)
    return kernel_call(
        join_kernel, "join_shards", [(x, whole_spec(x.shape)) for x in (a, b)],
        [(shape, a.dtype, whole_spec(shape))] * 2, after=after, flops=1000,
    )


def rotation(size, shift):
    return [(i, (i + shift) % size) for i in range(size)]


def assemble_kernel(mine_ref, *refs, parts, own, pieces):
    out_ref = refs[-1]
    D, _, rows = out_ref.shape
    mine = mine_ref[0]
    base = pl.multiple_of(mine * rows, 8)
    for u in range(own):
        here = [refs[u][pl.ds(base, rows), :]]
        here += [refs[own + i][at : at + rows, :] for i, at in pieces[u]]
        for place in range(parts):
            value = at_place(mine, place, here)[:, :D].astype(f32)
            out_ref[:, place * own + u, :] = jnp.transpose(value).astype(bf16)


def assemble(whole, groups, mine, D, after=()):
    own = len(whole)
    parts = lax.axis_size("tm")
    rows = whole[0].shape[0] // parts
    arrays = []
    pieces = {}
    for seqs, by_shift in groups:
        for index, u in enumerate(seqs):
            pieces[u] = [(len(arrays) + k, index * rows) for k in range(parts - 1)]
        arrays += by_shift
    operands = list(whole) + arrays
    shape = (D, parts * own, rows)
    return kernel_call(
        functools.partial(assemble_kernel, parts=parts, own=own, pieces=pieces), "assemble",
        [(mine, SCALARS)] + [(a, whole_spec(a.shape)) for a in operands],
        [(shape, bf16, whole_spec(shape))], after=after, flops=1000, vmem=MOST,
    )[0]


def send_pieces(pieces):
    return [
        lax.ppermute(p, "tm", rotation(len(pieces), shift)) if shift else p
        for shift, p in enumerate(pieces)
    ]


def send_frames(whole, mine):
    parts = lax.axis_size("tm")
    rows = whole[0].shape[0] // parts
    pieces = []
    for shift in range(1, parts):
        at = lax.rem(mine + shift, parts) * rows
        piece = jnp.concatenate([lax.dynamic_slice_in_dim(w, at, rows, 0) for w in whole])
        pieces.append(lax.ppermute(piece, "tm", rotation(parts, shift)))
    return pieces


def on_device(
    frames,
    lengths,
    cotangent,
    query_weight,
    key_weight,
    value_weight,
    position_weight,
    content_bias,
    position_bias,
    output_weight,
    attend_gain,
    attend_shift,
    inner_first,
    outer_first,
    first_gain,
    first_shift,
    glu_weight,
    depth_weight,
    batch_gain,
    batch_shift,
    point_weight,
    conv_gain,
    conv_shift,
    inner_second,
    outer_second,
    second_gain,
    second_shift,
):
    seq_local, local_rows, D = frames.shape
    H = HEADS
    hs = D // H
    F = inner_first.shape[1]
    taps = depth_weight.shape[0]
    half = D // 2
    at = half - LANE
    parts = lax.axis_size("tm")
    mine = lax.axis_index("tm")
    unit = 16 * scatter_parts()
    U = seq_local // parts
    T = local_rows * parts
    R = U * T
    lens = lax.dynamic_slice_in_dim(lengths, mine * U, U)

    place = mine.astype(jnp.int32).reshape(1)
    pieces = []
    for u in range(U):
        earlier = tuple(pieces[-1][1:]) if pieces else ()
        pieces.append(send_pieces(split_frames(frames, place, (u,), after=earlier)))
    zero = jnp.zeros((D,), f32)
    vec = jnp.stack(
        [
            content_bias, position_bias, attend_gain, attend_shift, first_gain, first_shift,
            batch_gain, batch_shift, conv_gain, conv_shift, second_gain, second_shift,
            zero, zero, zero, zero,
        ]
    )
    outer_first_t, outer_second_t = outer_first.T, outer_second.T
    (
        query_x, kv_x, pos_x, output_x, bias_x, back_x, lin_t, gate_t,
        sines, cosines, sines_low, sines_t, cosines_t,
    ) = prepare(
        T, vec, query_weight, key_weight, value_weight, position_weight, output_weight, glu_weight.T
    )

    attended = [
        attend_forward(
            u, hs, lens, place, pieces[u],
            query_x, kv_x, pos_x, bias_x, sines, cosines, sines_low,
        )
        for u in range(U)
    ]
    mixed = tuple(a[0] for a in attended)
    whole = tuple(a[5] for a in attended)
    upstream = Shifts(
        send_pieces(split_frames(cotangent, place, tuple(range(U)), after=mixed[-1:])), local_rows
    )
    unit_one, inv_one, inner_one, unit_two, inv_two, linear, sigma, spread = first_block(
        lens, T, (whole, mixed),
        (vec, output_x, inner_first, outer_first_t, lin_t, gate_t),
    )
    spread = spread.reshape(U, T, D)
    conv_out, stat = conv_forward(lens, spread, depth_weight)
    stat = butterfly_sum(stat)
    block_out, grad_centred, grad_three, sums, grad_point, grad_inner_two, grad_outer_two = (
        second_block(
            place, (unit_two, conv_out.reshape(R, D), upstream),
            (stat, vec, point_weight, inner_second, outer_second_t),
        )
    )
    early = lax.psum((grad_inner_two, grad_outer_two, grad_point), ("batch", "tm"))
    block_out = [block_out[u * T : (u + 1) * T] for u in range(U)]
    out_pieces = send_frames(block_out, mine)
    sums = butterfly_sum(sums)
    def backward(stat, sums, grad_centred, grad_three):
        grad_spread, grad_depth = conv_backward(
            lens, spread, grad_centred.reshape(U, T, D), conv_out, depth_weight, stat, sums, vec, BGAIN
        )
        grad_one, grad_mixed, small_one, middle = (
            third_block(
                lens, T, unit,
                (
                    grad_spread.reshape(R, D), linear, sigma, unit_two, inv_two, grad_three,
                    inner_one, unit_one, inv_one, mixed,
                ),
                (vec, lin_t, gate_t, inner_first, outer_first_t, output_x),
                after=tuple(out_pieces),
            )
        )
        middle_shard, arrived = scatter_sum(middle, split=True)
        waits = iter([()] + arrived)
        groups = 2
        count = H // groups
        back, frames_grad, grad_pieces = [], [], []
        for u in range(U):
            for g in range(groups):
                back.append(
                    attend_backward(
                        u, hs, g * count, count, *attended[u][1:5], grad_mixed, mixed[u], pos_x,
                        sines_low, sines_t, cosines_t, after=tuple(next(waits, ())) + tuple(b[2] for b in back[-1:]),
                        vmem=VMEM if back else MOST,
                    )
                )
            if u < U - 1:
                frames_grad.append(
                    frames_block(u, [b[0] for b in back[-groups:]], grad_one, back_x)
                )
                grad_pieces.append(send_frames(frames_grad[-1:], mine))
        earlier = tuple(p for row in grad_pieces for p in row)
        late = pack_block(
            unit, [tuple(b[0] for b in back[g::groups]) for g in range(groups)], whole,
            [b[1] for b in back], [b[2] for b in back], small_one, grad_depth, taps,
            after=tuple(next(waits, ())) + earlier,
        )
        block_raw = assemble(block_out, [(range(U), out_pieces)], place, D, after=(late,))
        late_shard, arrived = scatter_sum(late, after=(block_raw,))
        frames_grad.append(
            frames_block(
                U - 1, [b[0] for b in back[-groups:]], grad_one, back_x, after=tuple(arrived[1])
            )
        )
        grad_pieces.append(send_frames(frames_grad[-1:], mine))
        return block_raw, frames_grad, grad_pieces, middle_shard, late_shard

    shapes = jax.eval_shape(backward, stat, sums, grad_centred, grad_three)
    block_out, frames_grad, grad_pieces, middle_shard, late_shard = lax.cond(
        stat[2, 0] > 0.0,
        backward,
        lambda *_: jax.tree.map(lambda s: jnp.zeros(s.shape, s.dtype), shapes),
        stat, sums, grad_centred, grad_three,
    )
    frames_grad = assemble(
        frames_grad, [((u,), p) for u, p in enumerate(grad_pieces)], place, D
    )
    cuts = [s.shape[0] // 2 for s in (middle_shard, late_shard)]
    grad_inner_two, grad_outer_two, grad_point = widen(early)
    bit, value, other = gather_all(
        join_shards(middle_shard, late_shard, early[2:]), after=(frames_grad, grad_point)
    )
    (
        grad_inner_one, grad_outer_one, grad_glu, grad_output, grad_query, grad_key, grad_value, grad_position, small, grad_depth,
    ) = unpack(
        bit.astype(jnp.int32).reshape(1), value, other, bias_x, D, F, taps, *cuts, after=()
    )
    return (
        jnp.transpose(block_out, (1, 2, 0)),
        jnp.transpose(frames_grad, (1, 2, 0)),
        grad_query,
        grad_key,
        grad_value,
        grad_position,
        small[0],
        small[1],
        grad_output,
        small[8],
        small[9],
        grad_inner_one,
        grad_outer_one.T,
        small[10],
        small[11],
        grad_glu.T,
        grad_depth[:taps],
        sums[0],
        sums[1],
        grad_point,
        sums[2],
        sums[3],
        grad_inner_two,
        grad_outer_two.T,
        sums[4],
        sums[5],
    )


def solution(mesh):
    split = P("batch", "tm", None)
    return jax.shard_map(
        on_device,
        mesh=mesh,
        in_specs=(split, P("batch"), split) + (P(),) * 24,
        out_specs=(split, split) + (P(),) * 24,
        check_vma=False,
    )
```

```python
import functools
import math

import jax
import jax.numpy as jnp
from jax import lax
from jax.experimental import pallas as pl
from jax.experimental.pallas import tpu as pltpu
from jax.sharding import PartitionSpec as P

HEADS = 4
EPSILON = 1e-05
MASKED = -1e30
PAD = 16
LOG2E = 1.4426950408889634
LN2 = 0.6931471805599453
LANE = 128
WIDE = 256
FULL = 384
VMEM = 28 * 1024 * 1024
MOST = 56 * 1024 * 1024
bf16 = jnp.bfloat16
f32 = jnp.float32


def dot(a, b):
    return jnp.dot(a, b, preferred_element_type=f32)


def dot_nt(a, b):
    return lax.dot_general(a, b, (((1,), (1,)), ((), ())), preferred_element_type=f32)


def dot_tn(a, b):
    return lax.dot_general(a, b, (((0,), (0,)), ((), ())), preferred_element_type=f32)


def lanes(shape):
    return lax.broadcasted_iota(jnp.int32, shape, 1)


def sublanes(shape):
    return lax.broadcasted_iota(jnp.int32, shape, 0)


def kernel_call(kernel, name, operands, out, grid=(1,), after=(), scratch=(), flops=0, vmem=VMEM):
    count = len(operands)
    extra = len(after)

    def body(*refs):
        kernel(*refs[:count], *refs[count + extra :])

    return pl.pallas_call(
        body,
        grid=grid,
        in_specs=[spec for _, spec in operands] + [pl.BlockSpec(memory_space=pl.ANY)] * extra,
        out_specs=[spec for _, _, spec in out],
        out_shape=[jax.ShapeDtypeStruct(shape, kind) for shape, kind, _ in out],
        scratch_shapes=list(scratch),
        compiler_params=pltpu.CompilerParams(
            vmem_limit_bytes=vmem, dimension_semantics=("arbitrary",) * len(grid)
        ),
        cost_estimate=pl.CostEstimate(flops=flops, bytes_accessed=1000000, transcendentals=0)
        if flops
        else None,
        name=name,
    )(*[array for array, _ in operands], *after)


def whole_spec(shape):
    return pl.BlockSpec(tuple(shape), lambda *_: (0,) * len(shape))


SCALARS = pl.BlockSpec(memory_space=pltpu.SMEM)


def split_kernel(mine_ref, x_ref, *out_refs, parts, own, seqs):
    mine = mine_ref[0]
    D = x_ref.shape[0]
    for place in range(parts):
        shift = lax.rem(place - mine + parts, parts)
        for i, u in enumerate(seqs):
            rows = jnp.transpose(x_ref[:, place * own + u, :].astype(f32)).astype(bf16)
            spare = jnp.zeros((rows.shape[0], FULL - D), bf16)
            rows = jnp.concatenate([rows, spare], axis=1)
            for k in range(parts):

                @pl.when(shift == k)
                def _():
                    out_refs[k][i * rows.shape[0] : (i + 1) * rows.shape[0], :] = rows


def split_frames(frames, mine, seqs, after=()):
    count, rows, D = frames.shape
    parts = lax.axis_size("tm")
    across = jnp.transpose(frames, (2, 0, 1))
    pieces = kernel_call(
        functools.partial(split_kernel, parts=parts, own=count // parts, seqs=seqs),
        "split_frames",
        [(mine, SCALARS), (across, whole_spec(across.shape))],
        [((len(seqs) * rows, FULL), bf16, whole_spec((len(seqs) * rows, FULL)))] * parts,
        after=after, flops=3_000_000_000,
    )
    return pieces


def at_place(mine, place, pieces):
    parts = len(pieces)
    shift = lax.rem(mine - place + parts, parts)
    chosen = pieces[0]
    for k in range(1, parts):
        chosen = jnp.where(shift == k, pieces[k], chosen)
    return chosen


def pick(rows, cols, start, at, size):
    row, col = sublanes((rows, cols)), lanes((rows, cols))
    return jnp.where((row - start == col - at) & (row >= start) & (row < start + size), 1.0, 0.0)


def prepare_kernel(
    vec_ref, wq_ref, wk_ref, wv_ref, wp_ref, wout_ref, glu_ref,
    q_ref, kv_ref, pos_ref, out_ref, bias_ref, back_ref, lin_ref, gate_ref,
    sin_ref, cos_ref, low_ref, sin_t_ref, cos_t_ref, *, length,
):
    D = wq_ref.shape[0]
    hs = D // HEADS
    half = D // 2
    at = half - LANE
    wq, wk, wv = wq_ref[...], wk_ref[...], wv_ref[...]
    vec = vec_ref[...]
    feature = sublanes((2 * WIDE, D))
    column = lanes((2 * WIDE, D))
    spread_rows = jnp.where(
        ((feature == column) & (column < half))
        | ((feature - WIDE == column - half) & (column >= half)),
        1.0, 0.0,
    ).astype(bf16)
    pos = dot(spread_rows, wp_ref[...]).astype(bf16)
    for h in range(HEADS):
        mid = pick(D, LANE, h * hs, at, hs)
        low = mid.astype(bf16)
        first = pick(D, LANE, h * hs, 0, hs).astype(bf16)
        spare = jnp.zeros((FULL - D, LANE), f32)
        q_ref[h] = jnp.concatenate([dot(wq, low), spare], axis=0).astype(bf16)
        kv_ref[h, :, :LANE] = jnp.concatenate([dot(wk, low), spare], axis=0).astype(bf16)
        kv_ref[h, :, LANE:] = jnp.concatenate([dot(wv, first), spare], axis=0).astype(bf16)
        mid_t = pick(LANE, D, at, h * hs, hs).astype(bf16)
        pos_ref[h] = dot_nt(mid_t, pos).astype(bf16)
        bias_ref[h] = lax.dot_general(
            vec, mid, (((1,), (0,)), ((), ())), precision=lax.Precision.HIGHEST,
            preferred_element_type=f32,
        )
        out_ref[h * LANE : (h + 1) * LANE, :] = dot(
            pick(LANE, D, 0, h * hs, hs).astype(bf16), wout_ref[...]
        ).astype(bf16)
        back = None
        for i, w in enumerate((wv, wq, wk)):
            part = dot_nt(pick(WIDE, D, i * hs, h * hs, hs).astype(bf16), w)
            back = part if back is None else back + part
        back_ref[h * WIDE : (h + 1) * WIDE, :] = back.astype(bf16)
    lin_ref[...] = glu_ref[:D, :]
    gate_ref[...] = glu_ref[D:, :]

    rate = -2.0 * math.log(10000.0) / D

    def waves(position, index):
        angle = position.astype(f32) * jnp.exp(index.astype(f32) * rate)
        inside = index < half
        return jnp.where(inside, jnp.sin(angle), 0.0), jnp.where(inside, jnp.cos(angle), 0.0)

    shape = (32, WIDE)
    base_s, base_c = waves(sublanes(shape), lanes(shape))
    step_s, step_c = waves(sublanes(shape) * 32, lanes(shape))
    for i in range(length // 32):
        s, c = step_s[i : i + 1], step_c[i : i + 1]
        rows = pl.ds(i * 32, 32)
        sine = s * base_c + c * base_s
        sin_ref[rows, :] = sine
        cos_ref[rows, :] = c * base_c - s * base_s
        low_ref[rows, :] = sine.astype(bf16)
    shape = (WIDE, LANE)
    base_s, base_c = waves(lanes(shape), sublanes(shape))
    step_s, step_c = waves(lanes(shape) * LANE, sublanes(shape))
    for i in range(-(-length // LANE)):
        s, c = step_s[:, i : i + 1], step_c[:, i : i + 1]
        width = min(LANE, length - i * LANE)
        sine = (s * base_c + c * base_s).astype(bf16)
        cosine = (c * base_c - s * base_s).astype(bf16)
        sin_t_ref[:, i * LANE : i * LANE + width] = sine[:, :width]
        cos_t_ref[:, i * LANE : i * LANE + width] = cosine[:, :width]


def prepare(length, vec, wq, wk, wv, wp, wout, glu):
    D = wq.shape[0]
    arrays = (vec, wq, wk, wv, wp, wout, glu)
    shapes = (
        ((HEADS, FULL, LANE), bf16), ((HEADS, FULL, WIDE), bf16), ((HEADS, LANE, 2 * WIDE), bf16),
        ((HEADS * LANE, D), bf16), ((HEADS,) + vec.shape[:1] + (LANE,), f32),
        ((HEADS * WIDE, D), bf16), ((D, D), bf16), ((D, D), bf16),
        ((length, WIDE), f32), ((length, WIDE), f32), ((length, WIDE), bf16),
        ((WIDE, length), bf16), ((WIDE, length), bf16),
    )
    return kernel_call(
        functools.partial(prepare_kernel, length=length), "prepare",
        [(a, whole_spec(a.shape)) for a in arrays],
        [(s, k, whole_spec(s)) for s, k in shapes],
        flops=5_000_000_000, vmem=MOST,
    )


def attend_forward_kernel(
    len_ref, mine_ref, *refs, parts, seq, hs, tile,
):
    pieces = refs[:parts]
    q_ref, kv_ref, pos_ref, bias_ref, sin_ref, cos_ref, low_ref = refs[parts : parts + 7]
    mixed_ref, qa_ref, qb_ref, ka_ref, v_ref, f_ref = refs[parts + 7 :]
    T = f_ref.shape[0]
    count = pieces[0].shape[0]

    @pl.when(pl.program_id(0) == 0)
    def _():
        for place in range(parts):
            f_ref[place * count : (place + 1) * count, :] = at_place(
                mine_ref[0], place, [p[...] for p in pieces]
            )

    one = 3 * hs - LANE
    scale = LOG2E / math.sqrt(hs)
    valid = len_ref[seq]
    lane = lanes((tile, LANE))

    def key_rows(h, r0):
        rows = pl.ds(r0, tile)
        kv = dot(f_ref[rows, :], kv_ref[h])
        k = kv[:, :LANE] + cos_ref[rows, LANE:]
        row = sublanes((tile, LANE)) + r0
        k = jnp.where(lane == one, jnp.where(row < valid, 0.0, MASKED), k)
        k = jnp.where((lane > one) & (lane < one + 4), 1.0, k)
        ka_ref[h, rows, :LANE] = cos_ref[rows, :LANE].astype(bf16)
        ka_ref[h, rows, LANE:] = k.astype(bf16)
        v = jnp.where((lane == hs) | (lane == hs + 1), 1.0, kv[:, LANE:])
        v_ref[h, rows, :] = v.astype(bf16)

    def score_rows(h, r0):
        rows = pl.ds(r0, tile)
        q = dot(f_ref[rows, :], q_ref[h])
        e = dot((q + bias_ref[h, 1:2, :]).astype(bf16), pos_ref[h])
        es, ec = e[:, :WIDE], e[:, WIDE:]
        s, c = sin_ref[rows, :], cos_ref[rows, :]
        qb = ((ec * s - es * c) * scale).astype(bf16)
        qb_ref[h, rows, :] = qb
        a = (es * s + ec * c) * scale
        first = a[:, :LANE].astype(bf16)
        second = jnp.where(lane == one, 1.0, a[:, LANE:] + (q + bias_ref[h, 0:1, :]) * scale)
        second = second.astype(bf16)
        qa_ref[h, rows, :LANE] = first
        qa = jnp.concatenate([first, second], axis=1)
        return second, dot_nt(qa, ka_ref[h]) + dot_nt(qb, low_ref[...])

    def mix_rows(h, r0, second, scores):
        rows = pl.ds(r0, tile)
        peak = jnp.max(scores, axis=1, keepdims=True)
        p = jnp.exp2(scores - peak).astype(bf16)
        o = dot(p, v_ref[h])
        total = o[:, hs : hs + 1]
        mixed_ref[rows, h * LANE : (h + 1) * LANE] = (o / total).astype(bf16)
        log_total = -(peak + jnp.log2(total))
        hi = log_total.astype(bf16).astype(f32)
        mid = (log_total - hi).astype(bf16).astype(f32)
        rest = jnp.where(lane == one + 1, hi, jnp.where(lane == one + 2, mid, log_total - hi - mid))
        second = jnp.where((lane > one) & (lane < one + 4), rest, second.astype(f32))
        qa_ref[h, rows, LANE:] = second.astype(bf16)

    tasks = [(h, r0) for h in range(q_ref.shape[0]) for r0 in range(0, T, tile)]
    for task in tasks:
        key_rows(*task)
    waiting = None
    for task in tasks:
        current = (*task, *score_rows(*task))
        if waiting is not None:
            mix_rows(*waiting)
        waiting = current
    mix_rows(*waiting)


def attend_forward(seq, head_size, lens, mine, pieces, q, kv, pos, bias, sines, cosines, low, tile=496):
    T = sines.shape[0]
    H = q.shape[0]
    group = 2

    def head(shape):
        return pl.BlockSpec((group,) + shape[1:], lambda h: (h, 0, 0))

    def three(width):
        return ((H, T, width), bf16, pl.BlockSpec((group, T, width), lambda h: (h, 0, 0)))

    return kernel_call(
        functools.partial(
            attend_forward_kernel, parts=len(pieces), seq=seq, hs=head_size, tile=tile
        ),
        "attend_forward",
        [(lens, SCALARS), (mine, SCALARS)]
        + [(p, whole_spec(p.shape)) for p in pieces]
        + [(a, head(a.shape)) for a in (q, kv, pos, bias)]
        + [(a, whole_spec(a.shape)) for a in (sines, cosines, low)],
        [((T, H * LANE), bf16, pl.BlockSpec((T, group * LANE), lambda h: (0, h)))]
        + [three(w) for w in (WIDE, WIDE, WIDE, LANE)]
        + [((T, FULL), bf16, whole_spec((T, FULL)))],
        grid=(H // group,),
        flops=15_000_000_000, vmem=40 * 1024 * 1024,
    )


def attend_backward_kernel(
    qa_ref, qb_ref, ka_ref, v_ref, do_ref, mixed_ref, pos_ref, low_ref, sin_ref, cos_ref,
    d_ref, dpos_ref, bias_ref, *, hs, tile,
):
    T = qa_ref.shape[1]
    at = 2 * hs - LANE
    inv = 1.0 / math.sqrt(hs)
    do = do_ref[...]
    wide = do.astype(f32)
    delta = -jnp.sum(wide * mixed_ref[...].astype(f32), axis=1, keepdims=True)
    hi = delta.astype(bf16).astype(f32)
    lane = lanes((T, LANE))
    dox = jnp.where(lane == hs, hi, jnp.where(lane == hs + 1, delta - hi, wide)).astype(bf16)
    qa = qa_ref[0]
    qb = qb_ref[0]
    da = db = None
    parts = []
    for r0 in range(0, T, tile):
        rows = pl.ds(r0, tile)
        ka = ka_ref[0, rows, :]
        low = low_ref[rows, :]
        p = jnp.exp2(dot_nt(ka, qa) + dot_nt(low, qb))
        ds = (p * dot_nt(v_ref[0, rows, :], dox)).astype(bf16)
        dv = dot(p.astype(bf16), do)
        dk = dot(ds, qa[:, LANE:])
        a, b = dot_tn(ka, ds), dot_tn(low, ds)
        da = a if da is None else da + a
        db = b if db is None else db + b
        parts.append((dv, dk))
    s, c = sin_ref[...].astype(f32), cos_ref[...].astype(f32)
    des = (da * s - db * c) * inv
    dec = (da * c + db * s) * inv
    de = jnp.concatenate([des.astype(bf16), dec.astype(bf16)], axis=0)
    dqp = dot(pos_ref[0], de)
    dpos = dot(de, qa[:, LANE:])
    sub = sublanes((LANE, T))
    dqc = jnp.where((sub >= at) & (sub < at + hs), da[LANE:] * inv, 0.0)
    ones = jnp.ones((16, T), bf16)
    bias = jnp.where(
        sublanes((16, LANE)) == 0, dot_nt(ones, dqc.astype(bf16)), dot_nt(ones, dqp.astype(bf16))
    )

    dpos_ref[0] = dpos
    bias_ref[0] = bias
    dq = jnp.transpose(dqc + dqp)
    dq = pltpu.roll(jnp.concatenate([jnp.zeros((T, LANE), f32), dq], axis=1), WIDE - hs, 1)
    lane = lanes((tile, LANE))
    for i, (dv, dk) in enumerate(parts):
        rows = pl.ds(i * tile, tile)
        dq_rows = dq[i * tile : (i + 1) * tile]
        d_ref[rows, :LANE] = jnp.where(lane < hs, dv, dq_rows[:, :LANE]).astype(bf16)
        inside = (lane >= at) & (lane < at + hs)
        d_ref[rows, LANE:] = jnp.where(inside, dk * LN2, dq_rows[:, LANE:]).astype(bf16)


def attend_backward(
    seq, head_size, first, count, qa, qb, ka, v, do, mixed, pos, low, sin_t, cos_t, after, vmem=VMEM, tile=496,
):
    H, T, W = qa.shape

    def three(array):
        return array, pl.BlockSpec((1,) + array.shape[1:], lambda h: (first + h, 0, 0))

    def lane_block(array, u):
        return array, pl.BlockSpec((T, LANE), lambda h: (u, first + h))

    return kernel_call(
        functools.partial(attend_backward_kernel, hs=head_size, tile=tile), "attend_backward",
        [three(qa), three(qb), three(ka), three(v), lane_block(do, seq), lane_block(mixed, 0)]
        + [three(pos)]
        + [(a, whole_spec(a.shape)) for a in (low, sin_t, cos_t)],
        [
            ((T, count * W), bf16, pl.BlockSpec((T, W), lambda h: (0, h))),
            ((count, 2 * W, LANE), f32, pl.BlockSpec((1, 2 * W, LANE), lambda h: (h, 0, 0))),
            ((count, 16, LANE), f32, pl.BlockSpec((1, 16, LANE), lambda h: (h, 0, 0))),
        ],
        grid=(count,),
        after=after, vmem=vmem,
        flops=count * 5_500_000_000,
    )


def fill_padded(buf, value):
    T = value.shape[0]
    zero = jnp.zeros((PAD, buf.shape[1]), f32)
    buf[0:PAD, :] = zero
    buf[T + PAD : T + 2 * PAD, :] = zero
    buf[PAD : T + PAD, :] = value


def fill_weights(wide, w_ref, taps):
    for o in range(taps):
        wide[o] = jnp.broadcast_to(w_ref[o : o + 1, :], (8, LANE))


def tall(values):
    return values.reshape(values.shape[0] // 8, 8, LANE)


def chunks(T, step, body, carry):
    full = T // step
    carry = lax.fori_loop(
        0, full, lambda i, c: body(pl.multiple_of(i * step, 8), step, c), carry
    )
    return body(full * step, T - full * step, carry) if T % step else carry


def conv_forward_kernel(len_ref, x_ref, w_ref, out_ref, stat_ref, padded, wide, *, taps, step):
    u = pl.program_id(1)
    T = x_ref.shape[1]
    half = (taps - 1) // 2
    fill_padded(padded, x_ref[0].astype(f32))
    fill_weights(wide, w_ref, taps)
    valid = len_ref[u]

    def body(base, rows, sums):
        total = None
        for o in range(taps):
            term = wide[o] * tall(padded[pl.ds(base + PAD - half + o, rows), :])
            total = term if total is None else total + term
        out_ref[0, pl.ds(base, rows), :] = total.reshape(rows, LANE)
        row = 8 * lax.broadcasted_iota(jnp.int32, (rows // 8, 8, LANE), 0)
        row = row + lax.broadcasted_iota(jnp.int32, (rows // 8, 8, LANE), 1) + base
        masked = jnp.where(row < valid, total, 0.0)
        return sums[0] + jnp.sum(masked, axis=0), sums[1] + jnp.sum(masked * total, axis=0)

    zero = jnp.zeros((8, LANE), f32)
    first, second = chunks(T, step, body, (zero, zero))
    count = jnp.full((1, LANE), valid, jnp.int32).astype(f32)
    stat = jnp.concatenate(
        [
            jnp.sum(first, axis=0, keepdims=True),
            jnp.sum(second, axis=0, keepdims=True),
            count,
            jnp.zeros((5, LANE), f32),
        ],
        axis=0,
    )

    @pl.when(u == 0)
    def _():
        stat_ref[...] = stat

    @pl.when(u > 0)
    def _():
        stat_ref[...] += stat


def conv_forward(lens, x, w, step=256):
    U, T, C = x.shape
    block = pl.BlockSpec((1, T, LANE), lambda c, u: (u, 0, c))
    return kernel_call(
        functools.partial(conv_forward_kernel, taps=w.shape[0], step=step), "conv_forward",
        [(lens, SCALARS), (x, block), (w, pl.BlockSpec((w.shape[0], LANE), lambda c, u: (0, c)))],
        [((U, T, C), f32, block), ((8, C), f32, pl.BlockSpec((8, LANE), lambda c, u: (0, c)))],
        grid=(pl.cdiv(C, LANE), U),
        scratch=[pltpu.VMEM((T + 2 * PAD, LANE), f32), pltpu.VMEM((w.shape[0], 8, LANE), f32)],
        flops=10_000_000_000,
    )


def batch_moments(stat):
    count = stat[2:3, :]
    mean = stat[0:1, :] / count
    return count, mean, lax.rsqrt(stat[1:2, :] / count - mean * mean + EPSILON)


def conv_backward_kernel(
    len_ref, x_ref, dz_ref, conv_ref, w_ref, stat_ref, sums_ref, vec_ref, gs_ref, gw_ref,
    padded_x, padded_g, wide, *, taps, step, gain_row,
):
    u = pl.program_id(1)
    T = x_ref.shape[1]
    half = (taps - 1) // 2
    valid = len_ref[u]
    count, mean, rstd = batch_moments(stat_ref[...])
    gain = vec_ref[gain_row : gain_row + 1, :]
    grad_var = -0.5 * rstd * rstd * (sums_ref[0:1, :] * gain)
    grad_mean = -rstd * (sums_ref[1:2, :] * gain) - 2.0 * mean * grad_var
    shift = grad_mean / count
    slope = 2.0 * grad_var / count
    row = sublanes((T, LANE))
    g = dz_ref[0] * rstd + jnp.where(row < valid, shift + slope * conv_ref[0], 0.0)
    fill_padded(padded_g, g)
    fill_padded(padded_x, x_ref[0].astype(f32))

    fill_weights(wide, w_ref, taps)

    def spread(base, rows, carry):
        total = None
        for o in range(taps):
            term = wide[o] * tall(padded_g[pl.ds(base + PAD + half - o, rows), :])
            total = term if total is None else total + term
        gs_ref[0, pl.ds(base, rows), :] = total.reshape(rows, LANE)
        return carry

    chunks(T, step, spread, 0)

    zero = jnp.zeros((8, LANE), f32)

    def relate(base, rows, carry):
        centre = tall(padded_g[pl.ds(base + PAD, rows), :])
        new = []
        for o, kept in enumerate(carry):
            moved = tall(padded_x[pl.ds(base + PAD - half + o, rows), :])
            new.append(kept + jnp.sum(centre * moved, axis=0))
        return tuple(new)

    sums = chunks(T, step // 2, relate, (zero,) * taps)
    rows = [jnp.sum(s, axis=0, keepdims=True) for s in sums]
    gw = jnp.concatenate(rows + [jnp.zeros((-taps % 8, LANE), f32)], axis=0)

    @pl.when(u == 0)
    def _():
        gw_ref[...] = gw

    @pl.when(u > 0)
    def _():
        gw_ref[...] += gw


def conv_backward(lens, x, dz, conv, w, stat, sums, vec, gain_row, step=256):
    U, T, C = x.shape
    taps = w.shape[0]
    block = pl.BlockSpec((1, T, LANE), lambda c, u: (u, 0, c))

    def channel(array):
        return array, pl.BlockSpec((array.shape[0], LANE), lambda c, u: (0, c))

    return kernel_call(
        functools.partial(conv_backward_kernel, taps=taps, step=step, gain_row=gain_row),
        "conv_backward",
        [(lens, SCALARS), (x, block), (dz, block), (conv, block)]
        + [channel(a) for a in (w, stat, sums, vec)],
        [((U, T, C), f32, block), ((taps + -taps % 8, C), f32, pl.BlockSpec((taps + -taps % 8, LANE), lambda c, u: (0, c)))],
        grid=(pl.cdiv(C, LANE), U),
        scratch=[pltpu.VMEM((T + 2 * PAD, LANE), f32)] * 2 + [pltpu.VMEM((taps, 8, LANE), f32)],
        flops=20_000_000_000,
    )


CONTENT, POSITION, GAIN1, SHIFT1, GAIN2, SHIFT2, BGAIN, BSHIFT, GAIN3, SHIFT3, GAIN4, SHIFT4 = range(12)


def vector(ref, index):
    return ref[index : index + 1, :]


def sigmoid(x):
    return 0.5 * jnp.tanh(0.5 * x) + 0.5


def unit_norm(values):
    centred = values - jnp.mean(values, axis=-1, keepdims=True)
    inv_std = lax.rsqrt(jnp.mean(centred * centred, axis=-1, keepdims=True) + EPSILON)
    return centred * inv_std, inv_std


def unit_norm_back(unit, inv_std, gain, upstream):
    scaled = upstream * gain
    return inv_std * (
        scaled
        - jnp.mean(scaled, axis=-1, keepdims=True)
        - unit * jnp.mean(scaled * unit, axis=-1, keepdims=True)
    )


def col_sum(values):
    return jnp.sum(values, axis=0, keepdims=True)


def clear(refs):
    @pl.when(pl.program_id(0) == 0)
    def _():
        for ref in refs:
            ref[...] = jnp.zeros(ref.shape, ref.dtype)


def add_into(ref, value):
    rows, cols = value.shape
    ref[:rows, :cols] += value


def up(value, unit):
    return -(-value // unit) * unit


def put_blocks(packed_ref, at, value):
    rows, cols = value.shape
    for c in range(0, cols, LANE):
        packed_ref[at : at + rows, :] = value[:, c : c + LANE].astype(bf16)
        at += rows
    return at


def row_valid(len_ref, step, tile, length):
    per = length // tile
    row = sublanes((tile, 1)) + lax.rem(step, per) * tile
    return row < len_ref[lax.div(step, per)]


def first_kernel(
    len_ref, f_ref, mixed_ref, vec_ref, wout_ref, wi_ref, wo_ref, wl_ref, wg_ref,
    x1_ref, r1_ref, u_ref, x2_ref, r2_ref, lin_ref, sig_ref, spread_ref, *, tile, length,
):
    D = x1_ref.shape[1]
    resid = f_ref[...][:, :D].astype(f32) + dot(mixed_ref[...], wout_ref[...])
    unit, inv_std = unit_norm(resid)
    x1_ref[...] = unit
    r1_ref[...] = inv_std
    hidden = unit * vector(vec_ref, GAIN1) + vector(vec_ref, SHIFT1)
    inner = dot(hidden.astype(bf16), wi_ref[...])
    u_ref[...] = inner.astype(bf16)
    active = (inner * sigmoid(inner)).astype(bf16)
    resid = hidden + dot_nt(active, wo_ref[...])
    unit, inv_std = unit_norm(resid)
    x2_ref[...] = unit
    r2_ref[...] = inv_std
    entry = (unit * vector(vec_ref, GAIN2) + vector(vec_ref, SHIFT2)).astype(bf16)
    lin = dot_nt(entry, wl_ref[...])
    sig = sigmoid(dot_nt(entry, wg_ref[...]))
    lin_ref[...] = lin.astype(bf16)
    sig_ref[...] = sig.astype(bf16)
    valid = row_valid(len_ref, pl.program_id(0), tile, length)
    spread_ref[...] = jnp.where(valid, lin * sig, 0.0).astype(bf16)


def second_kernel(
    mine_ref, x2_ref, conv_ref, cot_ref, stat_ref, vec_ref, wp_ref, wi_ref, wo_ref,
    out_ref, dz_ref, g3_ref, small_ref, dwp_ref, dwi_ref, dwo_ref, sum_p, sum_i, sum_o,
):
    clear((small_ref, sum_p, sum_i, sum_o))
    _, mean, rstd = batch_moments(stat_ref[...])
    centred = (conv_ref[...] - mean) * rstd
    batch_gain = vector(vec_ref, BGAIN)
    normed = centred * batch_gain + vector(vec_ref, BSHIFT)
    sig_n = sigmoid(normed)
    swished = (normed * sig_n).astype(bf16)
    slope_n = (sig_n * (1.0 + normed * (1.0 - sig_n))).astype(bf16)
    hidden_two = x2_ref[...] * vector(vec_ref, GAIN2) + vector(vec_ref, SHIFT2)
    unit3, inv3 = unit_norm(hidden_two + dot(swished, wp_ref[...]))
    gain3 = vector(vec_ref, GAIN3)
    hidden = unit3 * gain3 + vector(vec_ref, SHIFT3)
    entry = hidden.astype(bf16)
    inner = dot(entry, wi_ref[...])
    sig = sigmoid(inner)
    active = (inner * sig).astype(bf16)
    slope = (sig * (1.0 + inner * (1.0 - sig))).astype(bf16)
    unit4, inv4 = unit_norm(hidden + dot_nt(active, wo_ref[...]))
    gain4 = vector(vec_ref, GAIN4)
    D = unit4.shape[1]
    out_ref[:, :D] = (unit4 * gain4 + vector(vec_ref, SHIFT4)).astype(bf16)
    out_ref[:, D:] = jnp.zeros((unit4.shape[0], FULL - D), bf16)
    upstream = cot_ref.value(mine_ref[0])[:, :D].astype(f32)
    grad4 = unit_norm_back(unit4, inv4, gain4, upstream)
    low4 = grad4.astype(bf16)
    add_into(sum_o, dot_tn(low4, active))
    dinner = (dot(low4, wo_ref[...]) * slope.astype(f32)).astype(bf16)
    add_into(sum_i, dot_tn(entry, dinner))
    up3 = grad4 + dot_nt(dinner, wi_ref[...])
    grad3 = unit_norm_back(unit3, inv3, gain3, up3)
    g3_ref[...] = grad3
    low3 = grad3.astype(bf16)
    add_into(sum_p, dot_tn(swished, low3))
    dnormed = dot_nt(low3, wp_ref[...]) * slope_n.astype(f32)
    dz_ref[...] = dnormed * batch_gain
    small = jnp.concatenate(
        [
            col_sum(dnormed * centred), col_sum(dnormed),
            col_sum(up3 * unit3), col_sum(up3),
            col_sum(upstream * unit4), col_sum(upstream),
            jnp.zeros((2, centred.shape[1]), f32),
        ],
        axis=0,
    )
    add_into(small_ref, small)

    @pl.when(pl.program_id(0) == pl.num_programs(0) - 1)
    def _():
        dwp_ref[...] = sum_p[...].astype(bf16)
        dwi_ref[...] = sum_i[...].astype(bf16)
        dwo_ref[...] = sum_o[...].astype(bf16)


def third_kernel(
    len_ref, gs_ref, lin_ref, sig_ref, x2_ref, r2_ref, g3_ref, u_ref, x1_ref, r1_ref, mixed_ref,
    vec_ref, wl_ref, wg_ref, wi_ref, wo_ref, wout_ref,
    g1_ref, gm_ref, small_ref, packed_ref, sum_i, sum_o, sum_l, sum_g, sum_out, *, tile, length,
):
    step = pl.program_id(0)
    clear((small_ref, sum_i, sum_o, sum_l, sum_g, sum_out))
    valid = row_valid(len_ref, step, tile, length)
    sig_g = sig_ref[...].astype(f32)
    gated = jnp.where(valid, gs_ref[...], 0.0) * sig_g
    low_l = gated.astype(bf16)
    low_g = (gated * lin_ref[...].astype(f32) * (1.0 - sig_g)).astype(bf16)
    unit2 = x2_ref[...]
    gain2 = vector(vec_ref, GAIN2)
    entry2 = (unit2 * gain2 + vector(vec_ref, SHIFT2)).astype(bf16)
    add_into(sum_l, dot_tn(low_l, entry2))
    add_into(sum_g, dot_tn(low_g, entry2))
    up2 = g3_ref[...] + dot(low_l, wl_ref[...]) + dot(low_g, wg_ref[...])
    grad2 = unit_norm_back(unit2, r2_ref[...], gain2, up2)
    low2 = grad2.astype(bf16)
    inner = u_ref[...].astype(f32)
    sig = sigmoid(inner)
    active = (inner * sig).astype(bf16)
    slope = (sig * (1.0 + inner * (1.0 - sig))).astype(bf16)
    add_into(sum_o, dot_tn(low2, active))
    dinner = (dot(low2, wo_ref[...]) * slope.astype(f32)).astype(bf16)
    unit1 = x1_ref[...]
    gain1 = vector(vec_ref, GAIN1)
    entry1 = (unit1 * gain1 + vector(vec_ref, SHIFT1)).astype(bf16)
    add_into(sum_i, dot_tn(entry1, dinner))
    up1 = grad2 + dot_nt(dinner, wi_ref[...])
    grad1 = unit_norm_back(unit1, r1_ref[...], gain1, up1)
    g1_ref[...] = grad1
    low1 = grad1.astype(bf16)
    add_into(sum_out, dot_tn(mixed_ref[...], low1))
    gm_ref[...] = dot_nt(low1, wout_ref[...]).astype(bf16)
    small = jnp.concatenate(
        [
            col_sum(up1 * unit1), col_sum(up1),
            col_sum(up2 * unit2), col_sum(up2),
            jnp.zeros((4, unit1.shape[1]), f32),
        ],
        axis=0,
    )
    add_into(small_ref, small)

    @pl.when(step == pl.num_programs(0) - 1)
    def _():
        D = unit1.shape[1]
        hs = D // HEADS
        at = 0
        for ref in (sum_i, sum_o, sum_l, sum_g):
            at = put_blocks(packed_ref, at, ref[...])
        rows = sum_l.shape[0]
        compact = jnp.zeros(sum_l.shape, f32)
        for h in range(HEADS):
            chosen = pick(rows, LANE, h * hs, 0, hs).astype(bf16)
            part = dot(chosen, sum_out[h * LANE : (h + 1) * LANE, :].astype(bf16))
            compact += jnp.concatenate(
                [part, jnp.zeros((rows, sum_l.shape[1] - D), f32)], axis=1
            )
        at = put_blocks(packed_ref, at, compact)
        if at < packed_ref.shape[0]:
            packed_ref[at:, :] = jnp.zeros((packed_ref.shape[0] - at, LANE), bf16)


def frames_kernel(*refs):
    heads = refs[:-3]
    g1_ref, back_ref, out_ref = refs[-3:]
    grads = jnp.concatenate([ref[...] for ref in heads], axis=1)
    D = g1_ref.shape[1]
    out_ref[:, :D] = (g1_ref[...] + dot(grads, back_ref[...])).astype(bf16)
    out_ref[:, D:] = jnp.zeros((out_ref.shape[0], FULL - D), bf16)


def frames_block(seq, heads, g1, back, after=(), tile=496):
    rows = heads[0].shape[0]
    per = rows // tile
    return kernel_call(
        frames_kernel, "frames_block",
        [(a, pl.BlockSpec((tile, a.shape[1]), lambda i: (i, 0))) for a in heads]
        + [(g1, pl.BlockSpec((tile, g1.shape[1]), lambda i: (seq * per + i, 0)))]
        + [(back, whole_spec(back.shape))],
        [((rows, FULL), bf16, pl.BlockSpec((tile, FULL), lambda i: (i, 0)))],
        grid=(per,), after=after, flops=3_000_000_000,
    )[0]


def pack_kernel(*refs, groups, seqs):
    d_refs = refs[:groups]
    f_ref = refs[groups]
    rest = refs[groups + 1 :]
    pos_refs, bias_refs = rest[: groups * seqs], rest[groups * seqs : 2 * groups * seqs]
    small_ref, depth_ref, packed_ref, sum_w = rest[2 * groups * seqs :]
    clear((sum_w,))
    grads = jnp.concatenate([ref[...] for ref in d_refs], axis=1)
    sum_w[...] += dot_tn(f_ref[...], grads)

    @pl.when(pl.program_id(0) == pl.num_programs(0) - 1)
    def _():
        D = small_ref.shape[1]
        wide = up(D, LANE)
        spare = jnp.zeros((16, wide - D), f32)
        at = put_blocks(packed_ref, 0, sum_w[: up(D, 16), :])
        kept = up(D // 2, 16)

        def over_seqs(items, group, take):
            total = None
            for s in range(seqs):
                value = take(items[s * groups + group])
                total = value if total is None else total + value
            return total

        for group in range(groups):
            for h in range(pos_refs[group].shape[0]):
                for half in range(2):
                    rows = slice(half * WIDE, half * WIDE + kept)
                    value = over_seqs(pos_refs, group, lambda ref: ref[h, rows, :])
                    at = put_blocks(packed_ref, at, value)
        for group in range(groups):
            for h in range(bias_refs[group].shape[0]):
                at = put_blocks(packed_ref, at, over_seqs(bias_refs, group, lambda ref: ref[h]))
        small = jnp.concatenate([small_ref[...], jnp.zeros((8, D), f32)], axis=0)
        at = put_blocks(packed_ref, at, jnp.concatenate([small, spare], axis=1))
        depth = depth_ref[...]
        spare = jnp.zeros((depth.shape[0], wide - D), f32)
        at = put_blocks(packed_ref, at, jnp.concatenate([depth, spare], axis=1))
        if at < packed_ref.shape[0]:
            packed_ref[at:, :] = jnp.zeros((packed_ref.shape[0] - at, LANE), bf16)


def middle_rows(D, F, unit):
    blocks = 2 * (up(F, LANE) // LANE) + 3 * (up(D, LANE) // LANE)
    return up(blocks * up(D, 16), unit)


def late_rows(D, taps, unit):
    blocks = up(D, LANE) // LANE
    rows = HEADS * WIDE // LANE * up(D, 16) + HEADS * (2 * up(D // 2, 16) + 16)
    return up(rows + blocks * (16 + up(taps, 16)), unit)


def unpack_kernel(
    bit_ref, value_ref, other_ref, bias_ref,
    wi1_ref, wo1_ref, glu_ref, wout_ref, q_ref, k_ref, v_ref, pos_ref, vec_ref, depth_ref, buf, *, middle, late,
):
    n = value_ref.shape[0]
    bit = bit_ref[0]
    buf[pl.ds(pl.multiple_of(bit * n, 16), n), :] = value_ref[...]
    buf[pl.ds(pl.multiple_of((1 - bit) * n, 16), n), :] = other_ref[...]
    D, F = wi1_ref.shape
    hs = D // HEADS
    half = D // 2
    at = half - LANE
    one = 3 * hs - LANE
    place = {"middle": 0, "late": 0}

    def fetch(kind, rows):
        cut = middle if kind == "middle" else late
        start = place[kind]
        place[kind] += rows
        parts = []
        while rows:
            shard, offset = divmod(start, cut)
            count = min(rows, cut - offset)
            base = shard * (middle + late) + offset + (0 if kind == "middle" else middle)
            parts.append(buf[base : base + count, :])
            start += count
            rows -= count
        return jnp.concatenate(parts, axis=0) if len(parts) > 1 else parts[0]

    def spread_blocks(ref, first, kind, rows, cols):
        for c in range(0, cols, LANE):
            width = min(LANE, cols - c)
            block = fetch(kind, up(rows, 16))[:rows, :width].astype(f32)
            ref[first : first + rows, c : c + width] = block

    spread_blocks(wi1_ref, 0, "middle", D, F)
    spread_blocks(wo1_ref, 0, "middle", D, F)
    spread_blocks(glu_ref, 0, "middle", D, D)
    spread_blocks(glu_ref, D, "middle", D, D)
    spread_blocks(wout_ref, 0, "middle", D, D)
    sums = [None, None, None]
    for h in range(HEADS):
        block = jnp.concatenate([fetch("late", up(D, 16)), fetch("late", up(D, 16))], axis=1)
        for i in range(3):
            part = dot(block, pick(WIDE, D, i * hs, h * hs, hs).astype(bf16))
            sums[i] = part if sums[i] is None else sums[i] + part
    v_ref[...] = sums[0][:D]
    q_ref[...] = sums[1][:D]
    k_ref[...] = sums[2][:D]
    halves = [None, None]
    scale = math.sqrt(hs) / LOG2E
    for h in range(HEADS):
        change = bias_ref[h, 1:2, :] - bias_ref[h, 0:1, :]
        chosen = pick(LANE, D, at, h * hs, hs).astype(bf16)
        for i in range(2):
            raw = fetch("late", up(half, 16)).astype(f32)
            full = raw * scale + raw[:, one : one + 1] * change
            high = full.astype(bf16)
            part = dot(high, chosen) + dot((full - high.astype(f32)).astype(bf16), chosen)
            halves[i] = part if halves[i] is None else halves[i] + part
    pos_ref[:half, :] = halves[0][:half]
    pos_ref[half:, :] = halves[1][:half]
    total = None
    for h in range(HEADS):
        part = dot(fetch("late", 16), pick(LANE, D, at, h * hs, hs).astype(bf16))
        total = part if total is None else total + part
    vec_ref[0:8, :] = total[:8]
    spread_blocks(vec_ref.at[8:16], 0, "late", 8, D)
    spread_blocks(depth_ref, 0, "late", depth_ref.shape[0], D)


def unpack(bit, value, other, bias, D, F, taps, middle, late, after):
    arrays = (value, other, bias)
    shapes = (
        (D, F), (D, F), (2 * D, D), (D, D), (D, D), (D, D), (D, D), (D, D),
        (16, D), (up(taps, 8), D),
    )
    return kernel_call(
        functools.partial(unpack_kernel, middle=middle, late=late), "unpack",
        [(bit, SCALARS)] + [(a, whole_spec(a.shape)) for a in arrays],
        [(s, f32, whole_spec(s)) for s in shapes],
        after=after, scratch=[pltpu.VMEM((2 * value.shape[0], LANE), bf16)], flops=1000,
    )


def widen_kernel(*refs):
    count = len(refs) // 2
    for source, target in zip(refs[:count], refs[count:]):
        target[...] = source[...].astype(f32)


def widen(arrays):
    return kernel_call(
        widen_kernel, "widen", [(a, whole_spec(a.shape)) for a in arrays],
        [(a.shape, f32, whole_spec(a.shape)) for a in arrays], flops=1000,
    )


class Rows:
    def __init__(self, refs, per):
        self.refs, self.per, self.shape = refs, per, refs[0].shape

    def __getitem__(self, _):
        step = pl.program_id(0)
        value = self.refs[0][...]
        for u in range(1, len(self.refs)):
            value = jnp.where(step >= u * self.per, self.refs[u][...], value)
        return value


class Shifts(list):
    def __init__(self, arrays, rows):
        super().__init__(arrays)
        self.rows = rows


class Places:
    def __init__(self, refs, per, rows):
        self.refs, self.per, self.rows = refs, per, rows

    def value(self, mine):
        step = pl.program_id(0)
        parts = len(self.refs)
        count = parts // self.per
        found = []
        for k in range(count):
            place = lax.rem(step, self.per) * count + k
            chosen = None
            for u in range(self.refs[0].shape[0] // self.rows):
                rows = slice(u * self.rows, (u + 1) * self.rows)
                here = at_place(mine, place, [ref[rows, :] for ref in self.refs])
                chosen = here if chosen is None else jnp.where(step >= u * self.per, here, chosen)
            found.append(chosen)
        return jnp.concatenate(found, axis=0) if count > 1 else found[0]


def row_call(kernel, name, rows, tile, scalars, tiled, fixed, tiled_out, fixed_out, after=(), scratch=(), flops=0):
    def block(width):
        return pl.BlockSpec((tile, width), lambda i: (i, 0))

    operands = [(a, SCALARS) for a in scalars]
    wraps = []
    for a in tiled:
        start = len(operands)
        if isinstance(a, list):
            count = a.rows
            per = len(a) * count // tile
            operands += [(p, whole_spec(p.shape)) for p in a]
            wraps.append((start, len(operands), lambda r, n=per, k=count: Places(r, n, k)))
        elif isinstance(a, tuple):
            per = a[0].shape[0] // tile
            for u, array in enumerate(a):
                spec = pl.BlockSpec(
                    (tile, array.shape[1]), lambda i, u=u: (jnp.clip(i - u * per, 0, per - 1), 0)
                )
                operands.append((array, spec))
            wraps.append((start, len(operands), lambda r, n=per: Rows(r, n)))
        else:
            operands.append((a, block(a.shape[1])))
            wraps.append((start, start + 1, lambda r: r[0]))
    first = len(scalars)
    last = len(operands)

    def body(*refs):
        kernel(*refs[:first], *[wrap(refs[i:j]) for i, j, wrap in wraps], *refs[last:])

    return kernel_call(
        body, name,
        operands + [(a, whole_spec(a.shape)) for a in fixed],
        [((rows, w), d, block(w)) for w, d in tiled_out]
        + [(s, k, whole_spec(s)) for s, k in fixed_out],
        grid=(rows // tile,),
        after=after,
        scratch=[pltpu.VMEM(s, f32) for s in scratch],
        flops=flops,
    )


def first_block(lens, length, tiled, fixed, tile=496):
    D, F = fixed[2].shape
    rows = len(tiled[0]) * length
    return row_call(
        functools.partial(first_kernel, tile=tile, length=length), "first_block", rows, tile,
        (lens,), tiled, fixed,
        ((D, f32), (1, f32), (F, bf16), (D, f32), (1, f32), (D, bf16), (D, bf16), (D, bf16)), (),
        flops=15_000_000_000,
    )


def second_block(mine, tiled, fixed, tile=496):
    rows, D = tiled[0].shape
    F = fixed[3].shape[1]
    return row_call(
        second_kernel, "second_block", rows, tile, (mine,), tiled, fixed,
        ((FULL, bf16), (D, f32), (D, f32)),
        (((8, D), f32), ((D, D), bf16), ((D, F), bf16), ((D, F), bf16)),
        scratch=((D, D), (D, F), (D, F)),
        flops=30_000_000_000,
    )


def third_block(lens, length, unit, tiled, fixed, after, tile=496):
    rows, D = tiled[0].shape
    M = tiled[-1][0].shape[1]
    F = fixed[3].shape[1]
    tall, wide, square = up(D, 16), up(F, LANE), up(D, LANE)
    return row_call(
        functools.partial(third_kernel, tile=tile, length=length), "third_block", rows, tile,
        (lens,), tiled, fixed, ((D, f32), (M, bf16)),
        (((8, D), f32), ((middle_rows(D, F, unit), LANE), bf16)),
        scratch=((tall, wide), (tall, wide), (tall, square), (tall, square), (M, D)),
        after=after, flops=30_000_000_000,
    )


def pack_block(unit, groups, whole, pos, bias, small, depth, taps, after, tile=496):
    seqs = len(whole)
    D = small.shape[1]
    rows = seqs * whole[0].shape[0]
    width = sum(g[0].shape[1] for g in groups)
    return row_call(
        functools.partial(pack_kernel, groups=len(groups), seqs=seqs), "pack_block", rows, tile,
        (), (*groups, whole), (*pos, *bias, small, depth),
        (), (((late_rows(D, taps, unit), LANE), bf16),),
        scratch=((FULL, width),), after=after, flops=5_000_000_000,
    )[0]


def swap_pairs(size, distance):
    return [(i, i ^ distance) for i in range(size)]


def axis_steps(axis, first=1):
    size = lax.axis_size(axis)
    steps = []
    distance = first
    while distance < size:
        steps.append((axis, size, distance))
        distance *= 2
    return steps


def butterfly_sum(value):
    for axis, size, distance in axis_steps("batch") + axis_steps("tm"):
        value = value + lax.ppermute(value, axis, swap_pairs(size, distance))
    return value


def scatter_step(value, step):
    axis, size, distance = step
    bit = (lax.axis_index(axis) // distance) % 2
    half = value.shape[0] // 2
    sent = lax.dynamic_slice_in_dim(value, (1 - bit) * half, half, 0).astype(bf16)
    kept = lax.dynamic_slice_in_dim(value, bit * half, half, 0).astype(f32)
    got = lax.ppermute(sent, axis, swap_pairs(size, distance))
    return kept + got.astype(f32), got


def gather_step(value, step):
    axis, size, distance = step
    bit = (lax.axis_index(axis) // distance) % 2
    other = lax.ppermute(value, axis, swap_pairs(size, distance))
    return jnp.concatenate(
        [jnp.where(bit == 0, value, other), jnp.where(bit == 0, other, value)]
    )


def ring_plan():
    batch = axis_steps("batch")
    return batch[:1], batch[1:2], axis_steps("tm"), batch[2:]


def exchange_sum(value, step):
    axis, size, distance = step
    low = value.astype(bf16)
    got = lax.ppermute(low, axis, swap_pairs(size, distance))
    return low.astype(f32) + got.astype(f32), got


def scatter_sum(value, after=(), split=False):
    core, across, tm, rest = ring_plan()
    arrived = []
    for step in core:
        value, got = scatter_step(value, step)
        arrived.append([got])
    half = value.shape[0] // 2
    streams = [value[:half], value[half:]]
    for steps in zip(across + tm, tm + across):
        pair = [scatter_step(v, s) for v, s in zip(streams, steps)]
        streams = [p[0] for p in pair]
        arrived.append([p[1] for p in pair])
    value = jnp.concatenate(streams)
    if split:
        for step in rest:
            value, got = scatter_step(value, step)
            arrived.append([got])
        value = value.astype(bf16)
        for step in rest[::-1]:
            value = gather_step(value, step)
        return value, arrived
    for index, step in enumerate(rest):
        if after and index == len(rest) - 1:
            value = hold(value, after)
        value, got = exchange_sum(value, step)
        arrived.append([got])
    return value.astype(bf16), arrived


def merge_kernel(bits_ref, *refs, joined):
    count = bits_ref.shape[0]
    out_refs = refs[2 * count :]
    at = 0
    for i in range(count):
        value, other = refs[i], refs[count + i]
        rows = value.shape[0]
        out_ref = out_refs[0] if joined else out_refs[i]
        for ref, place in ((value, bits_ref[i]), (other, 1 - bits_ref[i])):
            out_ref[pl.ds(pl.multiple_of(at + place * rows, 16), rows), :] = ref[...]
        at += 2 * rows if joined else 0


def merge(bits, values, others, joined, after):
    arrays = list(values) + list(others)
    shapes = [(2 * v.shape[0], LANE) for v in values]
    if joined:
        shapes = [(sum(s[0] for s in shapes), LANE)]
    return kernel_call(
        functools.partial(merge_kernel, joined=joined), "merge",
        [(jnp.stack(bits).astype(jnp.int32), SCALARS)]
        + [(a, whole_spec(a.shape)) for a in arrays],
        [(s, bf16, whole_spec(s)) for s in shapes], after=after, flops=1000,
    )


def gather_all(streams, after):
    core, across, tm, _ = ring_plan()
    stages = list(zip(across + tm, tm + across))[::-1]
    for index, steps in enumerate(stages):
        last = index == len(stages) - 1
        bits = [(lax.axis_index(a) // d) % 2 for a, _, d in steps]
        others = [lax.ppermute(v, a, swap_pairs(n, d)) for v, (a, n, d) in zip(streams, steps)]
        streams = merge(bits, streams, others, last, after if last else ())
    value = streams[0]
    axis, size, distance = core[0]
    bit = (lax.axis_index(axis) // distance) % 2
    return bit, value, lax.ppermute(value, axis, swap_pairs(size, distance))


def scatter_parts():
    core, across, tm, rest = ring_plan()
    return 2 ** (len(core) + 1 + len(across) + len(tm))


def hold_kernel(a_ref, out_ref):
    out_ref[...] = a_ref[...]


def hold(value, after):
    spec = whole_spec(value.shape)
    return kernel_call(
        hold_kernel, "hold", [(value, spec)], [(value.shape, value.dtype, spec)], after=after,
        flops=1000,
    )[0]


def join_kernel(a_ref, b_ref, first_ref, second_ref):
    a, b = a_ref.shape[0] // 2, b_ref.shape[0] // 2
    for i, ref in enumerate((first_ref, second_ref)):
        ref[:a, :] = a_ref[i * a : (i + 1) * a, :]
        ref[a:, :] = b_ref[i * b : (i + 1) * b, :]


def join_shards(a, b, after):
    shape = ((a.shape[0] + b.shape[0]) // 2, LANE)
    return kernel_call(
        join_kernel, "join_shards", [(x, whole_spec(x.shape)) for x in (a, b)],
        [(shape, a.dtype, whole_spec(shape))] * 2, after=after, flops=1000,
    )


def rotation(size, shift):
    return [(i, (i + shift) % size) for i in range(size)]


def assemble_kernel(mine_ref, *refs, parts, own, pieces):
    out_ref = refs[-1]
    D, _, rows = out_ref.shape
    mine = mine_ref[0]
    base = pl.multiple_of(mine * rows, 8)
    for u in range(own):
        here = [refs[u][pl.ds(base, rows), :]]
        here += [refs[own + i][at : at + rows, :] for i, at in pieces[u]]
        for place in range(parts):
            value = at_place(mine, place, here)[:, :D].astype(f32)
            out_ref[:, place * own + u, :] = jnp.transpose(value).astype(bf16)


def assemble(whole, groups, mine, D, after=()):
    own = len(whole)
    parts = lax.axis_size("tm")
    rows = whole[0].shape[0] // parts
    arrays = []
    pieces = {}
    for seqs, by_shift in groups:
        for index, u in enumerate(seqs):
            pieces[u] = [(len(arrays) + k, index * rows) for k in range(parts - 1)]
        arrays += by_shift
    operands = list(whole) + arrays
    shape = (D, parts * own, rows)
    return kernel_call(
        functools.partial(assemble_kernel, parts=parts, own=own, pieces=pieces), "assemble",
        [(mine, SCALARS)] + [(a, whole_spec(a.shape)) for a in operands],
        [(shape, bf16, whole_spec(shape))], after=after, flops=1000, vmem=MOST,
    )[0]


def send_pieces(pieces):
    return [
        lax.ppermute(p, "tm", rotation(len(pieces), shift)) if shift else p
        for shift, p in enumerate(pieces)
    ]


def send_frames(whole, mine):
    parts = lax.axis_size("tm")
    rows = whole[0].shape[0] // parts
    pieces = []
    for shift in range(1, parts):
        at = lax.rem(mine + shift, parts) * rows
        piece = jnp.concatenate([lax.dynamic_slice_in_dim(w, at, rows, 0) for w in whole])
        pieces.append(lax.ppermute(piece, "tm", rotation(parts, shift)))
    return pieces


def on_device(
    frames,
    lengths,
    cotangent,
    query_weight,
    key_weight,
    value_weight,
    position_weight,
    content_bias,
    position_bias,
    output_weight,
    attend_gain,
    attend_shift,
    inner_first,
    outer_first,
    first_gain,
    first_shift,
    glu_weight,
    depth_weight,
    batch_gain,
    batch_shift,
    point_weight,
    conv_gain,
    conv_shift,
    inner_second,
    outer_second,
    second_gain,
    second_shift,
):
    seq_local, local_rows, D = frames.shape
    H = HEADS
    hs = D // H
    F = inner_first.shape[1]
    taps = depth_weight.shape[0]
    half = D // 2
    at = half - LANE
    parts = lax.axis_size("tm")
    mine = lax.axis_index("tm")
    unit = 16 * scatter_parts()
    U = seq_local // parts
    T = local_rows * parts
    R = U * T
    lens = lax.dynamic_slice_in_dim(lengths, mine * U, U)

    place = mine.astype(jnp.int32).reshape(1)
    pieces = []
    for u in range(U):
        earlier = tuple(pieces[-1][1:]) if pieces else ()
        pieces.append(send_pieces(split_frames(frames, place, (u,), after=earlier)))
    zero = jnp.zeros((D,), f32)
    vec = jnp.stack(
        [
            content_bias, position_bias, attend_gain, attend_shift, first_gain, first_shift,
            batch_gain, batch_shift, conv_gain, conv_shift, second_gain, second_shift,
            zero, zero, zero, zero,
        ]
    )
    outer_first_t, outer_second_t = outer_first.T, outer_second.T
    (
        query_x, kv_x, pos_x, output_x, bias_x, back_x, lin_t, gate_t,
        sines, cosines, sines_low, sines_t, cosines_t,
    ) = prepare(
        T, vec, query_weight, key_weight, value_weight, position_weight, output_weight, glu_weight.T
    )

    attended = [
        attend_forward(
            u, hs, lens, place, pieces[u],
            query_x, kv_x, pos_x, bias_x, sines, cosines, sines_low,
        )
        for u in range(U)
    ]
    mixed = tuple(a[0] for a in attended)
    whole = tuple(a[5] for a in attended)
    upstream = Shifts(
        send_pieces(split_frames(cotangent, place, tuple(range(U)), after=mixed[-1:])), local_rows
    )
    unit_one, inv_one, inner_one, unit_two, inv_two, linear, sigma, spread = first_block(
        lens, T, (whole, mixed),
        (vec, output_x, inner_first, outer_first_t, lin_t, gate_t),
    )
    spread = spread.reshape(U, T, D)
    conv_out, stat = conv_forward(lens, spread, depth_weight)
    stat = butterfly_sum(stat)
    block_out, grad_centred, grad_three, sums, grad_point, grad_inner_two, grad_outer_two = (
        second_block(
            place, (unit_two, conv_out.reshape(R, D), upstream),
            (stat, vec, point_weight, inner_second, outer_second_t),
        )
    )
    early = lax.psum((grad_inner_two, grad_outer_two, grad_point), ("batch", "tm"))
    block_out = [block_out[u * T : (u + 1) * T] for u in range(U)]
    out_pieces = send_frames(block_out, mine)
    sums = butterfly_sum(sums)
    def backward(stat, sums, grad_centred, grad_three):
        grad_spread, grad_depth = conv_backward(
            lens, spread, grad_centred.reshape(U, T, D), conv_out, depth_weight, stat, sums, vec, BGAIN
        )
        grad_one, grad_mixed, small_one, middle = (
            third_block(
                lens, T, unit,
                (
                    grad_spread.reshape(R, D), linear, sigma, unit_two, inv_two, grad_three,
                    inner_one, unit_one, inv_one, mixed,
                ),
                (vec, lin_t, gate_t, inner_first, outer_first_t, output_x),
                after=tuple(out_pieces),
            )
        )
        middle_shard, arrived = scatter_sum(middle, split=True)
        waits = iter([()] + arrived)
        groups = 2
        count = H // groups
        back, frames_grad, grad_pieces = [], [], []
        for u in range(U):
            for g in range(groups):
                back.append(
                    attend_backward(
                        u, hs, g * count, count, *attended[u][1:5], grad_mixed, mixed[u], pos_x,
                        sines_low, sines_t, cosines_t, after=tuple(next(waits, ())) + tuple(b[2] for b in back[-1:]),
                        vmem=VMEM if back else MOST,
                    )
                )
            if u < U - 1:
                frames_grad.append(
                    frames_block(u, [b[0] for b in back[-groups:]], grad_one, back_x)
                )
                grad_pieces.append(send_frames(frames_grad[-1:], mine))
        earlier = tuple(p for row in grad_pieces for p in row)
        late = pack_block(
            unit, [tuple(b[0] for b in back[g::groups]) for g in range(groups)], whole,
            [b[1] for b in back], [b[2] for b in back], small_one, grad_depth, taps,
            after=tuple(next(waits, ())) + earlier,
        )
        block_raw = assemble(block_out, [(range(U), out_pieces)], place, D, after=(late,))
        late_shard, arrived = scatter_sum(late, after=(block_raw,))
        frames_grad.append(
            frames_block(
                U - 1, [b[0] for b in back[-groups:]], grad_one, back_x, after=tuple(arrived[1])
            )
        )
        grad_pieces.append(send_frames(frames_grad[-1:], mine))
        return block_raw, frames_grad, grad_pieces, middle_shard, late_shard

    shapes = jax.eval_shape(backward, stat, sums, grad_centred, grad_three)
    block_out, frames_grad, grad_pieces, middle_shard, late_shard = lax.cond(
        stat[2, 0] > 0.0,
        backward,
        lambda *_: jax.tree.map(lambda s: jnp.zeros(s.shape, s.dtype), shapes),
        stat, sums, grad_centred, grad_three,
    )
    frames_grad = assemble(
        frames_grad, [((u,), p) for u, p in enumerate(grad_pieces)], place, D
    )
    cuts = [s.shape[0] // 2 for s in (middle_shard, late_shard)]
    grad_inner_two, grad_outer_two, grad_point = widen(early)
    bit, value, other = gather_all(
        join_shards(middle_shard, late_shard, early[2:]), after=(frames_grad, grad_point)
    )
    (
        grad_inner_one, grad_outer_one, grad_glu, grad_output, grad_query, grad_key, grad_value, grad_position, small, grad_depth,
    ) = unpack(
        bit.astype(jnp.int32).reshape(1), value, other, bias_x, D, F, taps, *cuts, after=()
    )
    return (
        jnp.transpose(block_out, (1, 2, 0)),
        jnp.transpose(frames_grad, (1, 2, 0)),
        grad_query,
        grad_key,
        grad_value,
        grad_position,
        small[0],
        small[1],
        grad_output,
        small[8],
        small[9],
        grad_inner_one,
        grad_outer_one.T,
        small[10],
        small[11],
        grad_glu.T,
        grad_depth[:taps],
        sums[0],
        sums[1],
        grad_point,
        sums[2],
        sums[3],
        grad_inner_two,
        grad_outer_two.T,
        sums[4],
        sums[5],
    )


def solution(mesh):
    split = P("batch", "tm", None)
    return jax.shard_map(
        on_device,
        mesh=mesh,
        in_specs=(split, P("batch"), split) + (P(),) * 24,
        out_specs=(split, split) + (P(),) * 24,
        check_vma=False,
    )
```
